32 devices in a mesh: dp: 4 (over y, x), row: 2 (over core), col: 4 (over z).
Axes of the slice: x: 2, y: 2, z: 4, core: 2. Of those that a mesh axis runs over, the one named last changes fastest.
Arguments:
- tokens: bfloat16 [16384, 2048], P('dp', ('row', 'col')), may hold values from -6 to 6
- cotangent: bfloat16 [16384, 2048], P('dp', ('row', 'col')), may hold values from -6 to 6
- doc_lengths: int32 [8, 4], P(('dp', 'row')), may hold values from 1 to 1024, 2048 in all within a row
- qkv_weight: float32 [2048, 3, 2048], P('row', None, 'col'), may hold values from -0.198873782 to 0.198873782
- out_weight: float32 [2048, 2048], P('col', 'row'), may hold values from -0.198873782 to 0.198873782
- gate_weight: float32 [2048, 8192], P('row', 'col'), may hold values from -0.125 to 0.125
- up_weight: float32 [2048, 8192], P('row', 'col'), may hold values from -0.125 to 0.125
- down_weight: float32 [8192, 2048], P('col', 'row'), may hold values from -0.099436891 to 0.099436891
- head_gains: float32 [2, 2048], P(None, 'col'), may hold values from 0.5 to 1.5
- post_gains: float32 [2048, 2], P(('row', 'col')), may hold values from 0.5 to 1.5
- qkv_first: float32 [2048, 3, 2048], P(('row', 'dp'), None, 'col'), may hold values from -80 to 80
- qkv_second: float32 [2048, 3, 2048], P(('row', 'dp'), None, 'col'), may hold values from 491.52 to 6553.6
- out_first: float32 [2048, 2048], P(('col', 'dp'), 'row'), may hold values from -80 to 80
- out_second: float32 [2048, 2048], P(('col', 'dp'), 'row'), may hold values from 491.52 to 6553.6
- gate_first: float32 [2048, 8192], P(('row', 'dp'), 'col'), may hold values from -80 to 80
- gate_second: float32 [2048, 8192], P(('row', 'dp'), 'col'), may hold values from 491.52 to 6553.6
- up_first: float32 [2048, 8192], P(('row', 'dp'), 'col'), may hold values from -80 to 80
- up_second: float32 [2048, 8192], P(('row', 'dp'), 'col'), may hold values from 491.52 to 6553.6
- down_first: float32 [8192, 2048], P(('col', 'dp'), 'row'), may hold values from -80 to 80
- down_second: float32 [8192, 2048], P(('col', 'dp'), 'row'), may hold values from 491.52 to 6553.6
- head_first: float32 [2, 2048], P(None, 'col'), may hold values from -80 to 80
- head_second: float32 [2, 2048], P(None, 'col'), may hold values from 491.52 to 6553.6
- post_first: float32 [2048, 2], P(('row', 'col', 'dp')), may hold values from -80 to 80
- post_second: float32 [2048, 2], P(('row', 'col', 'dp')), may hold values from 491.52 to 6553.6
Outputs:
- mixed: bfloat16 [16384, 2048], P('dp', ('row', 'col'))
- dtokens: float32 [16384, 2048], P('dp', ('row', 'col'))
- qkv_first_new: float32 [2048, 3, 2048], P(('row', 'dp'), None, 'col')
- qkv_second_new: float32 [2048, 3, 2048], P(('row', 'dp'), None, 'col')
- qkv_weight_new: float32 [2048, 3, 2048], P(('row', 'dp'), None, 'col')
- out_first_new: float32 [2048, 2048], P(('col', 'dp'), 'row')
- out_second_new: float32 [2048, 2048], P(('col', 'dp'), 'row')
- out_weight_new: float32 [2048, 2048], P(('col', 'dp'), 'row')
- gate_first_new: float32 [2048, 8192], P(('row', 'dp'), 'col')
- gate_second_new: float32 [2048, 8192], P(('row', 'dp'), 'col')
- gate_weight_new: float32 [2048, 8192], P(('row', 'dp'), 'col')
- up_first_new: float32 [2048, 8192], P(('row', 'dp'), 'col')
- up_second_new: float32 [2048, 8192], P(('row', 'dp'), 'col')
- up_weight_new: float32 [2048, 8192], P(('row', 'dp'), 'col')
- down_first_new: float32 [8192, 2048], P(('col', 'dp'), 'row')
- down_second_new: float32 [8192, 2048], P(('col', 'dp'), 'row')
- down_weight_new: float32 [8192, 2048], P(('col', 'dp'), 'row')
- head_first_new: float32 [2, 2048], P(None, 'col')
- head_second_new: float32 [2, 2048], P(None, 'col')
- head_gains_new: float32 [2, 2048], P(None, 'col')
- post_first_new: float32 [2048, 2], P(('row', 'col', 'dp'))
- post_second_new: float32 [2048, 2], P(('row', 'col', 'dp'))
- post_gains_new: float32 [2048, 2], P(('row', 'col', 'dp'))
The draws below stay inside these ranges and needn't reach their ends.
Inputs may be any that keep to these rules, and one draw needn't show every extreme that they name: `doc_lengths`: each row holds the lengths of its sequence's documents in order and sums to 2048.
All inputs are finite; a program needn't handle non-finite values.
Results may differ from the reference program's by a relative error of at most 0.023.
Values may be sent and summed in bfloat16 or wider, within the bound.
A program may use at most 512 MiB of HBM per device.

```python
import math
import jax
import jax.numpy as jnp
import numpy as np
from jax import lax

D = 2048
H = 16
HD = 128
FF = 8192
SEQ = 2048
DOCS = 4
STEP = 10
SEQS = 8
TOKENS = 16384


def shaped(base, rise, fan_in):
    columns = base.shape[-1]
    places = jnp.arange(columns, dtype=jnp.float32) / max(columns - 1, 1)
    factor = jnp.exp(0.5 * rise * places) / math.sqrt((math.exp(rise) - 1.0) / rise)
    return base * factor * fan_in ** (-0.5)


def draw_qkv_weight(key, part):
    key = jax.random.fold_in(key, 11)
    base = jnp.clip(jax.random.normal(key, (D, 3, D), jnp.float32), -6.0, 6.0)
    return shaped(base, 1.1, D)


def draw_out_weight(key, part):
    key = jax.random.fold_in(key, 23)
    base = jnp.clip(jax.random.normal(key, (D, D), jnp.float32), -6.0, 6.0)
    return shaped(base, 1.1, D)


def draw_down_weight(key, part):
    key = jax.random.fold_in(key, 37)
    base = jnp.clip(jax.random.normal(key, (FF, D), jnp.float32), -6.0, 6.0)
    return shaped(base, 1.1, FF)


def block_scale(stream_key, extent, pieces, low, largest):
    loudness, own = 1.0, jax.random.fold_in(stream_key, 6)
    for dim, parts in pieces:
        steps = jnp.exp(jax.random.uniform(jax.random.fold_in(own, dim), (parts,), jnp.float32, low / len(pieces), largest / len(pieces)))
        loudness = loudness * jnp.repeat(steps, extent[dim] // parts).reshape([-1 if axis == dim else 1 for axis in range(len(extent))])
    return loudness


def length_profile(count, total, limit, slope):
    weights = [(1 << 20) // math.isqrt(standing ** slope) + 1 for standing in range(2, count + 1)]
    surplus, counts = total - limit - (count - 1), [1] * (count - 1)
    while surplus > 0:
        free = [i for i in range(count - 1) if counts[i] < limit]
        whole, remaining = sum([weights[i] for i in free]), surplus
        for i in free:
            extra = min(limit - counts[i], max(1, remaining * weights[i] // whole), surplus)
            counts[i] = counts[i] + extra
            surplus = surplus - extra
    return np.array([limit] + counts)


def ragged(stream_key, count, total, limit, skew):
    if count == 2:
        one = jax.random.randint(stream_key, (), max(1, total - limit), min(limit, total - 1) + 1)
        return jnp.stack([one, total - one])
    sizes = jnp.asarray(length_profile(count, total, limit, skew), jnp.int32)
    twos = (count - 1) // 2
    source_of, sink = sizes[1:1 + 2 * twos:2], sizes[2:2 + 2 * twos:2]
    slack = jnp.minimum(source_of - 1, limit - sink)
    passed = jax.random.randint(jax.random.fold_in(stream_key, 1), (twos,), 0, 1 << 20) % (slack + 1)
    sizes = sizes.at[1:1 + 2 * twos:2].set(source_of - passed).at[2:2 + 2 * twos:2].set(sink + passed)
    return sizes[jax.random.permutation(jax.random.fold_in(stream_key, 2), count)]


def noise(rng, dims, spread, limit, shards=(), kind=jnp.bfloat16):
    entries = spread * jax.random.normal(rng, dims, jnp.float32)
    if shards:
        entries = entries * block_scale(rng, dims, shards, -0.22, 0.18)
    return jnp.clip(entries, -limit, limit).astype(kind)


def setup_inputs(seed: int = 0) -> dict:
    arg_keys = jax.random.split(jax.random.key(seed), 25)
    return {
        "tokens": noise(arg_keys[0], (TOKENS, D), 1.0, 6.0, ((0, 4), (1, 8))),
        "cotangent": noise(arg_keys[1], (TOKENS, D), 1.0, 6.0, ((0, 4), (1, 8))),
        "doc_lengths": jax.vmap(lambda own: ragged(own, DOCS, SEQ, SEQ // 2, 2))(jax.random.split(arg_keys[2], SEQS)).reshape((SEQS, DOCS)).astype(jnp.int32),
        "qkv_weight": draw_qkv_weight(jax.random.fold_in(arg_keys[24], 71), 0),
        "out_weight": draw_out_weight(jax.random.fold_in(arg_keys[24], 71), 0),
        "gate_weight": noise(arg_keys[5], (D, FF), D ** -0.5, 0.125, ((0, 2), (1, 4)), jnp.float32),
        "up_weight": noise(arg_keys[6], (D, FF), D ** -0.5, 0.125, ((0, 2), (1, 4)), jnp.float32),
        "down_weight": draw_down_weight(jax.random.fold_in(arg_keys[24], 71), 0),
        "head_gains": jnp.clip(1.0 + 0.1 * jax.random.normal(arg_keys[8], (2, D), jnp.float32), 0.5, 1.5),
        "post_gains": jnp.clip(1.0 + 0.1 * jax.random.normal(arg_keys[9], (D, 2), jnp.float32), 0.5, 1.5),
        "qkv_first": noise(arg_keys[10], (D, 3, D), (0.11 * TOKENS ** 0.5), 80.0, ((0, 8), (2, 4)), jnp.float32),
        "qkv_second": jnp.clip(jnp.exp(math.log(6553.6) - 2.5902672 * jax.random.uniform(arg_keys[11], (D, 3, D), jnp.float32) ** block_scale(arg_keys[11], (D, 3, D), ((0, 8), (2, 4)), -0.2, 0.2)), 491.52, 6553.6),
        "out_first": noise(arg_keys[12], (D, D), (0.11 * TOKENS ** 0.5), 80.0, ((0, 16), (1, 2)), jnp.float32),
        "out_second": jnp.clip(jnp.exp(math.log(6553.6) - 2.5902672 * jax.random.uniform(arg_keys[13], (D, D), jnp.float32) ** block_scale(arg_keys[13], (D, D), ((0, 16), (1, 2)), -0.2, 0.2)), 491.52, 6553.6),
        "gate_first": noise(arg_keys[14], (D, FF), (0.11 * TOKENS ** 0.5), 80.0, ((0, 8), (1, 4)), jnp.float32),
        "gate_second": jnp.clip(jnp.exp(math.log(6553.6) - 2.5902672 * jax.random.uniform(arg_keys[15], (D, FF), jnp.float32) ** block_scale(arg_keys[15], (D, FF), ((0, 8), (1, 4)), -0.2, 0.2)), 491.52, 6553.6),
        "up_first": noise(arg_keys[16], (D, FF), (0.11 * TOKENS ** 0.5), 80.0, ((0, 8), (1, 4)), jnp.float32),
        "up_second": jnp.clip(jnp.exp(math.log(6553.6) - 2.5902672 * jax.random.uniform(arg_keys[17], (D, FF), jnp.float32) ** block_scale(arg_keys[17], (D, FF), ((0, 8), (1, 4)), -0.2, 0.2)), 491.52, 6553.6),
        "down_first": noise(arg_keys[18], (FF, D), (0.11 * TOKENS ** 0.5), 80.0, ((0, 16), (1, 2)), jnp.float32),
        "down_second": jnp.clip(jnp.exp(math.log(6553.6) - 2.5902672 * jax.random.uniform(arg_keys[19], (FF, D), jnp.float32) ** block_scale(arg_keys[19], (FF, D), ((0, 16), (1, 2)), -0.2, 0.2)), 491.52, 6553.6),
        "head_first": noise(arg_keys[20], (2, D), (0.11 * TOKENS ** 0.5), 80.0, ((1, 4),), jnp.float32),
        "head_second": jnp.clip(jnp.exp(math.log(6553.6) - 2.5902672 * jax.random.uniform(arg_keys[21], (2, D), jnp.float32) ** block_scale(arg_keys[21], (2, D), ((1, 4),), -0.2, 0.2)), 491.52, 6553.6),
        "post_first": noise(arg_keys[22], (D, 2), (0.11 * TOKENS ** 0.5), 80.0, ((0, 32),), jnp.float32),
        "post_second": jnp.clip(jnp.exp(math.log(6553.6) - 2.5902672 * jax.random.uniform(arg_keys[23], (D, 2), jnp.float32) ** block_scale(arg_keys[23], (D, 2), ((0, 32),), -0.2, 0.2)), 491.52, 6553.6),
    }


@jax.custom_vjp
def low(v):
    return lax.optimization_barrier(v.astype(jnp.bfloat16)).astype(jnp.float32)

@jax.custom_vjp
def low_back(v):
    return v

def low_keep(v):
    return (low(v), None)

def low_pass(kept, grad):
    return (grad,)

def back_keep(v):
    return (v, None)

def back_low(kept, grad):
    return (low(grad),)
low.defvjp(low_keep, low_pass)
low_back.defvjp(back_keep, back_low)
highest = lax.Precision.HIGHEST
norm_eps = 1e-06
rope_base = 500000.0
beta_one = 0.9
beta_two = 0.95
adam_eps = 1e-08
weight_decay = 0.1
rate_matrix = 0.02
rate_gain = 0.6
big_negative = -1e+30

def segments(lengths, seq_len):
    doc_ends = jnp.cumsum(lengths, axis=1)
    places = jnp.arange(seq_len, dtype=jnp.int32)
    return lax.optimization_barrier(jnp.sum((doc_ends[:, None, :] <= places[None, :, None]).astype(jnp.int32), axis=2))

def rotary(seq_len, head_size):
    half_width = head_size // 2
    freqs = rope_base ** (-(jnp.arange(half_width, dtype=jnp.float32) * 2.0) / head_size)
    angles = jnp.arange(seq_len, dtype=jnp.float32)[:, None] * freqs[None, :]
    return (jnp.cos(angles), jnp.sin(angles))

def rotate(values, cos_table, sin_table):
    half_width = values.shape[-1] // 2
    cos_part = cos_table[:, None, :]
    sin_part = sin_table[:, None, :]
    first_half = values[..., :half_width]
    second_half = values[..., half_width:]
    return jnp.concatenate([first_half * cos_part - second_half * sin_part, second_half * cos_part + first_half * sin_part], axis=-1)

def rms_norm(values, gains):
    scale = lax.rsqrt(lax.optimization_barrier(jnp.mean(values * values, axis=-1, keepdims=True)) + norm_eps)
    return values * scale * gains

def attention(query, key_rows, value_rows, seg_ids):
    seq_len = query.shape[0]
    block = min(512, seq_len)
    places = jnp.arange(seq_len, dtype=jnp.int32)
    scale_attn = HD ** (-0.5)

    def one_block(block_idx):
        first_row = block_idx * block
        query_block = lax.dynamic_slice_in_dim(query, first_row, block, 0)
        seg_block = lax.dynamic_slice_in_dim(seg_ids, first_row, block, 0)
        place_block = first_row + jnp.arange(block, dtype=jnp.int32)
        scores = low_back(jnp.einsum('qhd,khd->hqk', query_block, key_rows, precision=highest) * scale_attn)
        allowed = (places[None, :] <= place_block[:, None]) & (seg_ids[None, :] == seg_block[:, None])
        scores = jnp.where(allowed[None], scores, big_negative)
        attn_prob = jax.nn.softmax(scores, axis=-1)
        return jnp.einsum('hqk,khd->qhd', low(attn_prob), value_rows, precision=highest)
    blocks_out = lax.map(jax.checkpoint(one_block), jnp.arange(seq_len // block, dtype=jnp.int32))
    return blocks_out.reshape(seq_len, H, HD)

def layer_forward(params, inputs_seq, seg_ids):
    qkv_weight, out_weight, gate_weight, up_weight, down_weight, head_gains, post_gains = params
    seq_len = inputs_seq.shape[0]
    qkv = low_back(jnp.dot(inputs_seq, low(qkv_weight).reshape(D, 3 * D), precision=highest))
    query_pre = qkv[:, :D]
    key_pre = qkv[:, D:2 * D]
    value_part = qkv[:, 2 * D:]
    query_hat = rms_norm(query_pre, head_gains[0])
    key_hat = rms_norm(key_pre, head_gains[1])
    cos_table, sin_table = rotary(seq_len, HD)
    query_rot = low(rotate(query_hat.reshape(seq_len, H, HD), cos_table, sin_table))
    key_rot = low(rotate(key_hat.reshape(seq_len, H, HD), cos_table, sin_table))
    value_low = low(value_part.reshape(seq_len, H, HD))
    att_out = attention(query_rot, key_rot, value_low, seg_ids)
    att_low = low_back(low(att_out.reshape(seq_len, D)))
    a_pre = low_back(jnp.dot(att_low, low(out_weight), precision=highest))
    h_val = inputs_seq + rms_norm(a_pre, post_gains[:, 0])
    h_low = low(h_val)
    gate_val = low_back(jnp.dot(h_low, low(gate_weight), precision=highest))
    up_val = low_back(jnp.dot(h_low, low(up_weight), precision=highest))
    hidden = low_back(low(jax.nn.silu(gate_val) * up_val))
    m_pre = low_back(jnp.dot(hidden, low(down_weight), precision=highest))
    return h_val + rms_norm(m_pre, post_gains[:, 1])

def adamw_step(weight, gradient, first_mom, second_mom, step_rate, decay_rate):
    first_new = beta_one * first_mom + (1.0 - beta_one) * gradient
    second_new = beta_two * second_mom + (1.0 - beta_two) * gradient * gradient
    fix_one = 1.0 - beta_one ** STEP
    fix_two = 1.0 - beta_two ** STEP
    direction = first_new / fix_one / (jnp.sqrt(second_new / fix_two) + adam_eps)
    return (first_new, second_new, weight - step_rate * (direction + decay_rate * weight))

def reference(tokens, cotangent, doc_lengths, qkv_weight, out_weight, gate_weight, up_weight, down_weight, head_gains, post_gains, qkv_first, qkv_second, out_first, out_second, gate_first, gate_second, up_first, up_second, down_first, down_second, head_first, head_second, post_first, post_second):
    params = (qkv_weight, out_weight, gate_weight, up_weight, down_weight, head_gains, post_gains)
    inputs = tokens.astype(jnp.float32).reshape(SEQS, SEQ, D)
    back_rows = cotangent.astype(jnp.float32).reshape(SEQS, SEQ, D)

    def sequence_step(totals, packed):
        inputs_seq, back_seq, lengths = packed
        seg_ids = segments(lengths[None, :], SEQ)[0]
        out_seq, pullback = jax.vjp(lambda param_tree, values: layer_forward(param_tree, values, seg_ids), params, inputs_seq)
        grads, grad_input = pullback(back_seq)
        totals = jax.tree.map(lambda left, right: left + right, totals, grads)
        return (totals, (out_seq.astype(jnp.bfloat16), grad_input))
    zero_tree = jax.tree.map(lambda arr: jnp.zeros(arr.shape, jnp.float32), params)
    totals, (outs_seq, grads_seq) = lax.scan(sequence_step, zero_tree, (inputs, back_rows, doc_lengths))
    mixed = outs_seq.reshape(TOKENS, D)
    dtokens = grads_seq.reshape(TOKENS, D)
    g_qkv, g_out, g_gate, g_up, g_down, g_head, g_post = totals
    qkv_res = adamw_step(qkv_weight, g_qkv, qkv_first, qkv_second, rate_matrix, weight_decay)
    out_res = adamw_step(out_weight, g_out, out_first, out_second, rate_matrix, weight_decay)
    gate_res = adamw_step(gate_weight, g_gate, gate_first, gate_second, rate_matrix, weight_decay)
    up_res = adamw_step(up_weight, g_up, up_first, up_second, rate_matrix, weight_decay)
    down_res = adamw_step(down_weight, g_down, down_first, down_second, rate_matrix, weight_decay)
    head_res = adamw_step(head_gains, g_head, head_first, head_second, rate_gain, 0.0)
    post_res = adamw_step(post_gains, g_post, post_first, post_second, rate_gain, 0.0)
    return (mixed, dtokens, qkv_res[0], qkv_res[1], qkv_res[2], out_res[0], out_res[1], out_res[2], gate_res[0], gate_res[1], gate_res[2], up_res[0], up_res[1], up_res[2], down_res[0], down_res[1], down_res[2], head_res[0], head_res[1], head_res[2], post_res[0], post_res[1], post_res[2])
```

```python
import functools

import jax
import jax.numpy as jnp
from jax import lax
from jax.experimental import pallas as pl
from jax.experimental.pallas import tpu as pltpu
from jax.sharding import Mesh
from jax.sharding import PartitionSpec as P

HD = 128
STEP = 10

norm_eps = 1e-06
rope_base = 500000.0
beta_one = 0.9
beta_two = 0.95
adam_eps = 1e-08
weight_decay = 0.1
rate_matrix = 0.02
rate_gain = 0.6
big_negative = -1e30
log2_e = 1.4426950408889634

f32 = jnp.float32
bf16 = jnp.bfloat16
NN = (((1,), (0,)), ((), ()))
NT = (((1,), (1,)), ((), ()))
TN = (((0,), (0,)), ((), ()))


def swap(piece, axis):
    return lax.ppermute(piece, axis, [(0, 1), (1, 0)])


def shift(piece, axis, step):
    size = lax.axis_size(axis)
    return lax.ppermute(piece, axis, [(i, (i + step) % size) for i in range(size)])


def swap_bit(piece, axis, bit):
    return lax.ppermute(piece, axis, [(i, i ^ bit) for i in range(lax.axis_size(axis))])


def small_sum(vals, axes):
    for axis in axes:
        bit = 1
        while bit < lax.axis_size(axis):
            vals = vals + swap_bit(vals, axis, bit)
            bit *= 2
    return vals


def tie(*vals):
    return lax.optimization_barrier(vals)


def small_sum(vals, axes):
    for axis in axes:
        bit = 1
        while bit < lax.axis_size(axis):
            vals = vals + swap_bit(vals, axis, bit)
            bit *= 2
    return vals


def gather_kernel(
    chunks, tok_ref, low_ref, post_ref, x_ref, w_ref, all_ref, ex_ref,
    own_sem, zh_send, zh_recv, t_send, t_recv, r_send, r_recv,
    wz_send, wz_recv, wd_send, wd_recv, wr_send, wr_recv, wl_sem, p_send, p_recv,
):
    n_dp = lax.axis_size("dp")
    tp = lax.axis_size("zl")
    d, r, g, t = (lax.axis_index(name) for name in ("dp", "row", "zh", "zl"))
    same = r == g
    feat = tok_ref.shape[1]
    seq_len = tok_ref.shape[0] // 2
    step = seq_len // chunks
    half = low_ref.shape[0]
    rows = half // n_dp

    def place(row, zh, zl):
        return (row * 2 + zh) * tp + zl

    def land(block, c):
        return x_ref.at[block, pl.ds(c * step, step)]

    def remote(src, dst, send, recv, dev):
        return pltpu.make_async_remote_copy(
            src_ref=src, dst_ref=dst, send_sem=send, recv_sem=recv, device_id=dev,
            device_id_type=pl.DeviceIdType.MESH,
        )

    barrier = pltpu.get_barrier_semaphore()
    count = 0
    for dd in range(n_dp):
        for rr in range(2):
            if dd or rr:
                dev = (lax.rem(d + dd, n_dp), lax.rem(r + rr, 2), g, t)
                pl.semaphore_signal(barrier, inc=1, device_id=dev, device_id_type=pl.DeviceIdType.MESH)
                count += 1
    for rr in range(2):
        for gg in range(2):
            for tt in range(tp):
                if gg or tt:
                    dev = (d, lax.rem(r + rr, 2), lax.rem(g + gg, 2), lax.rem(t + tt, tp))
                    pl.semaphore_signal(barrier, inc=1, device_id=dev, device_id_type=pl.DeviceIdType.MESH)
                    count += 1
    pl.semaphore_wait(barrier, count)

    row_dev = (d, 1 - r, g, t)
    zh_dev = (d, r, 1 - g, t)
    mine = place(r, g, t)
    pending = []

    wz = remote(low_ref.at[pl.ds(pl.multiple_of(d * rows, rows), rows)], ex_ref, wz_send, wz_recv, zh_dev)
    wz.start()

    def own_src(c):
        return tok_ref.at[pl.ds(pl.multiple_of(g * seq_len + c * step, step), step)]

    zh_copies = []
    for c in range(chunks):
        src = tok_ref.at[pl.ds(pl.multiple_of((1 - g) * seq_len + c * step, step), step)]
        zh_copies.append(remote(src, land(mine, c), zh_send.at[c], zh_recv.at[c], zh_dev))
        for s in range(1, tp):
            cp = remote(
                own_src(c), land(mine, c), t_send.at[s, 0, c], t_recv.at[s, 0, c], (d, r, g, lax.rem(t + s, tp))
            )
            cp.start()
            pending.append(cp)
    local = []
    for c in range(chunks):
        cp = pltpu.make_async_copy(own_src(c), land(mine, c), own_sem.at[c])
        cp.start()
        local.append(cp)
        cp = remote(own_src(c), land(mine, c), r_send.at[0, 0, c], r_recv.at[0, 0, c], row_dev)
        cp.start()
        pending.append(cp)

    wz.wait_send()
    lead = max(1, chunks // 4)
    for cp in zh_copies[:lead]:
        cp.start()

    half_at = pl.ds(pl.multiple_of(r * half, half), half)
    w_row = remote(low_ref, w_ref.at[half_at], wr_send, wr_recv, row_dev)
    w_loc = pltpu.make_async_copy(low_ref, w_ref.at[half_at], wl_sem.at[0])

    @pl.when(same)
    def _():
        w_loc.start()

    @pl.when(jnp.logical_not(same))
    def _():
        w_row.start()

    posts = []
    n_all = 4 * tp
    p_loc = pltpu.make_async_copy(post_ref, all_ref.at[mine], wl_sem.at[1])
    p_loc.start()
    index = 0
    for rr in range(2):
        for gg in range(2):
            for tt in range(tp):
                if rr or gg or tt:
                    dev = (d, lax.rem(r + rr, 2), lax.rem(g + gg, 2), lax.rem(t + tt, tp))
                    cp = remote(post_ref, all_ref.at[mine], p_send.at[index], p_recv.at[index], dev)
                    cp.start()
                    posts.append(cp)
                    index += 1

    def drain_zh(c):
        zh_copies[c].wait_recv()
        theirs = place(r, 1 - g, t)
        for s in range(1, tp):
            cp = remote(
                land(theirs, c), land(theirs, c), t_send.at[s, 1, c], t_recv.at[s, 1, c],
                (d, r, g, lax.rem(t + s, tp)),
            )
            cp.start()
            pending.append(cp)
        cp = remote(land(theirs, c), land(theirs, c), r_send.at[0, 1, c], r_recv.at[0, 1, c], row_dev)
        cp.start()
        pending.append(cp)

    def drain_t(z, c):
        for s in range(1, tp):
            came = place(r, g if z == 0 else 1 - g, lax.rem(t + tp - s, tp))
            remote(
                land(came, c), land(came, c), t_send.at[s, z, c], t_recv.at[s, z, c],
                (d, r, g, lax.rem(t + s, tp)),
            ).wait_recv()
            cp = remote(land(came, c), land(came, c), r_send.at[s, z, c], r_recv.at[s, z, c], row_dev)
            cp.start()
            pending.append(cp)

    wz.wait_recv()
    spot = pl.ds(pl.multiple_of(r * half + d * rows, rows), rows)
    far = []
    for dd in range(1, n_dp):
        cp = remote(
            ex_ref, w_ref.at[spot], wd_send.at[dd], wd_recv.at[dd, r], (lax.rem(d + dd, n_dp), 1 - g, g, t)
        )
        cp.start()
        far.append(cp)
        for late in zh_copies[lead:][dd - 1 : dd]:
            late.start()
    for late in zh_copies[lead:][n_dp - 1 :]:
        late.start()
    near_remote = remote(ex_ref, w_ref.at[spot], wd_send.at[0], wd_recv.at[0, r], row_dev)
    near_local = pltpu.make_async_copy(ex_ref, w_ref.at[spot], wl_sem.at[2])

    @pl.when(same)
    def _():
        near_remote.start()

    @pl.when(jnp.logical_not(same))
    def _():
        near_local.start()

    for c in range(chunks):
        drain_t(0, c)
        drain_zh(c)
        if c >= 1:
            drain_t(1, c - 1)
    drain_t(1, chunks - 1)

    for c in range(chunks):
        for z in range(2):
            for s in range(tp):
                came = place(1 - r, g if z == 0 else 1 - g, lax.rem(t + tp - s, tp))
                remote(
                    land(came, c), land(came, c), r_send.at[s, z, c], r_recv.at[s, z, c], row_dev
                ).wait_recv()
    for cp in local:
        cp.wait()
    for cp in pending:
        cp.wait_send()
    for cp in zh_copies:
        cp.wait_send()
    p_loc.wait()
    for cp in posts:
        cp.wait_send()
    index = 0
    for rr in range(2):
        for gg in range(2):
            for tt in range(tp):
                if rr or gg or tt:
                    came = place(
                        lax.rem(r + 2 - rr, 2), lax.rem(g + 2 - gg, 2), lax.rem(t + tp - tt, tp)
                    )
                    remote(
                        post_ref, all_ref.at[came], p_send.at[index], p_recv.at[index], row_dev
                    ).wait_recv()
                    index += 1
    for cp in far:
        cp.wait_send()

    @pl.when(same)
    def _():
        w_loc.wait()
        near_remote.wait_send()
        remote(
            low_ref, w_ref.at[pl.ds(pl.multiple_of((1 - r) * half, half), half)], wr_send, wr_recv, row_dev
        ).wait_recv()

    @pl.when(jnp.logical_not(same))
    def _():
        w_row.wait_send()
        near_local.wait()
        for dd in range(n_dp):
            for rr in range(2):
                src_d = lax.rem(d + n_dp - dd, n_dp)
                src_r = r if rr == 0 else 1 - r
                if dd == 0 and rr == 0:
                    continue
                at = pl.ds(pl.multiple_of(src_r * half + src_d * rows, rows), rows)
                remote(ex_ref, w_ref.at[at], wd_send.at[dd], wd_recv.at[dd, src_r], row_dev).wait_recv()


def first_gather(tokens, low, post):
    n_dp = lax.axis_size("dp")
    tp = lax.axis_size("zl")
    rows_dev, feat = tokens.shape
    seq_len = rows_dev // 2
    width = feat * 4 * tp
    chunks = 4 if tp == 2 else 1
    anywhere = pl.BlockSpec(memory_space=pl.ANY)
    dma = pltpu.SemaphoreType.DMA
    x_shape = (4 * tp, seq_len, feat)
    x_full, w_full, post_all, _ = pl.pallas_call(
        functools.partial(gather_kernel, chunks),
        in_specs=[anywhere] * 3,
        out_specs=[anywhere] * 4,
        out_shape=[
            jax.ShapeDtypeStruct(x_shape, bf16),
            jax.ShapeDtypeStruct((2 * low.shape[0], low.shape[1]), bf16),
            jax.ShapeDtypeStruct((4 * tp, *post.shape), f32),
            jax.ShapeDtypeStruct((low.shape[0] // n_dp, low.shape[1]), bf16),
        ],
        scratch_shapes=[
            dma((chunks,)),
            dma((chunks,)),
            dma((chunks,)),
            dma((tp, 2, chunks)),
            dma((tp, 2, chunks)),
            dma((tp, 2, chunks)),
            dma((tp, 2, chunks)),
            dma(()),
            dma(()),
            dma((n_dp,)),
            dma((n_dp, 2)),
            dma(()),
            dma(()),
            dma((3,)),
            dma((4 * tp,)),
            dma((4 * tp,)),
        ],
        compiler_params=pltpu.CompilerParams(collective_id=0, has_side_effects=True),
        cost_estimate=pl.CostEstimate(flops=0, bytes_accessed=6 * seq_len * width, transcendentals=0),
        name="first_gather",
    )(tokens, low, post)
    x_full = x_full.transpose(1, 0, 2).reshape(seq_len, width)
    return x_full, w_full, post_all.transpose(1, 0, 2).reshape(2, width)


def doc_start(ends_ref, docs, places):
    start = jnp.zeros_like(places)
    for i in range(docs):
        end = ends_ref[i]
        start = jnp.where(places >= end, end, start)
    return start


def attend_kernel(docs, bk, ends_ref, q_ref, k_ref, vt_ref, o_ref, lse_ref):
    bq = q_ref.shape[0]
    q0 = pl.program_id(1) * bq
    places = q0 + lax.broadcasted_iota(jnp.int32, (1, bq), 1)
    start = doc_start(ends_ref, docs, places)
    lowest = jnp.int32(0)
    for i in range(docs):
        lowest = jnp.where(ends_ref[i] <= q0, ends_ref[i], lowest)
    query = q_ref[...]
    scale = log2_e * HD ** (-0.5)

    def step(j, carry):
        top, total, acc = carry
        k0 = pl.multiple_of(j * bk, bk)
        key = k_ref[pl.ds(k0, bk), :]
        scores = lax.dot_general(key, query, NT, preferred_element_type=f32) * scale
        rows = k0 + lax.broadcasted_iota(jnp.int32, (bk, 1), 0)
        scores = jnp.where((rows <= places) & (rows >= start), scores, big_negative)
        top_new = jnp.maximum(top, jnp.max(scores, axis=0, keepdims=True))
        prob = jnp.exp2(scores - top_new)
        fade = jnp.exp2(top - top_new)
        total = total * fade + jnp.sum(prob, axis=0, keepdims=True)
        acc = acc * fade + lax.dot_general(
            vt_ref[:, pl.ds(k0, bk)], prob.astype(bf16), NN, preferred_element_type=f32
        )
        return top_new, total, acc

    first = (
        jnp.full((1, bq), big_negative, f32),
        jnp.zeros((1, bq), f32),
        jnp.zeros((HD, bq), f32),
    )
    top, total, acc = lax.fori_loop(lowest // bk, (q0 + bq - 1) // bk + 1, step, first)
    o_ref[...] = (acc * (1.0 / total)).T.astype(bf16)
    lse_ref[0] = top + jnp.log2(total)


def attend(query, key, value_t, ends):
    seq_len, width = query.shape
    heads = width // HD
    block = min(512, seq_len)
    docs = ends.shape[0]
    return pl.pallas_call(
        functools.partial(attend_kernel, docs, block),
        grid_spec=pltpu.PrefetchScalarGridSpec(
            num_scalar_prefetch=1,
            grid=(heads, seq_len // block),
            in_specs=[
                pl.BlockSpec((block, HD), lambda h, i, e: (i, h)),
                pl.BlockSpec((seq_len, HD), lambda h, i, e: (0, h)),
                pl.BlockSpec((HD, seq_len), lambda h, i, e: (h, 0)),
            ],
            out_specs=[
                pl.BlockSpec((block, HD), lambda h, i, e: (i, h)),
                pl.BlockSpec((1, 1, block), lambda h, i, e: (h, 0, i)),
            ],
        ),
        out_shape=[
            jax.ShapeDtypeStruct((seq_len, width), bf16),
            jax.ShapeDtypeStruct((heads, 1, seq_len), f32),
        ],
        compiler_params=pltpu.CompilerParams(vmem_limit_bytes=48 << 20),
        cost_estimate=pl.CostEstimate(
            flops=2 * heads * seq_len * seq_len * HD,
            bytes_accessed=8 * seq_len * width,
            transcendentals=heads * seq_len * seq_len // 2,
        ),
        name="attend",
    )(ends, query, key, value_t)


def attend_back_kernel(
    docs, bq, ends_ref, q_ref, k_ref, kt_ref, v_ref, do_ref, o_ref, lse_ref,
    dqt_ref, dk_ref, dv_ref, dk_acc, dv_acc, delta_acc
):
    bk = k_ref.shape[0]
    seq_len = q_ref.shape[0]
    j = pl.program_id(1)
    k0 = j * bk
    scale = HD ** (-0.5)
    last = jnp.int32(seq_len)
    for i in reversed(range(docs)):
        last = jnp.where(ends_ref[i] > k0 + bk - 1, ends_ref[i], last)
    rows = k0 + lax.broadcasted_iota(jnp.int32, (bk, 1), 0)

    @pl.when(j == 0)
    def _():
        dqt_ref[...] = jnp.zeros_like(dqt_ref)
        ones = jnp.ones((8, HD), bf16)
        for i in range(seq_len // bq):
            part = slice(i * bq, (i + 1) * bq)
            prod = do_ref[part, :].astype(f32) * o_ref[part, :].astype(f32)
            high = prod.astype(bf16)
            low = (prod - high.astype(f32)).astype(bf16)
            delta_acc[:, part] = lax.dot_general(
                ones, high, NT, preferred_element_type=f32
            ) + lax.dot_general(ones, low, NT, preferred_element_type=f32)

    dk_acc[...] = jnp.zeros_like(dk_acc)
    dv_acc[...] = jnp.zeros_like(dv_acc)
    key = k_ref[...]
    value = v_ref[...]
    key_t = kt_ref[...]

    def step(i, carry):
        q0 = pl.multiple_of(i * bq, bq)
        cols = pl.ds(q0, bq)
        query = q_ref[cols, :]
        grad = do_ref[cols, :]
        places = q0 + lax.broadcasted_iota(jnp.int32, (1, bq), 1)
        start = doc_start(ends_ref, docs, places)
        scores = lax.dot_general(key, query, NT, preferred_element_type=f32) * (scale * log2_e)
        allowed = (rows <= places) & (rows >= start)
        prob = jnp.where(allowed, jnp.exp2(scores - lse_ref[0, :, cols]), 0.0)
        dv_acc[...] += lax.dot_general(prob.astype(bf16), grad, NN, preferred_element_type=f32)
        grad_prob = lax.dot_general(value, grad, NT, preferred_element_type=f32)
        grad_score = (prob * (grad_prob - delta_acc[0:1, cols])).astype(bf16)
        dk_acc[...] += lax.dot_general(grad_score, query, NN, preferred_element_type=f32)
        dqt_ref[:, cols] += lax.dot_general(key_t, grad_score, NN, preferred_element_type=f32) * scale
        return carry

    lax.fori_loop(k0 // bq, (last + bq - 1) // bq, step, 0)
    dk_ref[...] = dk_acc[...] * scale
    dv_ref[...] = dv_acc[...].astype(bf16)


def attend_back(query, key, key_t, value, grad, att, log_total, ends):
    seq_len, width = query.shape
    heads = width // HD
    block = min(512, seq_len)
    docs = ends.shape[0]
    whole = pl.BlockSpec((seq_len, HD), lambda h, j, e: (0, h))
    part = pl.BlockSpec((block, HD), lambda h, j, e: (j, h))
    line = pl.BlockSpec((1, 1, seq_len), lambda h, j, e: (h, 0, 0))
    return pl.pallas_call(
        functools.partial(attend_back_kernel, docs, block),
        grid_spec=pltpu.PrefetchScalarGridSpec(
            num_scalar_prefetch=1,
            grid=(heads, seq_len // block),
            in_specs=[
                whole,
                part,
                pl.BlockSpec((HD, block), lambda h, j, e: (h, j)),
                part,
                whole,
                whole,
                line,
            ],
            out_specs=[
                pl.BlockSpec((HD, seq_len), lambda h, j, e: (h, 0)),
                part,
                part,
            ],
            scratch_shapes=[
                pltpu.VMEM((block, HD), f32),
                pltpu.VMEM((block, HD), f32),
                pltpu.VMEM((8, seq_len), f32),
            ],
        ),
        out_shape=[
            jax.ShapeDtypeStruct((width, seq_len), f32),
            jax.ShapeDtypeStruct((seq_len, width), f32),
            jax.ShapeDtypeStruct((seq_len, width), bf16),
        ],
        compiler_params=pltpu.CompilerParams(vmem_limit_bytes=48 << 20),
        cost_estimate=pl.CostEstimate(
            flops=5 * heads * seq_len * seq_len * HD,
            bytes_accessed=20 * seq_len * width,
            transcendentals=heads * seq_len * seq_len // 2,
        ),
        name="attend_back",
    )(ends, query, key, key_t, value, grad, att, log_total)


def turn(values, cos_two, sin_two):
    return values * cos_two + pltpu.roll(values, HD // 2, 1) * sin_two


def prepare_kernel(qkv_ref, scale_ref, gains_ref, cos_ref, sin_ref, q_ref, k_ref, kt_ref, v_ref, vt_ref):
    width = q_ref.shape[1]
    cos_two = cos_ref[...]
    sin_two = sin_ref[...]
    for which, out_ref in ((0, q_ref), (1, k_ref)):
        scale = scale_ref[:, which : which + 1]
        for head in range(width // HD):
            cols = slice(head * HD, (head + 1) * HD)
            vals = qkv_ref[:, which * width + head * HD : which * width + (head + 1) * HD]
            out = turn(vals * scale * gains_ref[which : which + 1, cols], cos_two, sin_two)
            out_ref[:, cols] = out.astype(bf16)
            if which == 1:
                kt_ref[cols, :] = out.T.astype(bf16)
    value = qkv_ref[:, 2 * width :]
    v_ref[...] = value.astype(bf16)
    vt_ref[...] = value.T.astype(bf16)


def prepare(qkv, inv_scale, gains, cos_two, sin_two):
    seq_len, triple = qkv.shape
    width = triple // 3
    block = min(256, seq_len)
    flat = pl.BlockSpec((block, width), lambda i: (i, 0))
    tall = pl.BlockSpec((width, block), lambda i: (0, i))
    table = pl.BlockSpec((block, HD), lambda i: (i, 0))
    return pl.pallas_call(
        prepare_kernel,
        grid=(seq_len // block,),
        in_specs=[
            pl.BlockSpec((block, triple), lambda i: (i, 0)),
            pl.BlockSpec((block, 2), lambda i: (i, 0)),
            pl.BlockSpec((2, width), lambda i: (0, 0)),
            table,
            table,
        ],
        out_specs=[flat, flat, tall, flat, tall],
        out_shape=[
            jax.ShapeDtypeStruct((seq_len, width), bf16),
            jax.ShapeDtypeStruct((seq_len, width), bf16),
            jax.ShapeDtypeStruct((width, seq_len), bf16),
            jax.ShapeDtypeStruct((seq_len, width), bf16),
            jax.ShapeDtypeStruct((width, seq_len), bf16),
        ],
        compiler_params=pltpu.CompilerParams(vmem_limit_bytes=48 << 20),
        cost_estimate=pl.CostEstimate(flops=10 * seq_len * triple, bytes_accessed=8 * seq_len * triple, transcendentals=0),
        name="prepare",
    )(qkv, inv_scale, gains, cos_two, sin_two)


def unturn_kernel(dqt_ref, dk_ref, qkv_ref, scale_ref, gains_ref, cos_ref, sin_ref, hat_ref, inner_ref, gain_ref):
    width = dk_ref.shape[1]
    cos_two = cos_ref[...]
    sin_two = sin_ref[...]

    @pl.when(pl.program_id(0) == 0)
    def _():
        gain_ref[...] = jnp.zeros_like(gain_ref)

    for which in range(2):
        scale = scale_ref[:, which : which + 1]
        inner = jnp.zeros((dk_ref.shape[0], HD), f32)
        for head in range(width // HD):
            cols = slice(head * HD, (head + 1) * HD)
            off = which * width + head * HD
            grad = dqt_ref[cols, :].T if which == 0 else dk_ref[:, cols]
            hat = turn(grad, cos_two, -sin_two)
            pre = qkv_ref[:, off : off + HD]
            prod = hat * pre
            gain_ref[which : which + 1, cols] += jnp.sum(prod * scale, axis=0, keepdims=True)
            inner = inner + prod * gains_ref[which : which + 1, cols]
            hat_ref[:, off : off + HD] = hat * gains_ref[which : which + 1, cols]
        inner_ref[:, which : which + 1] = jnp.sum(inner, axis=1, keepdims=True)


def unturn(dqt, dk, qkv, inv_scale, gains, cos_two, sin_two):
    seq_len, width = dk.shape
    block = min(256, seq_len)
    table = pl.BlockSpec((block, HD), lambda i: (i, 0))
    pair = pl.BlockSpec((block, 2), lambda i: (i, 0))
    return pl.pallas_call(
        unturn_kernel,
        grid=(seq_len // block,),
        in_specs=[
            pl.BlockSpec((width, block), lambda i: (0, i)),
            pl.BlockSpec((block, width), lambda i: (i, 0)),
            pl.BlockSpec((block, 2 * width), lambda i: (i, 0)),
            pair,
            pl.BlockSpec((2, width), lambda i: (0, 0)),
            table,
            table,
        ],
        out_specs=[
            pl.BlockSpec((block, 2 * width), lambda i: (i, 0)),
            pair,
            pl.BlockSpec((2, width), lambda i: (0, 0)),
        ],
        out_shape=[
            jax.ShapeDtypeStruct((seq_len, 2 * width), f32),
            jax.ShapeDtypeStruct((seq_len, 2), f32),
            jax.ShapeDtypeStruct((2, width), f32),
        ],
        compiler_params=pltpu.CompilerParams(vmem_limit_bytes=48 << 20),
        cost_estimate=pl.CostEstimate(flops=20 * seq_len * width, bytes_accessed=24 * seq_len * width, transcendentals=0),
        name="unturn",
    )(dqt, dk, qkv, inv_scale, gains, cos_two, sin_two)


class Job:
    def __init__(self, gather, scatter, merge, weights, pieces, dim, spread, tile_ins, outs, slots, sums, body):
        self.gather, self.scatter, self.merge, self.spread = gather, scatter, merge, spread
        self.weights, self.pieces, self.dim = weights, pieces, dim
        self.tile_ins, self.outs = tile_ins, outs
        self.slots, self.sums, self.body = slots, sums, body


def tile_kernel(job, tp, chunks, *refs):
    refs = list(refs)

    def take(count):
        got = refs[:count]
        del refs[:count]
        return got

    (src_ref,) = take(1)
    w_hbm = [take(max(1, job.pieces)) for _ in range(job.weights)]
    ti_hbm = take(job.tile_ins)
    quarter_ref = take(1)[0] if job.spread else None
    full_ref = take(1)[0] if job.gather else src_ref
    out_hbm = take(job.outs)
    w_out = take(job.weights) if job.pieces else None
    spread_ref = take(1)[0] if job.spread else None
    total_ref = take(1)[0] if job.scatter else None
    w_ref = take(job.weights)
    (tile_ref,) = take(1)
    ti_ref = take(job.tile_ins)
    out_ref = take(job.outs)
    y_ref, rbuf, zbuf, tbuf = take(4) if job.scatter else (None,) * 4
    w_sem, tile_sem, ti_sem, out_sem, loc_sem = take(5)
    t_send, t_recv, r_send, r_recv = take(4)
    y_send, y_recv, z_send, z_recv = take(4)
    wl_sem, wr_send, wr_recv, q_send, q_recv = take(5)

    n_dp = lax.axis_size("dp")
    d, r, g, t = (lax.axis_index(name) for name in ("dp", "row", "zh", "zl"))
    rows = tile_ref.shape[1]
    if job.merge:
        mc = rows // (2 * chunks)
        order = [(s, 0) for s in range(tp)]
    else:
        mc = rows // 2
        order = [(s, c) for c in range(chunks) for s in range(tp)]
    if not job.gather:
        order = [(s, c) for s in list(range(1, tp)) + [0] for c in range(chunks)]
    row_dev = (d, 1 - r, g, t)

    def peer(step):
        return (d, r, g, lax.rem(t + step + tp, tp))

    def remote(src, dst, send, recv, dev):
        return pltpu.make_async_remote_copy(
            src_ref=src, dst_ref=dst, send_sem=send, recv_sem=recv, device_id=dev,
            device_id_type=pl.DeviceIdType.MESH,
        )

    def piece(s, c, rho):
        return full_ref.at[pl.ds(((s * chunks + c) * 2 + rho) * mc, mc)]

    barrier = pltpu.get_barrier_semaphore()
    pl.semaphore_signal(barrier, inc=1, device_id=row_dev, device_id_type=pl.DeviceIdType.MESH)
    for s in range(1, tp):
        pl.semaphore_signal(barrier, inc=1, device_id=peer(s), device_id_type=pl.DeviceIdType.MESH)

    count = tp
    if job.spread:
        for k in range(1, n_dp):
            dev = (lax.rem(d + k, n_dp), r, g, t)
            pl.semaphore_signal(barrier, inc=1, device_id=dev, device_id_type=pl.DeviceIdType.MESH)
            count += 1
    same = r == g
    other_core = jnp.logical_not(same)

    def half_view(i, half, row_at, row_count, col_at, col_count):
        ref = w_ref[i]
        if job.dim == 0:
            size = ref.shape[0] // 2
            start = pl.multiple_of(half * size + row_at, row_count)
            return ref.at[pl.ds(start, row_count), pl.ds(col_at, col_count)]
        size = ref.shape[1] // 2
        return ref.at[pl.ds(row_at, row_count), pl.ds(pl.multiple_of(half * size + col_at, col_count), col_count)]

    def piece_list(i):
        if len(w_hbm[i]) == 2:
            other = w_hbm[i][1]
            return [(other, 0, other.shape[0], 0, other.shape[1])]
        one, two, one_x, one_y, two_y, two_x = w_hbm[i][1:]
        rows_q, cut = one.shape
        low_bit, high_bit = lax.rem(d, 2), d // 2
        places = [
            ((high_bit * (1 - 2 * (k // 2)) + k // 2) * 2 + low_bit * (1 - 2 * (k % 2)) + k % 2) * rows_q
            for k in range(4)
        ]
        upper, lower = pl.ds(0, rows_q), pl.ds(rows_q, rows_q)
        return [
            (one, places[0], rows_q, 0, cut),
            (one_x, places[1], rows_q, 0, cut),
            (one_y.at[upper], places[2], rows_q, 0, cut),
            (one_y.at[lower], places[3], rows_q, 0, cut),
            (two, places[0], rows_q, cut, cut),
            (two_x.at[upper], places[1], rows_q, cut, cut),
            (two_y, places[2], rows_q, cut, cut),
            (two_x.at[lower], places[3], rows_q, cut, cut),
        ]

    def piece_recv_places(i):
        return [half_view(i, 1 - r, *spot[1:]) for spot in piece_list(i)]

    def low_copies(i):
        low = w_hbm[i][0]
        there = half_view(i, r, 0, low.shape[0], 0, low.shape[1])
        here = half_view(i, 1 - r, 0, low.shape[0], 0, low.shape[1])
        keep = pltpu.make_async_copy(low, there, wl_sem.at[i, 0])
        give = pltpu.make_async_remote_copy(
            src_ref=low, dst_ref=there, send_sem=wr_send.at[i, 0], recv_sem=wr_recv.at[i, 0],
            device_id=row_dev, device_id_type=pl.DeviceIdType.MESH,
        )
        got = pltpu.make_async_remote_copy(
            src_ref=low, dst_ref=here, send_sem=wr_send.at[i, 0], recv_sem=wr_recv.at[i, 0],
            device_id=row_dev, device_id_type=pl.DeviceIdType.MESH,
        )
        return keep, give, got

    def part_copies(i):
        keeps, gives, gots = [], [], []
        for p, spot in enumerate(piece_list(i)):
            there = half_view(i, r, *spot[1:])
            here = piece_recv_places(i)[p]
            keeps.append(pltpu.make_async_copy(spot[0], there, wl_sem.at[i, p]))
            for dst, into in ((there, gives), (here, gots)):
                into.append(
                    pltpu.make_async_remote_copy(
                        src_ref=spot[0], dst_ref=dst, send_sem=wr_send.at[i, p], recv_sem=wr_recv.at[i, p],
                        device_id=row_dev, device_id_type=pl.DeviceIdType.MESH,
                    )
                )
        return keeps, gives, gots

    def w_start(i):
        if not job.pieces:
            pltpu.make_async_copy(w_hbm[i][0], w_ref[i], w_sem.at[i]).start()
            return

        @pl.when(same)
        def _():
            low_copies(i)[0].start()
            for cp in part_copies(i)[1]:
                cp.start()

        @pl.when(other_core)
        def _():
            low_copies(i)[1].start()
            for cp in part_copies(i)[0]:
                cp.start()

    def w_wait(i):
        if not job.pieces:
            pltpu.make_async_copy(w_hbm[i][0], w_ref[i], w_sem.at[i]).wait()
            return

        @pl.when(same)
        def _():
            low_copies(i)[0].wait()
            low_copies(i)[2].wait_recv()

        @pl.when(other_core)
        def _():
            for cp in part_copies(i)[0]:
                cp.wait()
            for cp in part_copies(i)[2]:
                cp.wait_recv()

        pltpu.make_async_copy(w_ref[i], w_out[i], w_sem.at[i]).start()

    def w_end(i):

        @pl.when(same)
        def _():
            for cp in part_copies(i)[1]:
                cp.wait_send()

        @pl.when(other_core)
        def _():
            low_copies(i)[1].wait_send()

        pltpu.make_async_copy(w_ref[i], w_out[i], w_sem.at[i]).wait()

    if not job.pieces:
        for i in range(job.weights):
            w_start(i)
    pl.semaphore_wait(barrier, count)
    seen = set()

    def need(i):
        if i not in seen:
            seen.add(i)
            w_wait(i)

    sends = []

    def go(cp):
        cp.start()
        sends.append(cp)

    local = {}
    if job.gather:
        for c in range(chunks):
            own = src_ref.at[pl.ds(c * mc, mc)]
            for s in range(1, tp):
                go(remote(own, piece(s, c, 0), t_send.at[s, c], t_recv.at[s, c], peer(-s)))
            local[c] = pltpu.make_async_copy(own, piece(0, c, 0), loc_sem.at[c])
            local[c].start()
            go(remote(own, piece(0, c, 1), r_send.at[0, c], r_recv.at[0, c], row_dev))

    if job.pieces:
        for i in range(job.weights):
            w_start(i)
    if job.spread:
        rows_q = quarter_ref.shape[0]
        mine = spread_ref.at[pl.ds(pl.multiple_of(d * rows_q, rows_q), rows_q)]
        q_local = pltpu.make_async_copy(quarter_ref, mine, q_send.at[0])
        q_local.start()
        for k in range(1, n_dp):
            go(remote(quarter_ref, mine, q_send.at[k], q_recv.at[k], (lax.rem(d + k, n_dp), r, g, t)))

    relayed = set()

    def relay(s, c):
        if job.gather and s > 0 and (s, c) not in relayed:
            relayed.add((s, c))
            remote(piece(s, c, 0), piece(s, c, 0), t_send.at[s, c], t_recv.at[s, c], peer(-s)).wait_recv()
            go(remote(piece(s, c, 0), piece(s, c, 1), r_send.at[s, c], r_recv.at[s, c], row_dev))

    def tile_load(i):
        s, c = order[i]
        at = pl.ds((s if job.merge else s * chunks + c) * rows, rows)
        return pltpu.make_async_copy(full_ref.at[at], tile_ref.at[i % 2], tile_sem.at[i % 2])

    def ti_loads(i):
        s, c = order[i]
        at = pl.ds((s if job.merge else s * chunks + c) * rows, rows)
        return [pltpu.make_async_copy(ti_hbm[j].at[at], ti_ref[j], ti_sem.at[j]) for j in range(job.tile_ins)]

    def out_copies(i):
        s, c = order[i]
        at = pl.ds((s if job.merge else s * chunks + c) * rows, rows)
        slot = i % job.slots
        return [
            pltpu.make_async_copy(out_ref[j].at[slot], out_hbm[j].at[at], out_sem.at[j, slot])
            for j in range(job.outs)
        ]

    def combine(i):
        s, c = order[i]
        k = s * chunks + c
        cp = remote(
            y_ref.at[i % job.sums, pl.ds(mc, mc)], rbuf.at[k], y_send.at[s, c], y_recv.at[s, c], row_dev
        )
        cp.wait()
        step = min(64, mc)

        def add(b, carry):
            at = pl.ds(pl.multiple_of(b * step, step), step)
            summed = y_ref[i % job.sums, at, :].astype(f32) + rbuf[k, at, :].astype(f32)
            if s == 0:
                total_ref[pl.ds(pl.multiple_of(c * mc + b * step, step), step), :] = summed
            else:
                zbuf[k - chunks, at, :] = summed.astype(bf16)
            return carry

        lax.fori_loop(0, mc // step, add, 0)
        if s > 0:
            go(remote(zbuf.at[k - chunks], tbuf.at[k - chunks], z_send.at[s, c], z_recv.at[s, c], peer(s)))

    for cp in ti_loads(0):
        cp.start()
    if not job.gather:
        tile_load(0).start()
    for i, (s, c) in enumerate(order):
        if job.gather:
            held = range(chunks) if job.merge else [c]
            for cc in held:
                relay(s, cc)
                if s == 0:
                    local[cc].wait()
            for cc in held:
                remote(piece(s, cc, 1), piece(s, cc, 1), r_send.at[s, cc], r_recv.at[s, cc], row_dev).wait_recv()
            tile_load(i).start()
        tile_load(i).wait()
        if not job.gather and i + 1 < len(order):
            tile_load(i + 1).start()
        for cp in ti_loads(i):
            cp.wait()
        if i >= job.slots:
            for cp in out_copies(i - job.slots):
                cp.wait()

        def mid(i=i):
            if i + 1 < len(order):
                relay(*order[i + 1])
                for cp in ti_loads(i + 1):
                    cp.start()
            if job.scatter:
                for cp in out_copies(i):
                    cp.start()
                if i >= 1:
                    combine(i - 1)

        outs = [ref.at[i % job.slots] for ref in out_ref]
        y = y_ref.at[i % job.sums] if job.scatter else None
        job.body(tile_ref.at[i % 2], w_ref, need, ti_ref, outs, y, mid)
        if job.scatter:
            k = s * chunks + c
            remote(y.at[pl.ds(mc, mc)], rbuf.at[k], y_send.at[s, c], y_recv.at[s, c], row_dev).start()
        else:
            for cp in out_copies(i):
                cp.start()
    last = len(order)
    for i in range(max(0, last - job.slots), last):
        for cp in out_copies(i):
            cp.wait()
    if job.scatter:
        combine(last - 1)
        for c in range(chunks):
            for s in range(1, tp):
                k = (s - 1) * chunks + c
                remote(zbuf.at[k], tbuf.at[k], z_send.at[s, c], z_recv.at[s, c], peer(s)).wait_recv()
                step = min(64, mc)

                def add(b, carry, k=k, c=c):
                    at = pl.ds(pl.multiple_of(b * step, step), step)
                    to = pl.ds(pl.multiple_of(c * mc + b * step, step), step)
                    total_ref[to, :] = total_ref[to, :] + tbuf[k, at, :].astype(f32)
                    return carry

                lax.fori_loop(0, mc // step, add, 0)
    if job.pieces:
        for i in range(job.weights):
            w_end(i)
    if job.spread:
        q_local.wait()
        for k in range(1, n_dp):
            came = lax.rem(d + n_dp - k, n_dp)
            remote(
                quarter_ref, spread_ref.at[pl.ds(pl.multiple_of(came * rows_q, rows_q), rows_q)],
                q_send.at[k], q_recv.at[k], row_dev,
            ).wait_recv()
    for cp in sends:
        cp.wait_send()


def tile_call(job, ident, name, src, weights, shapes, tile_ins, out_widths, sum_width, flops, quarter=None):
    tp = lax.axis_size("zl")
    n_dp = lax.axis_size("dp")
    flat_weights = [v for group in weights for v in group]
    width = src.shape[1]
    m = src.shape[0] if job.gather else src.shape[0] // (2 * tp)
    chunks = 2 if tp == 2 else 1
    mc = m // chunks
    rows = 2 * (m if job.merge else mc)
    total_rows = 2 * tp * m
    anywhere = pl.BlockSpec(memory_space=pl.ANY)
    dma = pltpu.SemaphoreType.DMA
    out_specs, out_shape = [], []
    if job.gather:
        out_specs.append(anywhere)
        out_shape.append(jax.ShapeDtypeStruct((total_rows, width), bf16))
    for w in out_widths:
        out_specs.append(anywhere)
        out_shape.append(jax.ShapeDtypeStruct((total_rows, w), bf16))
    if job.pieces:
        out_specs.extend([anywhere] * len(shapes))
        out_shape.extend(jax.ShapeDtypeStruct(shape, bf16) for shape in shapes)
    if job.spread:
        out_specs.append(anywhere)
        out_shape.append(jax.ShapeDtypeStruct((n_dp * quarter.shape[0], quarter.shape[1]), bf16))
    if job.scatter:
        out_specs.append(pl.BlockSpec(memory_space=pltpu.VMEM))
        out_shape.append(jax.ShapeDtypeStruct((m, sum_width), f32))
    scratch = [pltpu.VMEM(shape, bf16) for shape in shapes]
    scratch.append(pltpu.VMEM((2, rows, width), bf16))
    scratch.extend(pltpu.VMEM((rows, v.shape[1]), bf16) for v in tile_ins)
    scratch.extend(pltpu.VMEM((job.slots, rows, w), bf16) for w in out_widths)
    if job.scatter:
        scratch.append(pltpu.VMEM((job.sums, rows, sum_width), bf16))
        scratch.append(pltpu.VMEM((tp * chunks, mc, sum_width), bf16))
        scratch.append(pltpu.VMEM(((tp - 1) * chunks, mc, sum_width), bf16))
        scratch.append(pltpu.VMEM(((tp - 1) * chunks, mc, sum_width), bf16))
    scratch.extend(
        [dma((len(weights),)), dma((2,)), dma((max(1, len(tile_ins)),)), dma((max(1, job.outs), job.slots)), dma((chunks,))]
    )
    scratch.extend(dma((tp, chunks)) for _ in range(8))
    scratch.extend(dma((len(weights), 8)) for _ in range(3))
    scratch.extend(dma((n_dp,)) for _ in range(2))
    extra = [quarter] if job.spread else []
    return pl.pallas_call(
        functools.partial(tile_kernel, job, tp, chunks),
        in_specs=[anywhere] * (1 + len(flat_weights) + len(tile_ins) + len(extra)),
        out_specs=out_specs,
        out_shape=out_shape,
        scratch_shapes=scratch,
        compiler_params=pltpu.CompilerParams(
            collective_id=ident, has_side_effects=True, vmem_limit_bytes=60 << 20
        ),
        cost_estimate=pl.CostEstimate(flops=flops, bytes_accessed=8 * total_rows * width, transcendentals=0),
        name=name,
    )(src, *flat_weights, *tile_ins, *extra)


def columns(n, size):
    return pl.ds(pl.multiple_of(n * size, size), size)


def loop(first, last, step):
    def body(n, carry):
        step(n)
        return carry

    lax.fori_loop(first, last, body, 0)


def gate_up_body(tile, w, need, ti, outs, y, mid):
    hidden_width = w[0].shape[1]
    nb = min(512, hidden_width)
    count = hidden_width // nb
    need(0)
    need(1)

    def step(n):
        cols = columns(n, nb)
        rows = tile[...]
        gate = jnp.dot(rows, w[0][:, cols], preferred_element_type=f32)
        up = jnp.dot(rows, w[1][:, cols], preferred_element_type=f32)
        outs[0][:, cols] = gate.astype(bf16)
        outs[1][:, cols] = up.astype(bf16)
        outs[2][:, cols] = (gate * jax.nn.sigmoid(gate) * up).astype(bf16)

    loop(0, count // 2, step)
    mid()
    loop(count // 2, count, step)


def down_body(tile, w, need, ti, outs, y, mid):
    nb = min(1024, w[0].shape[1])
    count = w[0].shape[1] // nb
    need(0)

    def step(n):
        cols = columns(n, nb)
        y[:, cols] = jnp.dot(tile[...], w[0][:, cols], preferred_element_type=f32).astype(bf16)

    loop(0, count // 2, step)
    mid()
    loop(count // 2, count, step)


def back_body(tile, w, need, ti, outs, y, mid):
    hidden_width = w[0].shape[0]
    nb = min(512, hidden_width)
    need(0)

    def first(n):
        cols = columns(n, nb)
        grad = lax.dot_general(tile[...], w[0][cols, :], NT, preferred_element_type=f32)
        grad = grad.astype(bf16).astype(f32)
        gate = ti[0][:, cols].astype(f32)
        up = ti[1][:, cols].astype(f32)
        sig = jax.nn.sigmoid(gate)
        passed = grad * sig
        outs[0][:, cols] = (passed * up * (1.0 + gate * (1.0 - sig))).astype(bf16)
        outs[1][:, cols] = (passed * gate).astype(bf16)

    loop(0, hidden_width // nb, first)
    mid()
    need(1)
    need(2)
    nd = 512

    def second(n):
        cols = columns(n, nd)
        grad = lax.dot_general(outs[0][...], w[1][cols, :], NT, preferred_element_type=f32)
        grad = grad + lax.dot_general(outs[1][...], w[2][cols, :], NT, preferred_element_type=f32)
        y[:, cols] = grad.astype(bf16)

    loop(0, w[1].shape[0] // nd, second)


gate_up_job = Job(True, False, True, 2, 7, 0, True, 0, 3, 2, 0, gate_up_body)
down_job = Job(False, True, False, 1, 2, 1, False, 0, 0, 1, 2, down_body)
back_job = Job(True, True, False, 3, 0, 0, False, 2, 2, 1, 1, back_body)


def last_kernel(
    chunks, dx_ref, grad_ref, out_ref, sum_ref, own, from_row, near, from_t, give, from_zh,
    g_own, g_in, g_sum, g_late,
    own_sem, row_send, row_recv, t_send, t_recv, zh_send, zh_recv, g_sem, d_send, d_recv, f_send, f_recv,
):
    n_dp = lax.axis_size("dp")
    tp = lax.axis_size("zl")
    d, r, g, t = (lax.axis_index(name) for name in ("dp", "row", "zh", "zl"))
    same = r == g
    other_core = jnp.logical_not(same)
    seq_len, width = dx_ref.shape
    half = width // 2
    feat = half // (2 * tp)
    step = seq_len // chunks
    part = g_own.shape[1]

    def remote(src, dst, send, recv, dev):
        return pltpu.make_async_remote_copy(
            src_ref=src, dst_ref=dst, send_sem=send, recv_sem=recv, device_id=dev,
            device_id_type=pl.DeviceIdType.MESH,
        )

    row_dev = (d, 1 - r, g, t)
    zh_dev = (d, r, 1 - g, t)
    cross_dev = (d, 1 - r, 1 - g, t)

    def dp_dev(k):
        return (lax.rem(d + k, n_dp), r, g, t)

    def t_dev(s):
        return (d, r, g, lax.rem(t + s, tp))

    partners = [row_dev, zh_dev, cross_dev]
    partners += [dp_dev(k) for k in range(1, n_dp)] + [t_dev(s) for s in range(1, tp)]
    barrier = pltpu.get_barrier_semaphore()
    for dev in partners:
        pl.semaphore_signal(barrier, inc=1, device_id=dev, device_id_type=pl.DeviceIdType.MESH)
    pl.semaphore_wait(barrier, len(partners))

    def cols_at(which):
        return pl.ds(pl.multiple_of(which * half, half), half)

    rows_copies, own_copies = [], []
    for c in range(chunks):
        rows = pl.ds(c * step, step)
        cp = remote(dx_ref.at[rows, cols_at(1 - r)], from_row.at[c], row_send.at[c], row_recv.at[c], row_dev)
        cp.start()
        rows_copies.append(cp)
        cp = pltpu.make_async_copy(dx_ref.at[rows, cols_at(r)], own.at[c], own_sem.at[c])
        cp.start()
        own_copies.append(cp)

    def grad_rows(which, group):
        return grad_ref.at[pl.ds(pl.multiple_of((which * n_dp + group) * part, part), part)]

    g_copies, g_loads = [], []
    for which in range(2):
        cp = pltpu.make_async_copy(grad_rows(which, d), g_own.at[which], g_sem.at[which])
        cp.start()
        g_loads.append(cp)
        for k in range(1, n_dp):
            cp = remote(
                grad_rows(which, lax.rem(d + k, n_dp)), g_in.at[k - 1, which],
                d_send.at[k, which], d_recv.at[k, which], dp_dev(k),
            )
            cp.start()
            g_copies.append(cp)

    t_copies = {}

    def row_stage(c):
        own_copies[c].wait()
        rows_copies[c].wait_recv()
        total = own[c].astype(f32) + from_row[c].astype(f32)
        for b in range(2 * tp):
            near[c, b] = total[:, b * feat : (b + 1) * feat].astype(bf16)
        for zh in range(2):
            for s in range(1, tp):
                cp = remote(
                    near.at[c, zh * tp + lax.rem(t + s, tp)], from_t.at[c, zh, s - 1],
                    t_send.at[c, zh, s], t_recv.at[c, zh, s], t_dev(s),
                )
                cp.start()
                t_copies[(c, zh, s)] = cp

    zh_copies = []

    def t_stage(c):
        for zh in range(2):
            for s in range(1, tp):
                t_copies[(c, zh, s)].wait_recv()

        def total_of(zh):
            total = near[c, zh * tp + t].astype(f32)
            for s in range(1, tp):
                total = total + from_t[c, zh, s - 1].astype(f32)
            return total

        give[c] = total_of(1 - g).astype(bf16)
        cp = remote(give.at[c], from_zh.at[c], zh_send.at[c], zh_recv.at[c], zh_dev)
        cp.start()
        zh_copies.append(cp)
        out_ref[pl.ds(pl.multiple_of(g * seq_len + c * step, step), step), :] = total_of(g)

    def grad_stage():
        for cp in g_loads:
            cp.wait()
        for cp in g_copies:
            cp.wait_recv()
        block = min(64, part)
        for which in range(2):

            def add(i, carry, which=which):
                at = pl.ds(pl.multiple_of(i * block, block), block)
                total = g_own[which, at, :].astype(f32)
                for k in range(n_dp - 1):
                    total = total + g_in[k, which, at, :].astype(f32)
                g_sum[which, at, :] = total.astype(bf16)
                return carry

            lax.fori_loop(0, part // block, add, 0)

    to_row = remote(g_sum.at[1 - r], g_late.at[0], f_send.at[0], f_recv.at[0], row_dev)
    to_zh = remote(g_sum.at[r], g_late.at[0], f_send.at[1], f_recv.at[1], zh_dev)
    to_cross = remote(g_sum.at[1 - r], g_late.at[1], f_send.at[2], f_recv.at[2], cross_dev)

    for c in range(chunks):
        row_stage(c)
        if c >= 2:
            t_stage(c - 2)
    grad_stage()

    @pl.when(same)
    def _():
        to_row.start()

    @pl.when(other_core)
    def _():
        to_zh.start()
        to_cross.start()

    for c in range(max(0, chunks - 2), chunks):
        t_stage(c)
    for c in range(chunks):
        zh_copies[c].wait_recv()
        out_ref[pl.ds(pl.multiple_of((1 - g) * seq_len + c * step, step), step), :] = from_zh[c].astype(f32)

    @pl.when(same)
    def _():
        to_zh.wait_recv()
        sum_ref[...] = g_sum[r].astype(f32) + g_late[0].astype(f32)
        to_row.wait_send()

    @pl.when(other_core)
    def _():
        to_row.wait_recv()
        to_cross.wait_recv()
        sum_ref[...] = g_late[0].astype(f32) + g_late[1].astype(f32)
        to_zh.wait_send()
        to_cross.wait_send()

    for cp in rows_copies + g_copies + list(t_copies.values()) + zh_copies:
        cp.wait_send()


def last_sums(dx, grad):
    n_dp = lax.axis_size("dp")
    tp = lax.axis_size("zl")
    seq_len, width = dx.shape
    chunks = 4
    half = width // 2
    feat = half // (2 * tp)
    step = seq_len // chunks
    part = grad.shape[0] // (2 * n_dp)
    cols = grad.shape[1]
    anywhere = pl.BlockSpec(memory_space=pl.ANY)
    vmem = pl.BlockSpec(memory_space=pltpu.VMEM)
    dma = pltpu.SemaphoreType.DMA
    return pl.pallas_call(
        functools.partial(last_kernel, chunks),
        in_specs=[anywhere] * 2,
        out_specs=[vmem] * 2,
        out_shape=[
            jax.ShapeDtypeStruct((2 * seq_len, feat), f32),
            jax.ShapeDtypeStruct((part, cols), f32),
        ],
        scratch_shapes=[
            pltpu.VMEM((chunks, step, half), bf16),
            pltpu.VMEM((chunks, step, half), bf16),
            pltpu.VMEM((chunks, 2 * tp, step, feat), bf16),
            pltpu.VMEM((chunks, 2, tp - 1, step, feat), bf16),
            pltpu.VMEM((chunks, step, feat), bf16),
            pltpu.VMEM((chunks, step, feat), bf16),
            pltpu.VMEM((2, part, cols), bf16),
            pltpu.VMEM((n_dp - 1, 2, part, cols), bf16),
            pltpu.VMEM((2, part, cols), bf16),
            pltpu.VMEM((2, part, cols), bf16),
            dma((chunks,)),
            dma((chunks,)),
            dma((chunks,)),
            dma((chunks, 2, tp)),
            dma((chunks, 2, tp)),
            dma((chunks,)),
            dma((chunks,)),
            dma((2,)),
            dma((n_dp, 2)),
            dma((n_dp, 2)),
            dma((3,)),
            dma((3,)),
        ],
        compiler_params=pltpu.CompilerParams(collective_id=4, has_side_effects=True, vmem_limit_bytes=60 << 20),
        cost_estimate=pl.CostEstimate(flops=0, bytes_accessed=8 * seq_len * width, transcendentals=0),
        name="last_sums",
    )(dx, grad)


def rotary(seq_len):
    half_width = HD // 2
    freqs = rope_base ** (-(jnp.arange(half_width, dtype=f32) * 2.0) / HD)
    angles = jnp.arange(seq_len, dtype=f32)[:, None] * freqs[None, :]
    cos_table, sin_table = jnp.cos(angles), jnp.sin(angles)
    return (
        jnp.concatenate([cos_table, cos_table], axis=1),
        jnp.concatenate([-sin_table, sin_table], axis=1),
    )


def norm_scale(vals):
    return lax.rsqrt(jnp.mean(vals * vals, axis=1, keepdims=True) + norm_eps)


def norm_back(pre_vals, scale, gains, gradient):
    weighted = gradient * gains
    inner = jnp.mean(weighted * pre_vals, axis=1, keepdims=True)
    grad_pre = scale * weighted - pre_vals * (scale * scale * scale * inner)
    grad_gain = jnp.sum(gradient * pre_vals * scale, axis=0)
    return grad_pre, grad_gain


def adamw_step(weight, gradient, first_mom, second_mom, step_rate, decay_rate):
    first_new = beta_one * first_mom + (1.0 - beta_one) * gradient
    second_new = beta_two * second_mom + (1.0 - beta_two) * gradient * gradient
    fix_one = 1.0 - beta_one**STEP
    fix_two = 1.0 - beta_two**STEP
    direction = first_new / fix_one / (jnp.sqrt(second_new / fix_two) + adam_eps)
    return (first_new, second_new, weight - step_rate * (direction + decay_rate * weight))


def matmul(left, right, dims=NN):
    return lax.dot_general(left, right, dims, preferred_element_type=f32)


def shards(
    tokens, cotangent, doc_lengths, qkv_weight, out_weight, gate_weight, up_weight, down_weight,
    head_gains, post_gains, qkv_first, qkv_second, out_first, out_second, gate_first, gate_second,
    up_first, up_second, down_first, down_second, head_first, head_second, post_first, post_second,
):
    n_dp = lax.axis_size("dp")
    tp = lax.axis_size("zl")
    group = 2 * tp
    n_col = 2 * tp
    d, r, g, t = (lax.axis_index(name) for name in ("dp", "row", "zh", "zl"))
    same = r == g
    block_at = r * tp + t
    rows_dev, feat = tokens.shape
    width = feat * 2 * n_col
    seq_len = rows_dev // 2
    mine = seq_len // group
    col_width = qkv_weight.shape[2]

    ends = jnp.cumsum(jnp.where(same, doc_lengths, swap(doc_lengths, "row")), axis=1)[0]

    qkv_low = jnp.concatenate([qkv_weight[:, i, :].astype(bf16) for i in range(3)], axis=1)
    x_full, qkv_full, post_all = first_gather(tokens, qkv_low, post_gains.T)
    x_tok = lax.dynamic_slice_in_dim(x_full, block_at * mine, mine, 0)

    def halves(quarter):
        cut = quarter.shape[1] // 2
        return quarter[:, :cut], quarter[:, cut:]

    def gathered(one, two, one_x, two_y):
        one_y = swap_bit(jnp.concatenate([one, one_x]), "dp", 2)
        two_x = swap_bit(jnp.concatenate([two, two_y]), "dp", 1)
        return [one, two, one_x, one_y, two_y, two_x]

    def quarter_of(weight):
        rows = weight.shape[0] // n_dp
        return lax.dynamic_slice_in_dim(weight, d * rows, rows, 0).astype(bf16)

    gate_one, gate_two = halves(quarter_of(gate_weight))
    gate_one, gate_two, post_all = tie(gate_one, gate_two, post_all)
    gate_one = swap(gate_one, "zh")

    out_rows = out_weight.shape[0] // n_dp
    out_part = lax.dynamic_slice_in_dim(out_weight, d * out_rows, out_rows, 0).astype(bf16)
    out_part, post_all = tie(lax.all_gather(out_part, ("zh", "zl"), axis=0), post_all)
    out_part = lax.all_gather(out_part, "dp", axis=1)

    cos_two, sin_two = rotary(seq_len)
    gains = jnp.where(same, head_gains, swap(head_gains, "zh"))
    qkv = matmul(x_full, qkv_full)
    squares = jnp.stack(
        [
            jnp.sum(jnp.square(qkv[:, :col_width]), axis=1),
            jnp.sum(jnp.square(qkv[:, col_width : 2 * col_width]), axis=1),
        ],
        axis=0,
    )
    inv_scale = lax.rsqrt(small_sum(squares, ("row", "zl")) / width + norm_eps).T
    gate_two = swap(gate_two, "zh")
    up_one, up_two = halves(quarter_of(up_weight))
    up_one, up_two = swap(up_one, "zh"), swap(up_two, "zh")
    down_quarter = swap(quarter_of(down_weight), "zh")
    inv_scale, gate_one = tie(inv_scale, gate_one)
    query, key, key_t, value, value_t = prepare(qkv, inv_scale, gains, cos_two, sin_two)
    ends, gate_two = tie(ends, gate_two)
    gate_one_x, gate_two_y = swap_bit(gate_one, "dp", 1), swap_bit(gate_two, "dp", 2)
    out_part, key_t = tie(out_part, key_t)
    out_full = lax.all_gather(out_part.reshape(width, width // 2), "row", axis=1, tiled=True)
    att, log_total = attend(query, key, value_t, ends)
    att, up_one, gate_one_x, gate_two_y = tie(att, up_one, gate_one_x, gate_two_y)
    gate_pieces = gathered(gate_one, gate_two, gate_one_x, gate_two_y)

    def to_tokens(vals):
        got = lax.all_to_all(vals.reshape(group, mine, col_width), ("row", "zl"), 0, 0)
        return got.transpose(1, 0, 2).reshape(mine, width)

    def to_heads(vals):
        sent = vals.reshape(mine, group, col_width).transpose(1, 0, 2)
        return lax.all_to_all(sent, ("row", "zl"), 0, 0).reshape(seq_len, col_width)

    att_tok = to_tokens(att)

    gain_attn, gain_mlp = post_all[0:1], post_all[1:2]
    att_tok, up_two, gate_pieces[3], gate_pieces[5] = tie(att_tok, up_two, gate_pieces[3], gate_pieces[5])
    a_pre = matmul(att_tok, out_full)
    a_scale = norm_scale(a_pre)
    h_tok = x_tok.astype(f32) + a_pre * a_scale * gain_attn

    cot = cotangent.reshape(2, 2, tp, mine, feat).transpose(1, 0, 2, 3, 4).reshape(2 * n_col, mine, feat)
    cot, a_scale = tie(cot, a_scale)
    cot = lax.all_to_all(cot, ("row", "zh", "zl"), 0, 0)
    cot_tok = cot.transpose(1, 0, 2).reshape(mine, width).astype(f32)

    up_pieces = gathered(up_one, up_two, swap_bit(up_one, "dp", 1), swap_bit(up_two, "dp", 2))
    gate_low, up_low, down_low = (
        v.astype(bf16) for v in (gate_weight, up_weight, down_weight)
    )
    hidden_width = gate_low.shape[1]
    work = 2 * seq_len * width * hidden_width
    wide, tall = (width, hidden_width), (hidden_width, width)
    h_full, gate_all, up_all, hidden, gate_full, up_full, down_other = tile_call(
        gate_up_job, 1, "gate_up", h_tok.astype(bf16), [[gate_low, *gate_pieces], [up_low, *up_pieces]],
        [wide, wide], [], [hidden_width] * 3, 0, 2 * work, down_quarter,
    )
    down_full, m_pre = tile_call(
        down_job, 2, "down", hidden, [[down_low, down_other]], [tall], [], [], width, work
    )
    m_scale = norm_scale(m_pre)
    mixed_tok = (h_tok + m_pre * m_scale * gain_mlp).astype(bf16)

    def to_features(vals):
        out = lax.all_to_all(
            vals.reshape(mine, 2 * n_col, feat).transpose(1, 0, 2), ("row", "zh", "zl"), 0, 0
        )
        return out.reshape(2, 2, tp, mine, feat).transpose(1, 0, 2, 3, 4).reshape(rows_dev, feat)

    mixed = to_features(mixed_tok)

    grad_m, grad_gain_mlp = norm_back(m_pre, m_scale, gain_mlp, cot_tok)
    dm_full, grad_gate, grad_up, dh_sum = tile_call(
        back_job, 3, "feed_back", grad_m.astype(bf16), [[down_full], [gate_full], [up_full]], [tall, wide, wide],
        [gate_all, up_all], [hidden_width] * 2, width, 3 * work,
    )
    grad_down_w = matmul(hidden, dm_full, TN).astype(bf16)
    grad_gate_w = matmul(h_full, grad_gate, TN).astype(bf16)
    grad_up_w = matmul(h_full, grad_up, TN).astype(bf16)
    dh_tok = cot_tok + dh_sum

    low_bit, high_bit = d % 2, d // 2

    def pick(vals, dim, index):
        return lax.dynamic_slice_in_dim(vals, index, 1, dim)

    def trade(vals, dim, bit, index):
        got = swap_bit(pick(vals, dim, 1 - index), "dp", bit)
        return (pick(vals, dim, index).astype(f32) + got.astype(f32)).astype(bf16)

    view = grad_down_w.reshape(n_dp // 2, 2, hidden_width // n_dp, width)
    down_one = trade(view[..., : width // 2], 1, 1, low_bit)
    down_two = trade(view[..., width // 2 :], 0, 2, high_bit)

    grad_a, grad_gain_attn = norm_back(a_pre, a_scale, gain_attn, dh_tok)
    grad_a = grad_a.astype(bf16)
    grad_att = to_heads(matmul(grad_a, out_full, NT).astype(bf16))
    grad_out = matmul(att_tok, grad_a, TN).astype(bf16)

    ends, down_one, down_two = tie(ends, down_one, down_two)
    dqt, dk, dv = attend_back(query, key, key_t, value, grad_att, att, log_total, ends)
    down_one = trade(down_one, 0, 2, high_bit)[0, 0]
    down_two = trade(down_two, 1, 1, low_bit)[0, 0]
    inv_scale, down_one, down_two = tie(inv_scale, down_one, down_two)
    weighted, inner, grad_head = unturn(dqt, dk, qkv, inv_scale, gains, cos_two, sin_two)
    inner = (small_sum(inner.T, ("row", "zl")) / width).T
    cube = inv_scale * inv_scale * inv_scale * inner
    dqkv = jnp.concatenate(
        [
            (inv_scale[:, 0:1] * weighted[:, :col_width] - qkv[:, :col_width] * cube[:, 0:1]).astype(bf16),
            (inv_scale[:, 1:2] * weighted[:, col_width:] - qkv[:, col_width : 2 * col_width] * cube[:, 1:2]).astype(bf16),
            dv,
        ],
        axis=1,
    )
    grad_qkv = matmul(x_full, dqkv, TN).astype(bf16)

    dx = matmul(dqkv, qkv_full, NT).astype(bf16)
    here = lax.dynamic_slice_in_dim(dx, block_at * mine, mine, 0).astype(f32) + dh_tok
    dx = lax.dynamic_update_slice_in_dim(dx, here.astype(bf16), block_at * mine, 0)
    dtokens, sum_qkv = last_sums(dx, grad_qkv)
    sum_qkv = sum_qkv.reshape(qkv_first.shape)

    def data_sums(grad):
        half = grad.shape[0] // 2
        return [
            lax.psum_scatter(grad[i * half : (i + 1) * half], "dp", scatter_dimension=0, tiled=True)
            for i in range(2)
        ]

    def to_owner(pieces):
        keep = jnp.where(r == 0, pieces[0], pieces[1])
        give = jnp.where(r == 0, pieces[1], pieces[0])
        axes = ("row", "zh")
        total = jnp.where(same, keep.astype(f32), 0.0)
        total = total + lax.ppermute(keep, axes, [(1, 0), (2, 3)]).astype(f32)
        total = total + lax.ppermute(give, axes, [(1, 2), (2, 1)]).astype(f32)
        return total + lax.ppermute(give, axes, [(0, 2), (3, 1)]).astype(f32)

    sum_down = to_owner([down_one, down_two])
    gate_sums, up_sums = data_sums(grad_gate_w), data_sums(grad_up_w)
    *gate_sums, grad_head = tie(*gate_sums, grad_head)
    *up_sums, sum_qkv = tie(*up_sums, sum_qkv)
    sum_gate = to_owner(gate_sums)
    sum_up = to_owner(up_sums)
    half_w = width // 2
    half = lax.dynamic_slice_in_dim(grad_out, r * half_w, half_w, 1).astype(f32) + swap(
        lax.dynamic_slice_in_dim(grad_out, (1 - r) * half_w, half_w, 1), "row"
    ).astype(f32)
    half = half.astype(bf16).reshape(n_col, n_dp, out_rows, width // 2)
    half = lax.psum_scatter(half, "dp", scatter_dimension=1, tiled=False)
    sum_out = lax.psum_scatter(half, ("zh", "zl"), scatter_dimension=0, tiled=False).astype(f32)

    head_place = lax.dynamic_update_slice_in_dim(
        jnp.zeros((2, width), f32), grad_head, block_at * col_width, 1
    )
    small = jnp.concatenate([head_place, grad_gain_attn[None], grad_gain_mlp[None]], axis=0)
    small = small_sum(small, ("dp", "row", "zh", "zl"))
    col_at = g * tp + t
    sum_head = lax.dynamic_slice_in_dim(small[:2], col_at * col_width, col_width, 1)
    post_rows = post_first.shape[0]
    sum_post = lax.dynamic_slice_in_dim(
        small[2:], ((r * n_col + col_at) * n_dp + d) * post_rows, post_rows, 1
    ).T

    def owned_rows(weight, part_rows):
        return lax.dynamic_slice_in_dim(weight, d * part_rows, part_rows, 0)

    results = []
    for weight, total, first, second in (
        (qkv_weight, sum_qkv, qkv_first, qkv_second),
        (out_weight, sum_out, out_first, out_second),
        (gate_weight, sum_gate, gate_first, gate_second),
        (up_weight, sum_up, up_first, up_second),
        (down_weight, sum_down, down_first, down_second),
    ):
        results.extend(
            adamw_step(owned_rows(weight, total.shape[0]), total, first, second, rate_matrix, weight_decay)
        )
    results.extend(adamw_step(head_gains, sum_head, head_first, head_second, rate_gain, 0.0))
    results.extend(
        adamw_step(owned_rows(post_gains, post_rows), sum_post, post_first, post_second, rate_gain, 0.0)
    )
    return (mixed, dtokens, *results)


def solution(mesh):
    n_dp, n_row, n_col = (mesh.shape[name] for name in ("dp", "row", "col"))
    grid = Mesh(mesh.devices.reshape(n_dp, n_row, 2, n_col // 2), ("dp", "row", "zh", "zl"))
    col = ("zh", "zl")
    moved = P("dp", ("row", *col))
    qkv_part = P(("row", "dp"), None, col)
    flat_part = P((*col, "dp"), "row")
    wide_part = P(("row", "dp"), col)
    head_part = P(None, col)
    post_part = P(("row", *col, "dp"), None)
    in_specs = (
        moved,
        moved,
        P(("dp", "row"), None),
        P("row", None, col),
        P(col, "row"),
        P("row", col),
        P("row", col),
        P(col, "row"),
        head_part,
        P(("row", *col), None),
        *[spec for spec in (qkv_part, flat_part, wide_part, wide_part, flat_part, head_part, post_part) for _ in range(2)],
    )
    out_specs = (
        moved,
        moved,
        *[spec for spec in (qkv_part, flat_part, wide_part, wide_part, flat_part, head_part, post_part) for _ in range(3)],
    )
    return jax.shard_map(shards, mesh=grid, in_specs=in_specs, out_specs=out_specs, check_vma=False)
```

```python
import functools

import jax
import jax.numpy as jnp
from jax import lax
from jax.experimental import pallas as pl
from jax.experimental.pallas import tpu as pltpu
from jax.sharding import Mesh
from jax.sharding import PartitionSpec as P

HD = 128
STEP = 10

norm_eps = 1e-06
rope_base = 500000.0
beta_one = 0.9
beta_two = 0.95
adam_eps = 1e-08
weight_decay = 0.1
rate_matrix = 0.02
rate_gain = 0.6
big_negative = -1e30
log2_e = 1.4426950408889634

f32 = jnp.float32
bf16 = jnp.bfloat16
NN = (((1,), (0,)), ((), ()))
NT = (((1,), (1,)), ((), ()))
TN = (((0,), (0,)), ((), ()))


def swap(piece, axis):
    return lax.ppermute(piece, axis, [(0, 1), (1, 0)])


def shift(piece, axis, step):
    size = lax.axis_size(axis)
    return lax.ppermute(piece, axis, [(i, (i + step) % size) for i in range(size)])


def swap_bit(piece, axis, bit):
    return lax.ppermute(piece, axis, [(i, i ^ bit) for i in range(lax.axis_size(axis))])


def small_sum(vals, axes):
    for axis in axes:
        bit = 1
        while bit < lax.axis_size(axis):
            vals = vals + swap_bit(vals, axis, bit)
            bit *= 2
    return vals


def tie(*vals):
    return lax.optimization_barrier(vals)


def small_sum(vals, axes):
    for axis in axes:
        bit = 1
        while bit < lax.axis_size(axis):
            vals = vals + swap_bit(vals, axis, bit)
            bit *= 2
    return vals


def gather_kernel(
    chunks, tok_ref, low_ref, post_ref, x_ref, w_ref, all_ref, ex_ref,
    own_sem, zh_send, zh_recv, t_send, t_recv, r_send, r_recv,
    wz_send, wz_recv, wd_send, wd_recv, wr_send, wr_recv, wl_sem, p_send, p_recv,
):
    n_dp = lax.axis_size("dp")
    tp = lax.axis_size("zl")
    d, r, g, t = (lax.axis_index(name) for name in ("dp", "row", "zh", "zl"))
    same = r == g
    feat = tok_ref.shape[1]
    seq_len = tok_ref.shape[0] // 2
    step = seq_len // chunks
    half = low_ref.shape[0]
    rows = half // n_dp

    def place(row, zh, zl):
        return (row * 2 + zh) * tp + zl

    def land(block, c):
        return x_ref.at[block, pl.ds(c * step, step)]

    def remote(src, dst, send, recv, dev):
        return pltpu.make_async_remote_copy(
            src_ref=src, dst_ref=dst, send_sem=send, recv_sem=recv, device_id=dev,
            device_id_type=pl.DeviceIdType.MESH,
        )

    barrier = pltpu.get_barrier_semaphore()
    count = 0
    for dd in range(n_dp):
        for rr in range(2):
            if dd or rr:
                dev = (lax.rem(d + dd, n_dp), lax.rem(r + rr, 2), g, t)
                pl.semaphore_signal(barrier, inc=1, device_id=dev, device_id_type=pl.DeviceIdType.MESH)
                count += 1
    for rr in range(2):
        for gg in range(2):
            for tt in range(tp):
                if gg or tt:
                    dev = (d, lax.rem(r + rr, 2), lax.rem(g + gg, 2), lax.rem(t + tt, tp))
                    pl.semaphore_signal(barrier, inc=1, device_id=dev, device_id_type=pl.DeviceIdType.MESH)
                    count += 1
    pl.semaphore_wait(barrier, count)

    row_dev = (d, 1 - r, g, t)
    zh_dev = (d, r, 1 - g, t)
    mine = place(r, g, t)
    pending = []

    wz = remote(low_ref.at[pl.ds(pl.multiple_of(d * rows, rows), rows)], ex_ref, wz_send, wz_recv, zh_dev)
    wz.start()

    def own_src(c):
        return tok_ref.at[pl.ds(pl.multiple_of(g * seq_len + c * step, step), step)]

    zh_copies = []
    for c in range(chunks):
        src = tok_ref.at[pl.ds(pl.multiple_of((1 - g) * seq_len + c * step, step), step)]
        zh_copies.append(remote(src, land(mine, c), zh_send.at[c], zh_recv.at[c], zh_dev))
        for s in range(1, tp):
            cp = remote(
                own_src(c), land(mine, c), t_send.at[s, 0, c], t_recv.at[s, 0, c], (d, r, g, lax.rem(t + s, tp))
            )
            cp.start()
            pending.append(cp)
    local = []
    for c in range(chunks):
        cp = pltpu.make_async_copy(own_src(c), land(mine, c), own_sem.at[c])
        cp.start()
        local.append(cp)
        cp = remote(own_src(c), land(mine, c), r_send.at[0, 0, c], r_recv.at[0, 0, c], row_dev)
        cp.start()
        pending.append(cp)

    wz.wait_send()
    lead = max(1, chunks // 4)
    for cp in zh_copies[:lead]:
        cp.start()

    half_at = pl.ds(pl.multiple_of(r * half, half), half)
    w_row = remote(low_ref, w_ref.at[half_at], wr_send, wr_recv, row_dev)
    w_loc = pltpu.make_async_copy(low_ref, w_ref.at[half_at], wl_sem.at[0])

    @pl.when(same)
    def _():
        w_loc.start()

    @pl.when(jnp.logical_not(same))
    def _():
        w_row.start()

    posts = []
    n_all = 4 * tp
    p_loc = pltpu.make_async_copy(post_ref, all_ref.at[mine], wl_sem.at[1])
    p_loc.start()
    index = 0
    for rr in range(2):
        for gg in range(2):
            for tt in range(tp):
                if rr or gg or tt:
                    dev = (d, lax.rem(r + rr, 2), lax.rem(g + gg, 2), lax.rem(t + tt, tp))
                    cp = remote(post_ref, all_ref.at[mine], p_send.at[index], p_recv.at[index], dev)
                    cp.start()
                    posts.append(cp)
                    index += 1

    def drain_zh(c):
        zh_copies[c].wait_recv()
        theirs = place(r, 1 - g, t)
        for s in range(1, tp):
            cp = remote(
                land(theirs, c), land(theirs, c), t_send.at[s, 1, c], t_recv.at[s, 1, c],
                (d, r, g, lax.rem(t + s, tp)),
            )
            cp.start()
            pending.append(cp)
        cp = remote(land(theirs, c), land(theirs, c), r_send.at[0, 1, c], r_recv.at[0, 1, c], row_dev)
        cp.start()
        pending.append(cp)

    def drain_t(z, c):
        for s in range(1, tp):
            came = place(r, g if z == 0 else 1 - g, lax.rem(t + tp - s, tp))
            remote(
                land(came, c), land(came, c), t_send.at[s, z, c], t_recv.at[s, z, c],
                (d, r, g, lax.rem(t + s, tp)),
            ).wait_recv()
            cp = remote(land(came, c), land(came, c), r_send.at[s, z, c], r_recv.at[s, z, c], row_dev)
            cp.start()
            pending.append(cp)

    wz.wait_recv()
    spot = pl.ds(pl.multiple_of(r * half + d * rows, rows), rows)
    far = []
    for dd in range(1, n_dp):
        cp = remote(
            ex_ref, w_ref.at[spot], wd_send.at[dd], wd_recv.at[dd, r], (lax.rem(d + dd, n_dp), 1 - g, g, t)
        )
        cp.start()
        far.append(cp)
        for late in zh_copies[lead:][dd - 1 : dd]:
            late.start()
    for late in zh_copies[lead:][n_dp - 1 :]:
        late.start()
    near_remote = remote(ex_ref, w_ref.at[spot], wd_send.at[0], wd_recv.at[0, r], row_dev)
    near_local = pltpu.make_async_copy(ex_ref, w_ref.at[spot], wl_sem.at[2])

    @pl.when(same)
    def _():
        near_remote.start()

    @pl.when(jnp.logical_not(same))
    def _():
        near_local.start()

    for c in range(chunks):
        drain_t(0, c)
        drain_zh(c)
        if c >= 1:
            drain_t(1, c - 1)
    drain_t(1, chunks - 1)

    for c in range(chunks):
        for z in range(2):
            for s in range(tp):
                came = place(1 - r, g if z == 0 else 1 - g, lax.rem(t + tp - s, tp))
                remote(
                    land(came, c), land(came, c), r_send.at[s, z, c], r_recv.at[s, z, c], row_dev
                ).wait_recv()
    for cp in local:
        cp.wait()
    for cp in pending:
        cp.wait_send()
    for cp in zh_copies:
        cp.wait_send()
    p_loc.wait()
    for cp in posts:
        cp.wait_send()
    index = 0
    for rr in range(2):
        for gg in range(2):
            for tt in range(tp):
                if rr or gg or tt:
                    came = place(
                        lax.rem(r + 2 - rr, 2), lax.rem(g + 2 - gg, 2), lax.rem(t + tp - tt, tp)
                    )
                    remote(
                        post_ref, all_ref.at[came], p_send.at[index], p_recv.at[index], row_dev
                    ).wait_recv()
                    index += 1
    for cp in far:
        cp.wait_send()

    @pl.when(same)
    def _():
        w_loc.wait()
        near_remote.wait_send()
        remote(
            low_ref, w_ref.at[pl.ds(pl.multiple_of((1 - r) * half, half), half)], wr_send, wr_recv, row_dev
        ).wait_recv()

    @pl.when(jnp.logical_not(same))
    def _():
        w_row.wait_send()
        near_local.wait()
        for dd in range(n_dp):
            for rr in range(2):
                src_d = lax.rem(d + n_dp - dd, n_dp)
                src_r = r if rr == 0 else 1 - r
                if dd == 0 and rr == 0:
                    continue
                at = pl.ds(pl.multiple_of(src_r * half + src_d * rows, rows), rows)
                remote(ex_ref, w_ref.at[at], wd_send.at[dd], wd_recv.at[dd, src_r], row_dev).wait_recv()


def first_gather(tokens, low, post):
    n_dp = lax.axis_size("dp")
    tp = lax.axis_size("zl")
    rows_dev, feat = tokens.shape
    seq_len = rows_dev // 2
    width = feat * 4 * tp
    chunks = 4 if tp == 2 else 1
    anywhere = pl.BlockSpec(memory_space=pl.ANY)
    dma = pltpu.SemaphoreType.DMA
    x_shape = (4 * tp, seq_len, feat)
    x_full, w_full, post_all, _ = pl.pallas_call(
        functools.partial(gather_kernel, chunks),
        in_specs=[anywhere] * 3,
        out_specs=[anywhere] * 4,
        out_shape=[
            jax.ShapeDtypeStruct(x_shape, bf16),
            jax.ShapeDtypeStruct((2 * low.shape[0], low.shape[1]), bf16),
            jax.ShapeDtypeStruct((4 * tp, *post.shape), f32),
            jax.ShapeDtypeStruct((low.shape[0] // n_dp, low.shape[1]), bf16),
        ],
        scratch_shapes=[
            dma((chunks,)),
            dma((chunks,)),
            dma((chunks,)),
            dma((tp, 2, chunks)),
            dma((tp, 2, chunks)),
            dma((tp, 2, chunks)),
            dma((tp, 2, chunks)),
            dma(()),
            dma(()),
            dma((n_dp,)),
            dma((n_dp, 2)),
            dma(()),
            dma(()),
            dma((3,)),
            dma((4 * tp,)),
            dma((4 * tp,)),
        ],
        compiler_params=pltpu.CompilerParams(collective_id=0, has_side_effects=True),
        cost_estimate=pl.CostEstimate(flops=0, bytes_accessed=6 * seq_len * width, transcendentals=0),
        name="first_gather",
    )(tokens, low, post)
    x_full = x_full.transpose(1, 0, 2).reshape(seq_len, width)
    return x_full, w_full, post_all


def doc_start(ends_ref, docs, places):
    start = jnp.zeros_like(places)
    for i in range(docs):
        end = ends_ref[i]
        start = jnp.where(places >= end, end, start)
    return start


def attend_kernel(docs, bk, ends_ref, q_ref, k_ref, vt_ref, o_ref, lse_ref):
    bq = q_ref.shape[0]
    q0 = pl.program_id(1) * bq
    places = q0 + lax.broadcasted_iota(jnp.int32, (1, bq), 1)
    start = doc_start(ends_ref, docs, places)
    lowest = jnp.int32(0)
    for i in range(docs):
        lowest = jnp.where(ends_ref[i] <= q0, ends_ref[i], lowest)
    query = q_ref[...]
    scale = log2_e * HD ** (-0.5)

    def step(j, carry):
        top, total, acc = carry
        k0 = pl.multiple_of(j * bk, bk)
        key = k_ref[pl.ds(k0, bk), :]
        scores = lax.dot_general(key, query, NT, preferred_element_type=f32) * scale
        rows = k0 + lax.broadcasted_iota(jnp.int32, (bk, 1), 0)
        scores = jnp.where((rows <= places) & (rows >= start), scores, big_negative)
        top_new = jnp.maximum(top, jnp.max(scores, axis=0, keepdims=True))
        prob = jnp.exp2(scores - top_new)
        fade = jnp.exp2(top - top_new)
        total = total * fade + jnp.sum(prob, axis=0, keepdims=True)
        acc = acc * fade + lax.dot_general(
            vt_ref[:, pl.ds(k0, bk)], prob.astype(bf16), NN, preferred_element_type=f32
        )
        return top_new, total, acc

    first = (
        jnp.full((1, bq), big_negative, f32),
        jnp.zeros((1, bq), f32),
        jnp.zeros((HD, bq), f32),
    )
    top, total, acc = lax.fori_loop(lowest // bk, (q0 + bq - 1) // bk + 1, step, first)
    o_ref[...] = (acc * (1.0 / total)).T.astype(bf16)
    lse_ref[0] = top + jnp.log2(total)


def attend(query, key, value_t, ends):
    seq_len, width = query.shape
    heads = width // HD
    block = min(512, seq_len)
    docs = ends.shape[0]
    return pl.pallas_call(
        functools.partial(attend_kernel, docs, block),
        grid_spec=pltpu.PrefetchScalarGridSpec(
            num_scalar_prefetch=1,
            grid=(heads, seq_len // block),
            in_specs=[
                pl.BlockSpec((block, HD), lambda h, i, e: (i, h)),
                pl.BlockSpec((seq_len, HD), lambda h, i, e: (0, h)),
                pl.BlockSpec((HD, seq_len), lambda h, i, e: (h, 0)),
            ],
            out_specs=[
                pl.BlockSpec((block, HD), lambda h, i, e: (i, h)),
                pl.BlockSpec((1, 1, block), lambda h, i, e: (h, 0, i)),
            ],
        ),
        out_shape=[
            jax.ShapeDtypeStruct((seq_len, width), bf16),
            jax.ShapeDtypeStruct((heads, 1, seq_len), f32),
        ],
        compiler_params=pltpu.CompilerParams(vmem_limit_bytes=48 << 20),
        cost_estimate=pl.CostEstimate(
            flops=2 * heads * seq_len * seq_len * HD,
            bytes_accessed=8 * seq_len * width,
            transcendentals=heads * seq_len * seq_len // 2,
        ),
        name="attend",
    )(ends, query, key, value_t)


def attend_back_kernel(
    docs, bq, ends_ref, q_ref, k_ref, kt_ref, v_ref, do_ref, o_ref, lse_ref,
    dqt_ref, dk_ref, dv_ref, dk_acc, dv_acc, delta_acc
):
    bk = k_ref.shape[0]
    seq_len = q_ref.shape[0]
    j = pl.program_id(1)
    k0 = j * bk
    scale = HD ** (-0.5)
    last = jnp.int32(seq_len)
    for i in reversed(range(docs)):
        last = jnp.where(ends_ref[i] > k0 + bk - 1, ends_ref[i], last)
    rows = k0 + lax.broadcasted_iota(jnp.int32, (bk, 1), 0)

    @pl.when(j == 0)
    def _():
        dqt_ref[...] = jnp.zeros_like(dqt_ref)
        ones = jnp.ones((8, HD), bf16)
        for i in range(seq_len // bq):
            part = slice(i * bq, (i + 1) * bq)
            prod = do_ref[part, :].astype(f32) * o_ref[part, :].astype(f32)
            high = prod.astype(bf16)
            low = (prod - high.astype(f32)).astype(bf16)
            delta_acc[:, part] = lax.dot_general(
                ones, high, NT, preferred_element_type=f32
            ) + lax.dot_general(ones, low, NT, preferred_element_type=f32)

    dk_acc[...] = jnp.zeros_like(dk_acc)
    dv_acc[...] = jnp.zeros_like(dv_acc)
    key = k_ref[...]
    value = v_ref[...]
    key_t = kt_ref[...]

    def step(i, carry):
        q0 = pl.multiple_of(i * bq, bq)
        cols = pl.ds(q0, bq)
        query = q_ref[cols, :]
        grad = do_ref[cols, :]
        places = q0 + lax.broadcasted_iota(jnp.int32, (1, bq), 1)
        start = doc_start(ends_ref, docs, places)
        scores = lax.dot_general(key, query, NT, preferred_element_type=f32) * (scale * log2_e)
        allowed = (rows <= places) & (rows >= start)
        prob = jnp.where(allowed, jnp.exp2(scores - lse_ref[0, :, cols]), 0.0)
        dv_acc[...] += lax.dot_general(prob.astype(bf16), grad, NN, preferred_element_type=f32)
        grad_prob = lax.dot_general(value, grad, NT, preferred_element_type=f32)
        grad_score = (prob * (grad_prob - delta_acc[0:1, cols])).astype(bf16)
        dk_acc[...] += lax.dot_general(grad_score, query, NN, preferred_element_type=f32)
        dqt_ref[:, cols] += lax.dot_general(key_t, grad_score, NN, preferred_element_type=f32) * scale
        return carry

    lax.fori_loop(k0 // bq, (last + bq - 1) // bq, step, 0)
    dk_ref[...] = dk_acc[...] * scale
    dv_ref[...] = dv_acc[...].astype(bf16)


def attend_back(query, key, key_t, value, grad, att, log_total, ends):
    seq_len, width = query.shape
    heads = width // HD
    block = min(512, seq_len)
    docs = ends.shape[0]
    whole = pl.BlockSpec((seq_len, HD), lambda h, j, e: (0, h))
    part = pl.BlockSpec((block, HD), lambda h, j, e: (j, h))
    line = pl.BlockSpec((1, 1, seq_len), lambda h, j, e: (h, 0, 0))
    return pl.pallas_call(
        functools.partial(attend_back_kernel, docs, block),
        grid_spec=pltpu.PrefetchScalarGridSpec(
            num_scalar_prefetch=1,
            grid=(heads, seq_len // block),
            in_specs=[
                whole,
                part,
                pl.BlockSpec((HD, block), lambda h, j, e: (h, j)),
                part,
                whole,
                whole,
                line,
            ],
            out_specs=[
                pl.BlockSpec((HD, seq_len), lambda h, j, e: (h, 0)),
                part,
                part,
            ],
            scratch_shapes=[
                pltpu.VMEM((block, HD), f32),
                pltpu.VMEM((block, HD), f32),
                pltpu.VMEM((8, seq_len), f32),
            ],
        ),
        out_shape=[
            jax.ShapeDtypeStruct((width, seq_len), f32),
            jax.ShapeDtypeStruct((seq_len, width), f32),
            jax.ShapeDtypeStruct((seq_len, width), bf16),
        ],
        compiler_params=pltpu.CompilerParams(vmem_limit_bytes=48 << 20),
        cost_estimate=pl.CostEstimate(
            flops=5 * heads * seq_len * seq_len * HD,
            bytes_accessed=20 * seq_len * width,
            transcendentals=heads * seq_len * seq_len // 2,
        ),
        name="attend_back",
    )(ends, query, key, key_t, value, grad, att, log_total)


def turn(values, cos_two, sin_two):
    return values * cos_two + pltpu.roll(values, HD // 2, 1) * sin_two


def prepare_kernel(qkv_ref, scale_ref, gains_ref, cos_ref, sin_ref, q_ref, k_ref, kt_ref, v_ref, vt_ref):
    width = q_ref.shape[1]
    cos_two = cos_ref[...]
    sin_two = sin_ref[...]
    for which, out_ref in ((0, q_ref), (1, k_ref)):
        scale = scale_ref[:, which : which + 1]
        for head in range(width // HD):
            cols = slice(head * HD, (head + 1) * HD)
            vals = qkv_ref[:, which * width + head * HD : which * width + (head + 1) * HD]
            out = turn(vals * scale * gains_ref[which : which + 1, cols], cos_two, sin_two)
            out_ref[:, cols] = out.astype(bf16)
            if which == 1:
                kt_ref[cols, :] = out.T.astype(bf16)
    value = qkv_ref[:, 2 * width :]
    v_ref[...] = value.astype(bf16)
    vt_ref[...] = value.T.astype(bf16)


def prepare(qkv, inv_scale, gains, cos_two, sin_two):
    seq_len, triple = qkv.shape
    width = triple // 3
    block = min(256, seq_len)
    flat = pl.BlockSpec((block, width), lambda i: (i, 0))
    tall = pl.BlockSpec((width, block), lambda i: (0, i))
    table = pl.BlockSpec((block, HD), lambda i: (i, 0))
    return pl.pallas_call(
        prepare_kernel,
        grid=(seq_len // block,),
        in_specs=[
            pl.BlockSpec((block, triple), lambda i: (i, 0)),
            pl.BlockSpec((block, 2), lambda i: (i, 0)),
            pl.BlockSpec((2, width), lambda i: (0, 0)),
            table,
            table,
        ],
        out_specs=[flat, flat, tall, flat, tall],
        out_shape=[
            jax.ShapeDtypeStruct((seq_len, width), bf16),
            jax.ShapeDtypeStruct((seq_len, width), bf16),
            jax.ShapeDtypeStruct((width, seq_len), bf16),
            jax.ShapeDtypeStruct((seq_len, width), bf16),
            jax.ShapeDtypeStruct((width, seq_len), bf16),
        ],
        compiler_params=pltpu.CompilerParams(vmem_limit_bytes=48 << 20),
        cost_estimate=pl.CostEstimate(flops=10 * seq_len * triple, bytes_accessed=8 * seq_len * triple, transcendentals=0),
        name="prepare",
    )(qkv, inv_scale, gains, cos_two, sin_two)


def unturn_kernel(dqt_ref, dk_ref, qkv_ref, scale_ref, gains_ref, cos_ref, sin_ref, hat_ref, inner_ref, gain_ref):
    width = dk_ref.shape[1]
    cos_two = cos_ref[...]
    sin_two = sin_ref[...]

    @pl.when(pl.program_id(0) == 0)
    def _():
        gain_ref[...] = jnp.zeros_like(gain_ref)

    for which in range(2):
        scale = scale_ref[:, which : which + 1]
        inner = jnp.zeros((dk_ref.shape[0], HD), f32)
        for head in range(width // HD):
            cols = slice(head * HD, (head + 1) * HD)
            off = which * width + head * HD
            grad = dqt_ref[cols, :].T if which == 0 else dk_ref[:, cols]
            hat = turn(grad, cos_two, -sin_two)
            pre = qkv_ref[:, off : off + HD]
            prod = hat * pre
            gain_ref[which : which + 1, cols] += jnp.sum(prod * scale, axis=0, keepdims=True)
            inner = inner + prod * gains_ref[which : which + 1, cols]
            hat_ref[:, off : off + HD] = hat * gains_ref[which : which + 1, cols]
        inner_ref[:, which : which + 1] = jnp.sum(inner, axis=1, keepdims=True)


def unturn(dqt, dk, qkv, inv_scale, gains, cos_two, sin_two):
    seq_len, width = dk.shape
    block = min(256, seq_len)
    table = pl.BlockSpec((block, HD), lambda i: (i, 0))
    pair = pl.BlockSpec((block, 2), lambda i: (i, 0))
    return pl.pallas_call(
        unturn_kernel,
        grid=(seq_len // block,),
        in_specs=[
            pl.BlockSpec((width, block), lambda i: (0, i)),
            pl.BlockSpec((block, width), lambda i: (i, 0)),
            pl.BlockSpec((block, 2 * width), lambda i: (i, 0)),
            pair,
            pl.BlockSpec((2, width), lambda i: (0, 0)),
            table,
            table,
        ],
        out_specs=[
            pl.BlockSpec((block, 2 * width), lambda i: (i, 0)),
            pair,
            pl.BlockSpec((2, width), lambda i: (0, 0)),
        ],
        out_shape=[
            jax.ShapeDtypeStruct((seq_len, 2 * width), f32),
            jax.ShapeDtypeStruct((seq_len, 2), f32),
            jax.ShapeDtypeStruct((2, width), f32),
        ],
        compiler_params=pltpu.CompilerParams(vmem_limit_bytes=48 << 20),
        cost_estimate=pl.CostEstimate(flops=20 * seq_len * width, bytes_accessed=24 * seq_len * width, transcendentals=0),
        name="unturn",
    )(dqt, dk, qkv, inv_scale, gains, cos_two, sin_two)


class Job:
    def __init__(self, gather, scatter, merge, weights, pieces, dim, spread, tile_ins, outs, slots, sums, body):
        self.gather, self.scatter, self.merge, self.spread = gather, scatter, merge, spread
        self.weights, self.pieces, self.dim = weights, pieces, dim
        self.tile_ins, self.outs = tile_ins, outs
        self.slots, self.sums, self.body = slots, sums, body


def tile_kernel(job, tp, chunks, *refs):
    refs = list(refs)

    def take(count):
        got = refs[:count]
        del refs[:count]
        return got

    (src_ref,) = take(1)
    w_hbm = [take(max(1, job.pieces)) for _ in range(job.weights)]
    ti_hbm = take(job.tile_ins)
    quarter_ref = take(1)[0] if job.spread else None
    full_ref = take(1)[0] if job.gather else src_ref
    out_hbm = take(job.outs)
    w_out = take(job.weights) if job.pieces else None
    spread_ref = take(1)[0] if job.spread else None
    total_ref = take(1)[0] if job.scatter else None
    w_ref = take(job.weights)
    (tile_ref,) = take(1)
    ti_ref = take(job.tile_ins)
    out_ref = take(job.outs)
    y_ref, rbuf, zbuf, tbuf = take(4) if job.scatter else (None,) * 4
    w_sem, tile_sem, ti_sem, out_sem, loc_sem = take(5)
    t_send, t_recv, r_send, r_recv = take(4)
    y_send, y_recv, z_send, z_recv = take(4)
    wl_sem, wr_send, wr_recv, q_send, q_recv = take(5)

    n_dp = lax.axis_size("dp")
    d, r, g, t = (lax.axis_index(name) for name in ("dp", "row", "zh", "zl"))
    rows = tile_ref.shape[1]
    if job.merge:
        mc = rows // (2 * chunks)
        order = [(s, 0) for s in range(tp)]
    else:
        mc = rows // 2
        order = [(s, c) for c in range(chunks) for s in range(tp)]
    if not job.gather:
        order = [(s, c) for s in list(range(1, tp)) + [0] for c in range(chunks)]
    row_dev = (d, 1 - r, g, t)

    def peer(step):
        return (d, r, g, lax.rem(t + step + tp, tp))

    def remote(src, dst, send, recv, dev):
        return pltpu.make_async_remote_copy(
            src_ref=src, dst_ref=dst, send_sem=send, recv_sem=recv, device_id=dev,
            device_id_type=pl.DeviceIdType.MESH,
        )

    def piece(s, c, rho):
        return full_ref.at[pl.ds(((s * chunks + c) * 2 + rho) * mc, mc)]

    barrier = pltpu.get_barrier_semaphore()
    pl.semaphore_signal(barrier, inc=1, device_id=row_dev, device_id_type=pl.DeviceIdType.MESH)
    for s in range(1, tp):
        pl.semaphore_signal(barrier, inc=1, device_id=peer(s), device_id_type=pl.DeviceIdType.MESH)

    count = tp
    if job.spread:
        for k in range(1, n_dp):
            dev = (lax.rem(d + k, n_dp), r, g, t)
            pl.semaphore_signal(barrier, inc=1, device_id=dev, device_id_type=pl.DeviceIdType.MESH)
            count += 1
    same = r == g
    other_core = jnp.logical_not(same)

    def half_view(i, half, row_at, row_count, col_at, col_count):
        ref = w_ref[i]
        if job.dim == 0:
            size = ref.shape[0] // 2
            start = pl.multiple_of(half * size + row_at, row_count)
            return ref.at[pl.ds(start, row_count), pl.ds(col_at, col_count)]
        size = ref.shape[1] // 2
        return ref.at[pl.ds(row_at, row_count), pl.ds(pl.multiple_of(half * size + col_at, col_count), col_count)]

    def piece_list(i):
        if len(w_hbm[i]) == 2:
            other = w_hbm[i][1]
            return [(other, 0, other.shape[0], 0, other.shape[1])]
        one, two, one_x, one_y, two_y, two_x = w_hbm[i][1:]
        rows_q, cut = one.shape
        low_bit, high_bit = lax.rem(d, 2), d // 2
        places = [
            ((high_bit * (1 - 2 * (k // 2)) + k // 2) * 2 + low_bit * (1 - 2 * (k % 2)) + k % 2) * rows_q
            for k in range(4)
        ]
        upper, lower = pl.ds(0, rows_q), pl.ds(rows_q, rows_q)
        return [
            (one, places[0], rows_q, 0, cut),
            (one_x, places[1], rows_q, 0, cut),
            (one_y.at[upper], places[2], rows_q, 0, cut),
            (one_y.at[lower], places[3], rows_q, 0, cut),
            (two, places[0], rows_q, cut, cut),
            (two_x.at[upper], places[1], rows_q, cut, cut),
            (two_y, places[2], rows_q, cut, cut),
            (two_x.at[lower], places[3], rows_q, cut, cut),
        ]

    def piece_recv_places(i):
        return [half_view(i, 1 - r, *spot[1:]) for spot in piece_list(i)]

    def low_copies(i):
        low = w_hbm[i][0]
        there = half_view(i, r, 0, low.shape[0], 0, low.shape[1])
        here = half_view(i, 1 - r, 0, low.shape[0], 0, low.shape[1])
        keep = pltpu.make_async_copy(low, there, wl_sem.at[i, 0])
        give = pltpu.make_async_remote_copy(
            src_ref=low, dst_ref=there, send_sem=wr_send.at[i, 0], recv_sem=wr_recv.at[i, 0],
            device_id=row_dev, device_id_type=pl.DeviceIdType.MESH,
        )
        got = pltpu.make_async_remote_copy(
            src_ref=low, dst_ref=here, send_sem=wr_send.at[i, 0], recv_sem=wr_recv.at[i, 0],
            device_id=row_dev, device_id_type=pl.DeviceIdType.MESH,
        )
        return keep, give, got

    def part_copies(i):
        keeps, gives, gots = [], [], []
        for p, spot in enumerate(piece_list(i)):
            there = half_view(i, r, *spot[1:])
            here = piece_recv_places(i)[p]
            keeps.append(pltpu.make_async_copy(spot[0], there, wl_sem.at[i, p]))
            for dst, into in ((there, gives), (here, gots)):
                into.append(
                    pltpu.make_async_remote_copy(
                        src_ref=spot[0], dst_ref=dst, send_sem=wr_send.at[i, p], recv_sem=wr_recv.at[i, p],
                        device_id=row_dev, device_id_type=pl.DeviceIdType.MESH,
                    )
                )
        return keeps, gives, gots

    def w_start(i):
        if not job.pieces:
            pltpu.make_async_copy(w_hbm[i][0], w_ref[i], w_sem.at[i]).start()
            return

        @pl.when(same)
        def _():
            low_copies(i)[0].start()
            for cp in part_copies(i)[1]:
                cp.start()

        @pl.when(other_core)
        def _():
            low_copies(i)[1].start()
            for cp in part_copies(i)[0]:
                cp.start()

    def w_wait(i):
        if not job.pieces:
            pltpu.make_async_copy(w_hbm[i][0], w_ref[i], w_sem.at[i]).wait()
            return

        @pl.when(same)
        def _():
            low_copies(i)[0].wait()
            low_copies(i)[2].wait_recv()

        @pl.when(other_core)
        def _():
            for cp in part_copies(i)[0]:
                cp.wait()
            for cp in part_copies(i)[2]:
                cp.wait_recv()

        pltpu.make_async_copy(w_ref[i], w_out[i], w_sem.at[i]).start()

    def w_end(i):

        @pl.when(same)
        def _():
            for cp in part_copies(i)[1]:
                cp.wait_send()

        @pl.when(other_core)
        def _():
            low_copies(i)[1].wait_send()

        pltpu.make_async_copy(w_ref[i], w_out[i], w_sem.at[i]).wait()

    if not job.pieces:
        for i in range(job.weights):
            w_start(i)
    pl.semaphore_wait(barrier, count)
    seen = set()

    def need(i):
        if i not in seen:
            seen.add(i)
            w_wait(i)

    sends = []

    def go(cp):
        cp.start()
        sends.append(cp)

    local = {}
    if job.gather:
        for c in range(chunks):
            own = src_ref.at[pl.ds(c * mc, mc)]
            for s in range(1, tp):
                go(remote(own, piece(s, c, 0), t_send.at[s, c], t_recv.at[s, c], peer(-s)))
            local[c] = pltpu.make_async_copy(own, piece(0, c, 0), loc_sem.at[c])
            local[c].start()
            go(remote(own, piece(0, c, 1), r_send.at[0, c], r_recv.at[0, c], row_dev))

    if job.pieces:
        for i in range(job.weights):
            w_start(i)
    if job.spread:
        rows_q = quarter_ref.shape[0]
        mine = spread_ref.at[pl.ds(pl.multiple_of(d * rows_q, rows_q), rows_q)]
        q_local = pltpu.make_async_copy(quarter_ref, mine, q_send.at[0])
        q_local.start()
        for k in range(1, n_dp):
            go(remote(quarter_ref, mine, q_send.at[k], q_recv.at[k], (lax.rem(d + k, n_dp), r, g, t)))

    relayed = set()

    def relay(s, c):
        if job.gather and s > 0 and (s, c) not in relayed:
            relayed.add((s, c))
            remote(piece(s, c, 0), piece(s, c, 0), t_send.at[s, c], t_recv.at[s, c], peer(-s)).wait_recv()
            go(remote(piece(s, c, 0), piece(s, c, 1), r_send.at[s, c], r_recv.at[s, c], row_dev))

    def tile_load(i):
        s, c = order[i]
        at = pl.ds((s if job.merge else s * chunks + c) * rows, rows)
        return pltpu.make_async_copy(full_ref.at[at], tile_ref.at[i % 2], tile_sem.at[i % 2])

    def ti_loads(i):
        s, c = order[i]
        at = pl.ds((s if job.merge else s * chunks + c) * rows, rows)
        return [pltpu.make_async_copy(ti_hbm[j].at[at], ti_ref[j], ti_sem.at[j]) for j in range(job.tile_ins)]

    def out_copies(i):
        s, c = order[i]
        at = pl.ds((s if job.merge else s * chunks + c) * rows, rows)
        slot = i % job.slots
        return [
            pltpu.make_async_copy(out_ref[j].at[slot], out_hbm[j].at[at], out_sem.at[j, slot])
            for j in range(job.outs)
        ]

    def combine(i):
        s, c = order[i]
        k = s * chunks + c
        cp = remote(
            y_ref.at[i % job.sums, pl.ds(mc, mc)], rbuf.at[k], y_send.at[s, c], y_recv.at[s, c], row_dev
        )
        cp.wait()
        step = min(64, mc)

        def add(b, carry):
            at = pl.ds(pl.multiple_of(b * step, step), step)
            summed = y_ref[i % job.sums, at, :].astype(f32) + rbuf[k, at, :].astype(f32)
            if s == 0:
                total_ref[pl.ds(pl.multiple_of(c * mc + b * step, step), step), :] = summed
            else:
                zbuf[k - chunks, at, :] = summed.astype(bf16)
            return carry

        lax.fori_loop(0, mc // step, add, 0)
        if s > 0:
            go(remote(zbuf.at[k - chunks], tbuf.at[k - chunks], z_send.at[s, c], z_recv.at[s, c], peer(s)))

    for cp in ti_loads(0):
        cp.start()
    if not job.gather:
        tile_load(0).start()
    for i, (s, c) in enumerate(order):
        if job.gather:
            held = range(chunks) if job.merge else [c]
            for cc in held:
                relay(s, cc)
                if s == 0:
                    local[cc].wait()
            for cc in held:
                remote(piece(s, cc, 1), piece(s, cc, 1), r_send.at[s, cc], r_recv.at[s, cc], row_dev).wait_recv()
            tile_load(i).start()
        tile_load(i).wait()
        if not job.gather and i + 1 < len(order):
            tile_load(i + 1).start()
        for cp in ti_loads(i):
            cp.wait()
        if i >= job.slots:
            for cp in out_copies(i - job.slots):
                cp.wait()

        def mid(i=i):
            if i + 1 < len(order):
                relay(*order[i + 1])
                for cp in ti_loads(i + 1):
                    cp.start()
            if job.scatter:
                for cp in out_copies(i):
                    cp.start()
                if i >= 1:
                    combine(i - 1)

        outs = [ref.at[i % job.slots] for ref in out_ref]
        y = y_ref.at[i % job.sums] if job.scatter else None
        job.body(tile_ref.at[i % 2], w_ref, need, ti_ref, outs, y, mid)
        if job.scatter:
            k = s * chunks + c
            remote(y.at[pl.ds(mc, mc)], rbuf.at[k], y_send.at[s, c], y_recv.at[s, c], row_dev).start()
        else:
            for cp in out_copies(i):
                cp.start()
    last = len(order)
    for i in range(max(0, last - job.slots), last):
        for cp in out_copies(i):
            cp.wait()
    if job.scatter:
        combine(last - 1)
        for c in range(chunks):
            for s in range(1, tp):
                k = (s - 1) * chunks + c
                remote(zbuf.at[k], tbuf.at[k], z_send.at[s, c], z_recv.at[s, c], peer(s)).wait_recv()
                step = min(64, mc)

                def add(b, carry, k=k, c=c):
                    at = pl.ds(pl.multiple_of(b * step, step), step)
                    to = pl.ds(pl.multiple_of(c * mc + b * step, step), step)
                    total_ref[to, :] = total_ref[to, :] + tbuf[k, at, :].astype(f32)
                    return carry

                lax.fori_loop(0, mc // step, add, 0)
    if job.pieces:
        for i in range(job.weights):
            w_end(i)
    if job.spread:
        q_local.wait()
        for k in range(1, n_dp):
            came = lax.rem(d + n_dp - k, n_dp)
            remote(
                quarter_ref, spread_ref.at[pl.ds(pl.multiple_of(came * rows_q, rows_q), rows_q)],
                q_send.at[k], q_recv.at[k], row_dev,
            ).wait_recv()
    for cp in sends:
        cp.wait_send()


def tile_call(job, ident, name, src, weights, shapes, tile_ins, out_widths, sum_width, flops, quarter=None):
    tp = lax.axis_size("zl")
    n_dp = lax.axis_size("dp")
    flat_weights = [v for group in weights for v in group]
    width = src.shape[1]
    m = src.shape[0] if job.gather else src.shape[0] // (2 * tp)
    chunks = 2 if tp == 2 else 1
    mc = m // chunks
    rows = 2 * (m if job.merge else mc)
    total_rows = 2 * tp * m
    anywhere = pl.BlockSpec(memory_space=pl.ANY)
    dma = pltpu.SemaphoreType.DMA
    out_specs, out_shape = [], []
    if job.gather:
        out_specs.append(anywhere)
        out_shape.append(jax.ShapeDtypeStruct((total_rows, width), bf16))
    for w in out_widths:
        out_specs.append(anywhere)
        out_shape.append(jax.ShapeDtypeStruct((total_rows, w), bf16))
    if job.pieces:
        out_specs.extend([anywhere] * len(shapes))
        out_shape.extend(jax.ShapeDtypeStruct(shape, bf16) for shape in shapes)
    if job.spread:
        out_specs.append(anywhere)
        out_shape.append(jax.ShapeDtypeStruct((n_dp * quarter.shape[0], quarter.shape[1]), bf16))
    if job.scatter:
        out_specs.append(pl.BlockSpec(memory_space=pltpu.VMEM))
        out_shape.append(jax.ShapeDtypeStruct((m, sum_width), f32))
    scratch = [pltpu.VMEM(shape, bf16) for shape in shapes]
    scratch.append(pltpu.VMEM((2, rows, width), bf16))
    scratch.extend(pltpu.VMEM((rows, v.shape[1]), bf16) for v in tile_ins)
    scratch.extend(pltpu.VMEM((job.slots, rows, w), bf16) for w in out_widths)
    if job.scatter:
        scratch.append(pltpu.VMEM((job.sums, rows, sum_width), bf16))
        scratch.append(pltpu.VMEM((tp * chunks, mc, sum_width), bf16))
        scratch.append(pltpu.VMEM(((tp - 1) * chunks, mc, sum_width), bf16))
        scratch.append(pltpu.VMEM(((tp - 1) * chunks, mc, sum_width), bf16))
    scratch.extend(
        [dma((len(weights),)), dma((2,)), dma((max(1, len(tile_ins)),)), dma((max(1, job.outs), job.slots)), dma((chunks,))]
    )
    scratch.extend(dma((tp, chunks)) for _ in range(8))
    scratch.extend(dma((len(weights), 8)) for _ in range(3))
    scratch.extend(dma((n_dp,)) for _ in range(2))
    extra = [quarter] if job.spread else []
    return pl.pallas_call(
        functools.partial(tile_kernel, job, tp, chunks),
        in_specs=[anywhere] * (1 + len(flat_weights) + len(tile_ins) + len(extra)),
        out_specs=out_specs,
        out_shape=out_shape,
        scratch_shapes=scratch,
        compiler_params=pltpu.CompilerParams(
            collective_id=ident, has_side_effects=True, vmem_limit_bytes=60 << 20
        ),
        cost_estimate=pl.CostEstimate(flops=flops, bytes_accessed=8 * total_rows * width, transcendentals=0),
        name=name,
    )(src, *flat_weights, *tile_ins, *extra)


def columns(n, size):
    return pl.ds(pl.multiple_of(n * size, size), size)


def loop(first, last, step):
    def body(n, carry):
        step(n)
        return carry

    lax.fori_loop(first, last, body, 0)


def gate_up_body(tile, w, need, ti, outs, y, mid):
    hidden_width = w[0].shape[1]
    nb = min(256, hidden_width)
    mb = min(128, tile.shape[0])
    count = hidden_width // nb
    need(0)
    need(1)

    def step(n):
        cols = columns(n, nb)
        for m in range(tile.shape[0] // mb):
            at = slice(m * mb, (m + 1) * mb)
            gate = jnp.dot(tile[at, :], w[0][:, cols], preferred_element_type=f32)
            up = jnp.dot(tile[at, :], w[1][:, cols], preferred_element_type=f32)
            outs[0][at, cols] = gate.astype(bf16)
            outs[1][at, cols] = up.astype(bf16)
            outs[2][at, cols] = (gate * jax.nn.sigmoid(gate) * up).astype(bf16)

    loop(0, count // 2, step)
    mid()
    loop(count // 2, count, step)


def down_body(tile, w, need, ti, outs, y, mid):
    nb = min(1024, w[0].shape[1])
    count = w[0].shape[1] // nb
    need(0)

    def step(n):
        cols = columns(n, nb)
        y[:, cols] = jnp.dot(tile[...], w[0][:, cols], preferred_element_type=f32).astype(bf16)

    loop(0, count // 2, step)
    mid()
    loop(count // 2, count, step)


def back_body(tile, w, need, ti, outs, y, mid):
    hidden_width = w[0].shape[0]
    nb = min(512, hidden_width)
    need(0)

    def first(n):
        cols = columns(n, nb)
        grad = lax.dot_general(tile[...], w[0][cols, :], NT, preferred_element_type=f32)
        grad = grad.astype(bf16).astype(f32)
        gate = ti[0][:, cols].astype(f32)
        up = ti[1][:, cols].astype(f32)
        sig = jax.nn.sigmoid(gate)
        passed = grad * sig
        outs[0][:, cols] = (passed * up * (1.0 + gate * (1.0 - sig))).astype(bf16)
        outs[1][:, cols] = (passed * gate).astype(bf16)

    loop(0, hidden_width // nb, first)
    mid()
    need(1)
    need(2)
    nd = 512

    def second(n):
        cols = columns(n, nd)
        grad = lax.dot_general(outs[0][...], w[1][cols, :], NT, preferred_element_type=f32)
        grad = grad + lax.dot_general(outs[1][...], w[2][cols, :], NT, preferred_element_type=f32)
        y[:, cols] = grad.astype(bf16)

    loop(0, w[1].shape[0] // nd, second)


gate_up_job = Job(True, False, False, 2, 7, 0, True, 0, 3, 2, 0, gate_up_body)
down_job = Job(False, True, False, 1, 2, 1, False, 0, 0, 1, 2, down_body)
back_job = Job(True, True, False, 3, 0, 0, False, 2, 2, 1, 1, back_body)


def last_kernel(
    chunks, dx_ref, grad_ref, far_one, far_two, out_ref, sum_ref, far_out_one, far_out_two,
    own, from_row, near, from_t, give, from_zh,
    g_own, g_in, g_sum, g_late, stay_one, stay_two, late_one, late_two, far_local, far_send, far_recv,
    own_sem, row_send, row_recv, t_send, t_recv, zh_send, zh_recv, g_sem, d_send, d_recv, f_send, f_recv,
):
    n_dp = lax.axis_size("dp")
    tp = lax.axis_size("zl")
    d, r, g, t = (lax.axis_index(name) for name in ("dp", "row", "zh", "zl"))
    same = r == g
    other_core = jnp.logical_not(same)
    seq_len, width = dx_ref.shape
    half = width // 2
    feat = half // (2 * tp)
    step = seq_len // chunks
    part = g_own.shape[1]

    def remote(src, dst, send, recv, dev):
        return pltpu.make_async_remote_copy(
            src_ref=src, dst_ref=dst, send_sem=send, recv_sem=recv, device_id=dev,
            device_id_type=pl.DeviceIdType.MESH,
        )

    row_dev = (d, 1 - r, g, t)
    zh_dev = (d, r, 1 - g, t)
    cross_dev = (d, 1 - r, 1 - g, t)

    def dp_dev(k):
        return (lax.rem(d + k, n_dp), r, g, t)

    def t_dev(s):
        return (d, r, g, lax.rem(t + s, tp))

    partners = [row_dev, zh_dev, cross_dev]
    partners += [dp_dev(k) for k in range(1, n_dp)] + [t_dev(s) for s in range(1, tp)]
    barrier = pltpu.get_barrier_semaphore()
    for dev in partners:
        pl.semaphore_signal(barrier, inc=1, device_id=dev, device_id_type=pl.DeviceIdType.MESH)
    pl.semaphore_wait(barrier, len(partners))

    fars = [(far_one, far_out_one, stay_one, late_one), (far_two, far_out_two, stay_two, late_two)]

    def far_copies(i):
        pieces, _, stay, late = fars[i]
        return (
            pltpu.make_async_copy(pieces.at[r], stay, far_local.at[i]),
            remote(pieces.at[1 - r], late.at[0], far_send.at[i, 0], far_recv.at[i, 0], row_dev),
            remote(pieces.at[r], late.at[0], far_send.at[i, 1], far_recv.at[i, 1], zh_dev),
            remote(pieces.at[1 - r], late.at[1], far_send.at[i, 2], far_recv.at[i, 2], cross_dev),
        )

    def far_start(i):
        @pl.when(same)
        def _():
            far_copies(i)[0].start()
            far_copies(i)[1].start()

        @pl.when(other_core)
        def _():
            far_copies(i)[2].start()
            far_copies(i)[3].start()

    def far_end(i):
        pieces, total, stay, late = fars[i]

        @pl.when(same)
        def _():
            far_copies(i)[0].wait()
            far_copies(i)[2].wait_recv()
            total[...] = stay[...].astype(f32) + late[0].astype(f32)
            far_copies(i)[1].wait_send()

        @pl.when(other_core)
        def _():
            far_copies(i)[1].wait_recv()
            far_copies(i)[3].wait_recv()
            total[...] = late[0].astype(f32) + late[1].astype(f32)
            far_copies(i)[2].wait_send()
            far_copies(i)[3].wait_send()

    far_start(0)

    def cols_at(which):
        return pl.ds(pl.multiple_of(which * half, half), half)

    rows_copies, own_copies = [], []
    for c in range(chunks):
        rows = pl.ds(c * step, step)
        cp = remote(dx_ref.at[rows, cols_at(1 - r)], from_row.at[c], row_send.at[c], row_recv.at[c], row_dev)
        cp.start()
        rows_copies.append(cp)
        cp = pltpu.make_async_copy(dx_ref.at[rows, cols_at(r)], own.at[c], own_sem.at[c])
        cp.start()
        own_copies.append(cp)

    def grad_rows(which, group):
        return grad_ref.at[pl.ds(pl.multiple_of((which * n_dp + group) * part, part), part)]

    g_copies, g_loads = [], []
    for which in range(2):
        cp = pltpu.make_async_copy(grad_rows(which, d), g_own.at[which], g_sem.at[which])
        cp.start()
        g_loads.append(cp)
        for k in range(1, n_dp):
            cp = remote(
                grad_rows(which, lax.rem(d + k, n_dp)), g_in.at[k - 1, which],
                d_send.at[k, which], d_recv.at[k, which], dp_dev(k),
            )
            cp.start()
            g_copies.append(cp)

    t_copies = {}

    def row_stage(c):
        own_copies[c].wait()
        rows_copies[c].wait_recv()
        total = own[c].astype(f32) + from_row[c].astype(f32)
        for b in range(2 * tp):
            near[c, b] = total[:, b * feat : (b + 1) * feat].astype(bf16)
        for zh in range(2):
            for s in range(1, tp):
                cp = remote(
                    near.at[c, zh * tp + lax.rem(t + s, tp)], from_t.at[c, zh, s - 1],
                    t_send.at[c, zh, s], t_recv.at[c, zh, s], t_dev(s),
                )
                cp.start()
                t_copies[(c, zh, s)] = cp

    zh_copies = []

    def t_stage(c):
        for zh in range(2):
            for s in range(1, tp):
                t_copies[(c, zh, s)].wait_recv()

        def total_of(zh):
            total = near[c, zh * tp + t].astype(f32)
            for s in range(1, tp):
                total = total + from_t[c, zh, s - 1].astype(f32)
            return total

        give[c] = total_of(1 - g).astype(bf16)
        cp = remote(give.at[c], from_zh.at[c], zh_send.at[c], zh_recv.at[c], zh_dev)
        cp.start()
        zh_copies.append(cp)
        out_ref[pl.ds(pl.multiple_of(g * seq_len + c * step, step), step), :] = total_of(g)

    def grad_stage():
        for cp in g_loads:
            cp.wait()
        for cp in g_copies:
            cp.wait_recv()
        block = min(64, part)
        for which in range(2):

            def add(i, carry, which=which):
                at = pl.ds(pl.multiple_of(i * block, block), block)
                total = g_own[which, at, :].astype(f32)
                for k in range(n_dp - 1):
                    total = total + g_in[k, which, at, :].astype(f32)
                g_sum[which, at, :] = total.astype(bf16)
                return carry

            lax.fori_loop(0, part // block, add, 0)

    to_row = remote(g_sum.at[1 - r], g_late.at[0], f_send.at[0], f_recv.at[0], row_dev)
    to_zh = remote(g_sum.at[r], g_late.at[0], f_send.at[1], f_recv.at[1], zh_dev)
    to_cross = remote(g_sum.at[1 - r], g_late.at[1], f_send.at[2], f_recv.at[2], cross_dev)

    far_start(1)
    for c in range(chunks):
        row_stage(c)
        if c >= 2:
            t_stage(c - 2)
    grad_stage()

    @pl.when(same)
    def _():
        to_row.start()

    @pl.when(other_core)
    def _():
        to_zh.start()
        to_cross.start()

    for c in range(max(0, chunks - 2), chunks):
        t_stage(c)
    for c in range(chunks):
        zh_copies[c].wait_recv()
        out_ref[pl.ds(pl.multiple_of((1 - g) * seq_len + c * step, step), step), :] = from_zh[c].astype(f32)

    @pl.when(same)
    def _():
        to_zh.wait_recv()
        sum_ref[...] = g_sum[r].astype(f32) + g_late[0].astype(f32)
        to_row.wait_send()

    @pl.when(other_core)
    def _():
        to_row.wait_recv()
        to_cross.wait_recv()
        sum_ref[...] = g_late[0].astype(f32) + g_late[1].astype(f32)
        to_zh.wait_send()
        to_cross.wait_send()

    far_end(0)
    far_end(1)
    for cp in rows_copies + g_copies + list(t_copies.values()) + zh_copies:
        cp.wait_send()


def last_sums(dx, grad, fars):
    n_dp = lax.axis_size("dp")
    tp = lax.axis_size("zl")
    seq_len, width = dx.shape
    chunks = 4
    half = width // 2
    feat = half // (2 * tp)
    step = seq_len // chunks
    part = grad.shape[0] // (2 * n_dp)
    cols = grad.shape[1]
    anywhere = pl.BlockSpec(memory_space=pl.ANY)
    vmem = pl.BlockSpec(memory_space=pltpu.VMEM)
    dma = pltpu.SemaphoreType.DMA
    return pl.pallas_call(
        functools.partial(last_kernel, chunks),
        in_specs=[anywhere] * 4,
        out_specs=[vmem] * 4,
        out_shape=[
            jax.ShapeDtypeStruct((2 * seq_len, feat), f32),
            jax.ShapeDtypeStruct((part, cols), f32),
            *[jax.ShapeDtypeStruct(v.shape[1:], f32) for v in fars],
        ],
        scratch_shapes=[
            pltpu.VMEM((chunks, step, half), bf16),
            pltpu.VMEM((chunks, step, half), bf16),
            pltpu.VMEM((chunks, 2 * tp, step, feat), bf16),
            pltpu.VMEM((chunks, 2, tp - 1, step, feat), bf16),
            pltpu.VMEM((chunks, step, feat), bf16),
            pltpu.VMEM((chunks, step, feat), bf16),
            pltpu.VMEM((2, part, cols), bf16),
            pltpu.VMEM((n_dp - 1, 2, part, cols), bf16),
            pltpu.VMEM((2, part, cols), bf16),
            pltpu.VMEM((2, part, cols), bf16),
            *[pltpu.VMEM(v.shape[1:], bf16) for v in fars],
            *[pltpu.VMEM(v.shape, bf16) for v in fars],
            dma((2,)),
            dma((2, 3)),
            dma((2, 3)),
            dma((chunks,)),
            dma((chunks,)),
            dma((chunks,)),
            dma((chunks, 2, tp)),
            dma((chunks, 2, tp)),
            dma((chunks,)),
            dma((chunks,)),
            dma((2,)),
            dma((n_dp, 2)),
            dma((n_dp, 2)),
            dma((3,)),
            dma((3,)),
        ],
        compiler_params=pltpu.CompilerParams(collective_id=4, has_side_effects=True, vmem_limit_bytes=60 << 20),
        cost_estimate=pl.CostEstimate(flops=0, bytes_accessed=8 * seq_len * width, transcendentals=0),
        name="last_sums",
    )(dx, grad, *fars)


def rotary(seq_len):
    half_width = HD // 2
    freqs = rope_base ** (-(jnp.arange(half_width, dtype=f32) * 2.0) / HD)
    angles = jnp.arange(seq_len, dtype=f32)[:, None] * freqs[None, :]
    cos_table, sin_table = jnp.cos(angles), jnp.sin(angles)
    return (
        jnp.concatenate([cos_table, cos_table], axis=1),
        jnp.concatenate([-sin_table, sin_table], axis=1),
    )


def norm_scale(vals):
    return lax.rsqrt(jnp.mean(vals * vals, axis=1, keepdims=True) + norm_eps)


def norm_back(pre_vals, scale, gains, gradient):
    weighted = gradient * gains
    inner = jnp.mean(weighted * pre_vals, axis=1, keepdims=True)
    grad_pre = scale * weighted - pre_vals * (scale * scale * scale * inner)
    grad_gain = jnp.sum(gradient * pre_vals * scale, axis=0)
    return grad_pre, grad_gain


def adamw_step(weight, gradient, first_mom, second_mom, step_rate, decay_rate):
    first_new = beta_one * first_mom + (1.0 - beta_one) * gradient
    second_new = beta_two * second_mom + (1.0 - beta_two) * gradient * gradient
    fix_one = 1.0 - beta_one**STEP
    fix_two = 1.0 - beta_two**STEP
    direction = first_new / fix_one / (jnp.sqrt(second_new / fix_two) + adam_eps)
    return (first_new, second_new, weight - step_rate * (direction + decay_rate * weight))


def matmul(left, right, dims=NN):
    return lax.dot_general(left, right, dims, preferred_element_type=f32)


def shards(
    tokens, cotangent, doc_lengths, qkv_weight, out_weight, gate_weight, up_weight, down_weight,
    head_gains, post_gains, qkv_first, qkv_second, out_first, out_second, gate_first, gate_second,
    up_first, up_second, down_first, down_second, head_first, head_second, post_first, post_second,
):
    n_dp = lax.axis_size("dp")
    tp = lax.axis_size("zl")
    group = 2 * tp
    n_col = 2 * tp
    d, r, g, t = (lax.axis_index(name) for name in ("dp", "row", "zh", "zl"))
    same = r == g
    block_at = r * tp + t
    rows_dev, feat = tokens.shape
    width = feat * 2 * n_col
    seq_len = rows_dev // 2
    mine = seq_len // group
    col_width = qkv_weight.shape[2]

    qkv_low = jnp.concatenate([qkv_weight[:, i, :].astype(bf16) for i in range(3)], axis=1)
    docs = doc_lengths.shape[1]
    small = [post_gains.T.reshape(-1), head_gains.reshape(-1), doc_lengths[0].astype(f32)]
    small = jnp.concatenate(small)
    pad = -small.shape[0] % 1024
    small = jnp.concatenate([small, jnp.zeros((pad,), f32)]).reshape(-1, 128)
    x_full, qkv_full, small_all = first_gather(tokens, qkv_low, small)
    small_all = small_all.reshape(2 * n_col, -1)
    cut_one, cut_two = 2 * feat, 2 * feat + 2 * col_width
    post_all = small_all[:, :cut_one].reshape(2 * n_col, 2, feat).transpose(1, 0, 2).reshape(2, width)
    gains = lax.dynamic_slice_in_dim(small_all, block_at, 1, 0)[0, cut_one:cut_two].reshape(2, col_width)
    lengths = lax.dynamic_slice_in_dim(small_all, g * n_col, 1, 0)[0, cut_two : cut_two + docs]
    ends = jnp.cumsum(lengths.astype(jnp.int32))
    x_tok = lax.dynamic_slice_in_dim(x_full, block_at * mine, mine, 0)

    def halves(quarter):
        cut = quarter.shape[1] // 2
        return quarter[:, :cut], quarter[:, cut:]

    def gathered(one, two, one_x, two_y):
        one_y = swap_bit(jnp.concatenate([one, one_x]), "dp", 2)
        two_x = swap_bit(jnp.concatenate([two, two_y]), "dp", 1)
        return [one, two, one_x, one_y, two_y, two_x]

    def quarter_of(weight):
        rows = weight.shape[0] // n_dp
        return lax.dynamic_slice_in_dim(weight, d * rows, rows, 0).astype(bf16)

    gate_one, gate_two = halves(quarter_of(gate_weight))
    gate_one, gate_two, post_all = tie(gate_one, gate_two, post_all)
    gate_one = swap(gate_one, "zh")

    out_rows = out_weight.shape[0] // n_dp
    out_part = lax.dynamic_slice_in_dim(out_weight, d * out_rows, out_rows, 0).astype(bf16)
    out_part, post_all = tie(lax.all_gather(out_part, ("zh", "zl"), axis=0), post_all)
    out_part = lax.all_gather(out_part, "dp", axis=1)

    cos_two, sin_two = rotary(seq_len)
    qkv = matmul(x_full, qkv_full)
    squares = jnp.stack(
        [
            jnp.sum(jnp.square(qkv[:, :col_width]), axis=1),
            jnp.sum(jnp.square(qkv[:, col_width : 2 * col_width]), axis=1),
        ],
        axis=0,
    )
    inv_scale = lax.rsqrt(small_sum(squares, ("row", "zl")) / width + norm_eps).T
    gate_two = swap(gate_two, "zh")
    up_one, up_two = halves(quarter_of(up_weight))
    up_one, up_two = swap(up_one, "zh"), swap(up_two, "zh")
    down_quarter = swap(quarter_of(down_weight), "zh")
    inv_scale, gate_one = tie(inv_scale, gate_one)
    query, key, key_t, value, value_t = prepare(qkv, inv_scale, gains, cos_two, sin_two)
    ends, gate_two = tie(ends, gate_two)
    gate_one_x, gate_two_y = swap_bit(gate_one, "dp", 1), swap_bit(gate_two, "dp", 2)
    out_part, key_t = tie(out_part, key_t)
    out_full = lax.all_gather(out_part.reshape(width, width // 2), "row", axis=1, tiled=True)
    att, log_total = attend(query, key, value_t, ends)
    att, up_one, gate_one_x, gate_two_y = tie(att, up_one, gate_one_x, gate_two_y)
    gate_pieces = gathered(gate_one, gate_two, gate_one_x, gate_two_y)

    def to_tokens(vals):
        got = lax.all_to_all(vals.reshape(group, mine, col_width), ("row", "zl"), 0, 0)
        return got.transpose(1, 0, 2).reshape(mine, width)

    def to_heads(vals):
        sent = vals.reshape(mine, group, col_width).transpose(1, 0, 2)
        return lax.all_to_all(sent, ("row", "zl"), 0, 0).reshape(seq_len, col_width)

    att_tok = to_tokens(att)

    gain_attn, gain_mlp = post_all[0:1], post_all[1:2]
    att_tok, up_two, gate_pieces[3], gate_pieces[5] = tie(att_tok, up_two, gate_pieces[3], gate_pieces[5])
    a_pre = matmul(att_tok, out_full)
    a_scale = norm_scale(a_pre)
    h_tok = x_tok.astype(f32) + a_pre * a_scale * gain_attn

    cot = cotangent.reshape(2, 2, tp, mine, feat).transpose(1, 0, 2, 3, 4).reshape(2 * n_col, mine, feat)
    cot, a_scale = tie(cot, a_scale)
    cot = lax.all_to_all(cot, ("row", "zh", "zl"), 0, 0)
    cot_tok = cot.transpose(1, 0, 2).reshape(mine, width).astype(f32)

    up_pieces = gathered(up_one, up_two, swap_bit(up_one, "dp", 1), swap_bit(up_two, "dp", 2))
    gate_low, up_low, down_low = (
        v.astype(bf16) for v in (gate_weight, up_weight, down_weight)
    )
    hidden_width = gate_low.shape[1]
    work = 2 * seq_len * width * hidden_width
    wide, tall = (width, hidden_width), (hidden_width, width)
    h_full, gate_all, up_all, hidden, gate_full, up_full, down_other = tile_call(
        gate_up_job, 1, "gate_up", h_tok.astype(bf16), [[gate_low, *gate_pieces], [up_low, *up_pieces]],
        [wide, wide], [], [hidden_width] * 3, 0, 2 * work, down_quarter,
    )
    down_full, m_pre = tile_call(
        down_job, 2, "down", hidden, [[down_low, down_other]], [tall], [], [], width, work
    )
    m_scale = norm_scale(m_pre)
    mixed_tok = (h_tok + m_pre * m_scale * gain_mlp).astype(bf16)

    def to_features(vals):
        out = lax.all_to_all(
            vals.reshape(mine, 2 * n_col, feat).transpose(1, 0, 2), ("row", "zh", "zl"), 0, 0
        )
        return out.reshape(2, 2, tp, mine, feat).transpose(1, 0, 2, 3, 4).reshape(rows_dev, feat)

    mixed = to_features(mixed_tok)

    grad_m, grad_gain_mlp = norm_back(m_pre, m_scale, gain_mlp, cot_tok)
    dm_full, grad_gate, grad_up, dh_sum = tile_call(
        back_job, 3, "feed_back", grad_m.astype(bf16), [[down_full], [gate_full], [up_full]], [tall, wide, wide],
        [gate_all, up_all], [hidden_width] * 2, width, 3 * work,
    )
    dh_tok = cot_tok + dh_sum

    grad_a, grad_gain_attn = norm_back(a_pre, a_scale, gain_attn, dh_tok)
    grad_a = grad_a.astype(bf16)
    datt = matmul(grad_a, out_full, NT).astype(bf16)
    datt, hidden, h_full = tie(datt, hidden, h_full)
    grad_att = to_heads(datt)
    grad_gate_w = matmul(h_full, grad_gate, TN).astype(bf16)
    grad_up_w = matmul(h_full, grad_up, TN).astype(bf16)
    grad_down_w = matmul(hidden, dm_full, TN).astype(bf16)
    grad_out = matmul(att_tok, grad_a, TN).astype(bf16)

    low_bit, high_bit = d % 2, d // 2

    def pick(vals, dim, index):
        return lax.dynamic_slice_in_dim(vals, index, 1, dim)

    def trade(vals, dim, bit, index):
        got = swap_bit(pick(vals, dim, 1 - index), "dp", bit)
        return (pick(vals, dim, index).astype(f32) + got.astype(f32)).astype(bf16)

    view = grad_down_w.reshape(n_dp // 2, 2, hidden_width // n_dp, width)
    down_one = trade(view[..., : width // 2], 1, 1, low_bit)
    down_two = trade(view[..., width // 2 :], 0, 2, high_bit)

    dqt, dk, dv = attend_back(query, key, key_t, value, grad_att, att, log_total, ends)
    inv_scale, down_one, down_two = tie(inv_scale, down_one, down_two)
    down_one = trade(down_one, 0, 2, high_bit)[0, 0]
    down_two = trade(down_two, 1, 1, low_bit)[0, 0]
    weighted, inner, grad_head = unturn(dqt, dk, qkv, inv_scale, gains, cos_two, sin_two)
    def data_sums(grad):
        half = grad.shape[0] // 2
        return [
            lax.psum_scatter(grad[i * half : (i + 1) * half], "dp", scatter_dimension=0, tiled=True)
            for i in range(2)
        ]

    def owner_parts(pieces):
        keep = jnp.where(r == 0, pieces[0], pieces[1])
        give = jnp.where(r == 0, pieces[1], pieces[0])
        axes = ("row", "zh")
        return [
            keep,
            lax.ppermute(keep, axes, [(1, 0), (2, 3)]),
            lax.ppermute(give, axes, [(1, 2), (2, 1)]),
            lax.ppermute(give, axes, [(0, 2), (3, 1)]),
        ]

    gate_parts = owner_parts(data_sums(grad_gate_w))
    up_sums = data_sums(grad_up_w)
    inner, *gate_parts = tie(inner, *gate_parts)
    sum_gate = jnp.where(same, gate_parts[0].astype(f32), 0.0)
    for part in gate_parts[1:]:
        sum_gate = sum_gate + part.astype(f32)
    inner = (small_sum(inner.T, ("row", "zl")) / width).T
    cube = inv_scale * inv_scale * inv_scale * inner
    dqkv = jnp.concatenate(
        [
            (inv_scale[:, 0:1] * weighted[:, :col_width] - qkv[:, :col_width] * cube[:, 0:1]).astype(bf16),
            (inv_scale[:, 1:2] * weighted[:, col_width:] - qkv[:, col_width : 2 * col_width] * cube[:, 1:2]).astype(bf16),
            dv,
        ],
        axis=1,
    )
    grad_qkv = matmul(x_full, dqkv, TN).astype(bf16)

    dx = matmul(dqkv, qkv_full, NT).astype(bf16)
    here = lax.dynamic_slice_in_dim(dx, block_at * mine, mine, 0).astype(f32) + dh_tok
    dx = lax.dynamic_update_slice_in_dim(dx, here.astype(bf16), block_at * mine, 0)
    dtokens, sum_qkv, sum_up, sum_down = last_sums(
        dx, grad_qkv, [jnp.stack(up_sums), jnp.stack([down_one, down_two])]
    )
    sum_qkv = sum_qkv.reshape(qkv_first.shape)

    half_w = width // 2
    half = lax.dynamic_slice_in_dim(grad_out, r * half_w, half_w, 1).astype(f32) + swap(
        lax.dynamic_slice_in_dim(grad_out, (1 - r) * half_w, half_w, 1), "row"
    ).astype(f32)
    half = half.astype(bf16).reshape(n_col, n_dp, out_rows, width // 2)
    half = lax.psum_scatter(half, "dp", scatter_dimension=1, tiled=False)
    sum_out = lax.psum_scatter(half, ("zh", "zl"), scatter_dimension=0, tiled=False).astype(f32)

    head_place = lax.dynamic_update_slice_in_dim(
        jnp.zeros((2, width), f32), grad_head, block_at * col_width, 1
    )
    small = jnp.concatenate([head_place, grad_gain_attn[None], grad_gain_mlp[None]], axis=0)
    small = small_sum(small, ("dp", "row", "zh", "zl"))
    col_at = g * tp + t
    sum_head = lax.dynamic_slice_in_dim(small[:2], col_at * col_width, col_width, 1)
    post_rows = post_first.shape[0]
    sum_post = lax.dynamic_slice_in_dim(
        small[2:], ((r * n_col + col_at) * n_dp + d) * post_rows, post_rows, 1
    ).T

    def owned_rows(weight, part_rows):
        return lax.dynamic_slice_in_dim(weight, d * part_rows, part_rows, 0)

    results = []
    for weight, total, first, second in (
        (qkv_weight, sum_qkv, qkv_first, qkv_second),
        (out_weight, sum_out, out_first, out_second),
        (gate_weight, sum_gate, gate_first, gate_second),
        (up_weight, sum_up, up_first, up_second),
        (down_weight, sum_down, down_first, down_second),
    ):
        results.extend(
            adamw_step(owned_rows(weight, total.shape[0]), total, first, second, rate_matrix, weight_decay)
        )
    results.extend(adamw_step(head_gains, sum_head, head_first, head_second, rate_gain, 0.0))
    results.extend(
        adamw_step(owned_rows(post_gains, post_rows), sum_post, post_first, post_second, rate_gain, 0.0)
    )
    return (mixed, dtokens, *results)


def solution(mesh):
    n_dp, n_row, n_col = (mesh.shape[name] for name in ("dp", "row", "col"))
    grid = Mesh(mesh.devices.reshape(n_dp, n_row, 2, n_col // 2), ("dp", "row", "zh", "zl"))
    col = ("zh", "zl")
    moved = P("dp", ("row", *col))
    qkv_part = P(("row", "dp"), None, col)
    flat_part = P((*col, "dp"), "row")
    wide_part = P(("row", "dp"), col)
    head_part = P(None, col)
    post_part = P(("row", *col, "dp"), None)
    in_specs = (
        moved,
        moved,
        P(("dp", "row"), None),
        P("row", None, col),
        P(col, "row"),
        P("row", col),
        P("row", col),
        P(col, "row"),
        head_part,
        P(("row", *col), None),
        *[spec for spec in (qkv_part, flat_part, wide_part, wide_part, flat_part, head_part, post_part) for _ in range(2)],
    )
    out_specs = (
        moved,
        moved,
        *[spec for spec in (qkv_part, flat_part, wide_part, wide_part, flat_part, head_part, post_part) for _ in range(3)],
    )
    return jax.shard_map(shards, mesh=grid, in_specs=in_specs, out_specs=out_specs, check_vma=False)
```

```python
import functools

import jax
import jax.numpy as jnp
from jax import lax
from jax.experimental import pallas as pl
from jax.experimental.pallas import tpu as pltpu
from jax.sharding import Mesh
from jax.sharding import PartitionSpec as P

HD = 128
STEP = 10

norm_eps = 1e-06
rope_base = 500000.0
beta_one = 0.9
beta_two = 0.95
adam_eps = 1e-08
weight_decay = 0.1
rate_matrix = 0.02
rate_gain = 0.6
big_negative = -1e30
log2_e = 1.4426950408889634

f32 = jnp.float32
bf16 = jnp.bfloat16
NN = (((1,), (0,)), ((), ()))
NT = (((1,), (1,)), ((), ()))
TN = (((0,), (0,)), ((), ()))


def swap(piece, axis):
    return lax.ppermute(piece, axis, [(0, 1), (1, 0)])


def shift(piece, axis, step):
    size = lax.axis_size(axis)
    return lax.ppermute(piece, axis, [(i, (i + step) % size) for i in range(size)])


def swap_bit(piece, axis, bit):
    return lax.ppermute(piece, axis, [(i, i ^ bit) for i in range(lax.axis_size(axis))])


def small_sum(vals, axes):
    for axis in axes:
        bit = 1
        while bit < lax.axis_size(axis):
            vals = vals + swap_bit(vals, axis, bit)
            bit *= 2
    return vals


def tie(*vals):
    return lax.optimization_barrier(vals)


def small_sum(vals, axes):
    for axis in axes:
        bit = 1
        while bit < lax.axis_size(axis):
            vals = vals + swap_bit(vals, axis, bit)
            bit *= 2
    return vals


def gather_kernel(
    chunks, tok_ref, low_ref, post_ref, next_ref, x_ref, w_ref, all_ref, ex_ref, got_ref,
    own_sem, zh_send, zh_recv, t_send, t_recv, r_send, r_recv,
    wz_send, wz_recv, wd_send, wd_recv, wr_send, wr_recv, wl_sem, p_send, p_recv, n_send, n_recv,
):
    n_dp = lax.axis_size("dp")
    tp = lax.axis_size("zl")
    d, r, g, t = (lax.axis_index(name) for name in ("dp", "row", "zh", "zl"))
    same = r == g
    feat = tok_ref.shape[1]
    seq_len = tok_ref.shape[0] // 2
    step = seq_len // chunks
    half = low_ref.shape[0]
    rows = half // n_dp

    def place(row, zh, zl):
        return (row * 2 + zh) * tp + zl

    def land(block, c):
        return x_ref.at[block, pl.ds(c * step, step)]

    def remote(src, dst, send, recv, dev):
        return pltpu.make_async_remote_copy(
            src_ref=src, dst_ref=dst, send_sem=send, recv_sem=recv, device_id=dev,
            device_id_type=pl.DeviceIdType.MESH,
        )

    barrier = pltpu.get_barrier_semaphore()
    count = 0
    for dd in range(n_dp):
        for rr in range(2):
            if dd or rr:
                dev = (lax.rem(d + dd, n_dp), lax.rem(r + rr, 2), g, t)
                pl.semaphore_signal(barrier, inc=1, device_id=dev, device_id_type=pl.DeviceIdType.MESH)
                count += 1
    for rr in range(2):
        for gg in range(2):
            for tt in range(tp):
                if gg or tt:
                    dev = (d, lax.rem(r + rr, 2), lax.rem(g + gg, 2), lax.rem(t + tt, tp))
                    pl.semaphore_signal(barrier, inc=1, device_id=dev, device_id_type=pl.DeviceIdType.MESH)
                    count += 1
    pl.semaphore_wait(barrier, count)

    row_dev = (d, 1 - r, g, t)
    zh_dev = (d, r, 1 - g, t)
    mine = place(r, g, t)
    pending = []

    wz = remote(low_ref.at[pl.ds(pl.multiple_of(d * rows, rows), rows)], ex_ref, wz_send, wz_recv, zh_dev)
    wz.start()

    def own_src(c):
        return tok_ref.at[pl.ds(pl.multiple_of(g * seq_len + c * step, step), step)]

    zh_copies = []
    for c in range(chunks):
        src = tok_ref.at[pl.ds(pl.multiple_of((1 - g) * seq_len + c * step, step), step)]
        zh_copies.append(remote(src, land(mine, c), zh_send.at[c], zh_recv.at[c], zh_dev))
        for s in range(1, tp):
            cp = remote(
                own_src(c), land(mine, c), t_send.at[s, 0, c], t_recv.at[s, 0, c], (d, r, g, lax.rem(t + s, tp))
            )
            cp.start()
            pending.append(cp)
    local = []
    for c in range(chunks):
        cp = pltpu.make_async_copy(own_src(c), land(mine, c), own_sem.at[c])
        cp.start()
        local.append(cp)
        cp = remote(own_src(c), land(mine, c), r_send.at[0, 0, c], r_recv.at[0, 0, c], row_dev)
        cp.start()
        pending.append(cp)

    wz.wait_send()
    lead = max(1, chunks // 4)
    for cp in zh_copies[:lead]:
        cp.start()

    half_at = pl.ds(pl.multiple_of(r * half, half), half)
    w_row = remote(low_ref, w_ref.at[half_at], wr_send, wr_recv, row_dev)
    w_loc = pltpu.make_async_copy(low_ref, w_ref.at[half_at], wl_sem.at[0])

    @pl.when(same)
    def _():
        w_loc.start()

    @pl.when(jnp.logical_not(same))
    def _():
        w_row.start()

    posts = []
    n_all = 4 * tp
    p_loc = pltpu.make_async_copy(post_ref, all_ref.at[mine], wl_sem.at[1])
    p_loc.start()
    index = 0
    for rr in range(2):
        for gg in range(2):
            for tt in range(tp):
                if rr or gg or tt:
                    dev = (d, lax.rem(r + rr, 2), lax.rem(g + gg, 2), lax.rem(t + tt, tp))
                    cp = remote(post_ref, all_ref.at[mine], p_send.at[index], p_recv.at[index], dev)
                    cp.start()
                    posts.append(cp)
                    index += 1

    def drain_zh(c):
        zh_copies[c].wait_recv()
        theirs = place(r, 1 - g, t)
        for s in range(1, tp):
            cp = remote(
                land(theirs, c), land(theirs, c), t_send.at[s, 1, c], t_recv.at[s, 1, c],
                (d, r, g, lax.rem(t + s, tp)),
            )
            cp.start()
            pending.append(cp)
        cp = remote(land(theirs, c), land(theirs, c), r_send.at[0, 1, c], r_recv.at[0, 1, c], row_dev)
        cp.start()
        pending.append(cp)

    def drain_t(z, c):
        for s in range(1, tp):
            came = place(r, g if z == 0 else 1 - g, lax.rem(t + tp - s, tp))
            remote(
                land(came, c), land(came, c), t_send.at[s, z, c], t_recv.at[s, z, c],
                (d, r, g, lax.rem(t + s, tp)),
            ).wait_recv()
            cp = remote(land(came, c), land(came, c), r_send.at[s, z, c], r_recv.at[s, z, c], row_dev)
            cp.start()
            pending.append(cp)

    wz.wait_recv()
    spot = pl.ds(pl.multiple_of(r * half + d * rows, rows), rows)
    far = []
    for dd in range(1, n_dp):
        cp = remote(
            ex_ref, w_ref.at[spot], wd_send.at[dd], wd_recv.at[dd, r], (lax.rem(d + dd, n_dp), 1 - g, g, t)
        )
        cp.start()
        far.append(cp)
        for late in zh_copies[lead:][dd - 1 : dd]:
            late.start()
    for late in zh_copies[lead:][n_dp - 1 :]:
        late.start()
    following = remote(next_ref, got_ref, n_send, n_recv, zh_dev)
    following.start()
    near_remote = remote(ex_ref, w_ref.at[spot], wd_send.at[0], wd_recv.at[0, r], row_dev)
    near_local = pltpu.make_async_copy(ex_ref, w_ref.at[spot], wl_sem.at[2])

    @pl.when(same)
    def _():
        near_remote.start()

    @pl.when(jnp.logical_not(same))
    def _():
        near_local.start()

    for c in range(chunks):
        drain_t(0, c)
        drain_zh(c)
        if c >= 1:
            drain_t(1, c - 1)
    drain_t(1, chunks - 1)

    for c in range(chunks):
        for z in range(2):
            for s in range(tp):
                came = place(1 - r, g if z == 0 else 1 - g, lax.rem(t + tp - s, tp))
                remote(
                    land(came, c), land(came, c), r_send.at[s, z, c], r_recv.at[s, z, c], row_dev
                ).wait_recv()
    for cp in local:
        cp.wait()
    for cp in pending:
        cp.wait_send()
    for cp in zh_copies:
        cp.wait_send()
    following.wait()
    p_loc.wait()
    for cp in posts:
        cp.wait_send()
    index = 0
    for rr in range(2):
        for gg in range(2):
            for tt in range(tp):
                if rr or gg or tt:
                    came = place(
                        lax.rem(r + 2 - rr, 2), lax.rem(g + 2 - gg, 2), lax.rem(t + tp - tt, tp)
                    )
                    remote(
                        post_ref, all_ref.at[came], p_send.at[index], p_recv.at[index], row_dev
                    ).wait_recv()
                    index += 1
    for cp in far:
        cp.wait_send()

    @pl.when(same)
    def _():
        w_loc.wait()
        near_remote.wait_send()
        remote(
            low_ref, w_ref.at[pl.ds(pl.multiple_of((1 - r) * half, half), half)], wr_send, wr_recv, row_dev
        ).wait_recv()

    @pl.when(jnp.logical_not(same))
    def _():
        w_row.wait_send()
        near_local.wait()
        for dd in range(n_dp):
            for rr in range(2):
                src_d = lax.rem(d + n_dp - dd, n_dp)
                src_r = r if rr == 0 else 1 - r
                if dd == 0 and rr == 0:
                    continue
                at = pl.ds(pl.multiple_of(src_r * half + src_d * rows, rows), rows)
                remote(ex_ref, w_ref.at[at], wd_send.at[dd], wd_recv.at[dd, src_r], row_dev).wait_recv()


def first_gather(tokens, low, post, following):
    n_dp = lax.axis_size("dp")
    tp = lax.axis_size("zl")
    rows_dev, feat = tokens.shape
    seq_len = rows_dev // 2
    width = feat * 4 * tp
    chunks = 4 if tp == 2 else 1
    anywhere = pl.BlockSpec(memory_space=pl.ANY)
    dma = pltpu.SemaphoreType.DMA
    x_shape = (4 * tp, seq_len, feat)
    x_full, w_full, post_all, _, got = pl.pallas_call(
        functools.partial(gather_kernel, chunks),
        in_specs=[anywhere] * 4,
        out_specs=[anywhere] * 5,
        out_shape=[
            jax.ShapeDtypeStruct(x_shape, bf16),
            jax.ShapeDtypeStruct((2 * low.shape[0], low.shape[1]), bf16),
            jax.ShapeDtypeStruct((4 * tp, *post.shape), f32),
            jax.ShapeDtypeStruct((low.shape[0] // n_dp, low.shape[1]), bf16),
            jax.ShapeDtypeStruct(following.shape, bf16),
        ],
        scratch_shapes=[
            dma((chunks,)),
            dma((chunks,)),
            dma((chunks,)),
            dma((tp, 2, chunks)),
            dma((tp, 2, chunks)),
            dma((tp, 2, chunks)),
            dma((tp, 2, chunks)),
            dma(()),
            dma(()),
            dma((n_dp,)),
            dma((n_dp, 2)),
            dma(()),
            dma(()),
            dma((3,)),
            dma((4 * tp,)),
            dma((4 * tp,)),
            dma(()),
            dma(()),
        ],
        compiler_params=pltpu.CompilerParams(collective_id=0, has_side_effects=True),
        cost_estimate=pl.CostEstimate(flops=0, bytes_accessed=6 * seq_len * width, transcendentals=0),
        name="first_gather",
    )(tokens, low, post, following)
    x_full = x_full.transpose(1, 0, 2).reshape(seq_len, width)
    return x_full, w_full, post_all, got


def doc_start(ends_ref, docs, places):
    start = jnp.zeros_like(places)
    for i in range(docs):
        end = ends_ref[i]
        start = jnp.where(places >= end, end, start)
    return start


def attend_kernel(docs, bk, ends_ref, q_ref, k_ref, vt_ref, o_ref, lse_ref):
    bq = q_ref.shape[0]
    q0 = pl.program_id(1) * bq
    places = q0 + lax.broadcasted_iota(jnp.int32, (1, bq), 1)
    start = doc_start(ends_ref, docs, places)
    lowest = jnp.int32(0)
    for i in range(docs):
        lowest = jnp.where(ends_ref[i] <= q0, ends_ref[i], lowest)
    query = q_ref[...]
    scale = log2_e * HD ** (-0.5)

    def step(j, carry):
        top, total, acc = carry
        k0 = pl.multiple_of(j * bk, bk)
        key = k_ref[pl.ds(k0, bk), :]
        scores = lax.dot_general(key, query, NT, preferred_element_type=f32) * scale
        rows = k0 + lax.broadcasted_iota(jnp.int32, (bk, 1), 0)
        scores = jnp.where((rows <= places) & (rows >= start), scores, big_negative)
        top_new = jnp.maximum(top, jnp.max(scores, axis=0, keepdims=True))
        prob = jnp.exp2(scores - top_new)
        fade = jnp.exp2(top - top_new)
        total = total * fade + jnp.sum(prob, axis=0, keepdims=True)
        acc = acc * fade + lax.dot_general(
            vt_ref[:, pl.ds(k0, bk)], prob.astype(bf16), NN, preferred_element_type=f32
        )
        return top_new, total, acc

    first = (
        jnp.full((1, bq), big_negative, f32),
        jnp.zeros((1, bq), f32),
        jnp.zeros((HD, bq), f32),
    )
    top, total, acc = lax.fori_loop(lowest // bk, (q0 + bq - 1) // bk + 1, step, first)
    o_ref[...] = (acc * (1.0 / total)).T.astype(bf16)
    lse_ref[0] = top + jnp.log2(total)


def attend(query, key, value_t, ends):
    seq_len, width = query.shape
    heads = width // HD
    block = min(512, seq_len)
    docs = ends.shape[0]
    return pl.pallas_call(
        functools.partial(attend_kernel, docs, block),
        grid_spec=pltpu.PrefetchScalarGridSpec(
            num_scalar_prefetch=1,
            grid=(heads, seq_len // block),
            in_specs=[
                pl.BlockSpec((block, HD), lambda h, i, e: (i, h)),
                pl.BlockSpec((seq_len, HD), lambda h, i, e: (0, h)),
                pl.BlockSpec((HD, seq_len), lambda h, i, e: (h, 0)),
            ],
            out_specs=[
                pl.BlockSpec((block, HD), lambda h, i, e: (i, h)),
                pl.BlockSpec((1, 1, block), lambda h, i, e: (h, 0, i)),
            ],
        ),
        out_shape=[
            jax.ShapeDtypeStruct((seq_len, width), bf16),
            jax.ShapeDtypeStruct((heads, 1, seq_len), f32),
        ],
        compiler_params=pltpu.CompilerParams(vmem_limit_bytes=48 << 20),
        cost_estimate=pl.CostEstimate(
            flops=2 * heads * seq_len * seq_len * HD,
            bytes_accessed=8 * seq_len * width,
            transcendentals=heads * seq_len * seq_len // 2,
        ),
        name="attend",
    )(ends, query, key, value_t)


def attend_back_kernel(
    docs, bq, ends_ref, q_ref, k_ref, kt_ref, v_ref, do_ref, o_ref, lse_ref,
    dqt_ref, dk_ref, dv_ref, dk_acc, dv_acc, delta_acc
):
    bk = k_ref.shape[0]
    seq_len = q_ref.shape[0]
    j = pl.program_id(1)
    k0 = j * bk
    scale = HD ** (-0.5)
    last = jnp.int32(seq_len)
    for i in reversed(range(docs)):
        last = jnp.where(ends_ref[i] > k0 + bk - 1, ends_ref[i], last)
    rows = k0 + lax.broadcasted_iota(jnp.int32, (bk, 1), 0)

    @pl.when(j == 0)
    def _():
        dqt_ref[...] = jnp.zeros_like(dqt_ref)
        ones = jnp.ones((8, HD), bf16)
        for i in range(seq_len // bq):
            part = slice(i * bq, (i + 1) * bq)
            prod = do_ref[part, :].astype(f32) * o_ref[part, :].astype(f32)
            high = prod.astype(bf16)
            low = (prod - high.astype(f32)).astype(bf16)
            delta_acc[:, part] = lax.dot_general(
                ones, high, NT, preferred_element_type=f32
            ) + lax.dot_general(ones, low, NT, preferred_element_type=f32)

    dk_acc[...] = jnp.zeros_like(dk_acc)
    dv_acc[...] = jnp.zeros_like(dv_acc)
    key = k_ref[...]
    value = v_ref[...]
    key_t = kt_ref[...]

    def step(i, carry):
        q0 = pl.multiple_of(i * bq, bq)
        cols = pl.ds(q0, bq)
        query = q_ref[cols, :]
        grad = do_ref[cols, :]
        places = q0 + lax.broadcasted_iota(jnp.int32, (1, bq), 1)
        start = doc_start(ends_ref, docs, places)
        scores = lax.dot_general(key, query, NT, preferred_element_type=f32) * (scale * log2_e)
        allowed = (rows <= places) & (rows >= start)
        prob = jnp.where(allowed, jnp.exp2(scores - lse_ref[0, :, cols]), 0.0)
        dv_acc[...] += lax.dot_general(prob.astype(bf16), grad, NN, preferred_element_type=f32)
        grad_prob = lax.dot_general(value, grad, NT, preferred_element_type=f32)
        grad_score = (prob * (grad_prob - delta_acc[0:1, cols])).astype(bf16)
        dk_acc[...] += lax.dot_general(grad_score, query, NN, preferred_element_type=f32)
        dqt_ref[:, cols] += lax.dot_general(key_t, grad_score, NN, preferred_element_type=f32) * scale
        return carry

    lax.fori_loop(k0 // bq, (last + bq - 1) // bq, step, 0)
    dk_ref[...] = dk_acc[...] * scale
    dv_ref[...] = dv_acc[...].astype(bf16)


def attend_back(query, key, key_t, value, grad, att, log_total, ends):
    seq_len, width = query.shape
    heads = width // HD
    block = min(512, seq_len)
    docs = ends.shape[0]
    whole = pl.BlockSpec((seq_len, HD), lambda h, j, e: (0, h))
    part = pl.BlockSpec((block, HD), lambda h, j, e: (j, h))
    line = pl.BlockSpec((1, 1, seq_len), lambda h, j, e: (h, 0, 0))
    return pl.pallas_call(
        functools.partial(attend_back_kernel, docs, block),
        grid_spec=pltpu.PrefetchScalarGridSpec(
            num_scalar_prefetch=1,
            grid=(heads, seq_len // block),
            in_specs=[
                whole,
                part,
                pl.BlockSpec((HD, block), lambda h, j, e: (h, j)),
                part,
                whole,
                whole,
                line,
            ],
            out_specs=[
                pl.BlockSpec((HD, seq_len), lambda h, j, e: (h, 0)),
                part,
                part,
            ],
            scratch_shapes=[
                pltpu.VMEM((block, HD), f32),
                pltpu.VMEM((block, HD), f32),
                pltpu.VMEM((8, seq_len), f32),
            ],
        ),
        out_shape=[
            jax.ShapeDtypeStruct((width, seq_len), f32),
            jax.ShapeDtypeStruct((seq_len, width), f32),
            jax.ShapeDtypeStruct((seq_len, width), bf16),
        ],
        compiler_params=pltpu.CompilerParams(vmem_limit_bytes=48 << 20),
        cost_estimate=pl.CostEstimate(
            flops=5 * heads * seq_len * seq_len * HD,
            bytes_accessed=20 * seq_len * width,
            transcendentals=heads * seq_len * seq_len // 2,
        ),
        name="attend_back",
    )(ends, query, key, key_t, value, grad, att, log_total)


def turn(values, cos_two, sin_two):
    return values * cos_two + pltpu.roll(values, HD // 2, 1) * sin_two


def prepare_kernel(qkv_ref, scale_ref, gains_ref, cos_ref, sin_ref, q_ref, k_ref, kt_ref, v_ref, vt_ref):
    width = q_ref.shape[1]
    cos_two = cos_ref[...]
    sin_two = sin_ref[...]
    for which, out_ref in ((0, q_ref), (1, k_ref)):
        scale = scale_ref[:, which : which + 1]
        for head in range(width // HD):
            cols = slice(head * HD, (head + 1) * HD)
            vals = qkv_ref[:, which * width + head * HD : which * width + (head + 1) * HD]
            out = turn(vals * scale * gains_ref[which : which + 1, cols], cos_two, sin_two)
            out_ref[:, cols] = out.astype(bf16)
            if which == 1:
                kt_ref[cols, :] = out.T.astype(bf16)
    value = qkv_ref[:, 2 * width :]
    v_ref[...] = value.astype(bf16)
    vt_ref[...] = value.T.astype(bf16)


def prepare(qkv, inv_scale, gains, cos_two, sin_two):
    seq_len, triple = qkv.shape
    width = triple // 3
    block = min(256, seq_len)
    flat = pl.BlockSpec((block, width), lambda i: (i, 0))
    tall = pl.BlockSpec((width, block), lambda i: (0, i))
    table = pl.BlockSpec((block, HD), lambda i: (i, 0))
    return pl.pallas_call(
        prepare_kernel,
        grid=(seq_len // block,),
        in_specs=[
            pl.BlockSpec((block, triple), lambda i: (i, 0)),
            pl.BlockSpec((block, 2), lambda i: (i, 0)),
            pl.BlockSpec((2, width), lambda i: (0, 0)),
            table,
            table,
        ],
        out_specs=[flat, flat, tall, flat, tall],
        out_shape=[
            jax.ShapeDtypeStruct((seq_len, width), bf16),
            jax.ShapeDtypeStruct((seq_len, width), bf16),
            jax.ShapeDtypeStruct((width, seq_len), bf16),
            jax.ShapeDtypeStruct((seq_len, width), bf16),
            jax.ShapeDtypeStruct((width, seq_len), bf16),
        ],
        compiler_params=pltpu.CompilerParams(vmem_limit_bytes=48 << 20),
        cost_estimate=pl.CostEstimate(flops=10 * seq_len * triple, bytes_accessed=8 * seq_len * triple, transcendentals=0),
        name="prepare",
    )(qkv, inv_scale, gains, cos_two, sin_two)


def unturn_kernel(dqt_ref, dk_ref, qkv_ref, scale_ref, gains_ref, cos_ref, sin_ref, hat_ref, inner_ref, gain_ref):
    width = dk_ref.shape[1]
    cos_two = cos_ref[...]
    sin_two = sin_ref[...]

    @pl.when(pl.program_id(0) == 0)
    def _():
        gain_ref[...] = jnp.zeros_like(gain_ref)

    for which in range(2):
        scale = scale_ref[:, which : which + 1]
        inner = jnp.zeros((dk_ref.shape[0], HD), f32)
        for head in range(width // HD):
            cols = slice(head * HD, (head + 1) * HD)
            off = which * width + head * HD
            grad = dqt_ref[cols, :].T if which == 0 else dk_ref[:, cols]
            hat = turn(grad, cos_two, -sin_two)
            pre = qkv_ref[:, off : off + HD]
            prod = hat * pre
            gain_ref[which : which + 1, cols] += jnp.sum(prod * scale, axis=0, keepdims=True)
            inner = inner + prod * gains_ref[which : which + 1, cols]
            hat_ref[:, off : off + HD] = hat * gains_ref[which : which + 1, cols]
        inner_ref[:, which : which + 1] = jnp.sum(inner, axis=1, keepdims=True)


def unturn(dqt, dk, qkv, inv_scale, gains, cos_two, sin_two):
    seq_len, width = dk.shape
    block = min(256, seq_len)
    table = pl.BlockSpec((block, HD), lambda i: (i, 0))
    pair = pl.BlockSpec((block, 2), lambda i: (i, 0))
    return pl.pallas_call(
        unturn_kernel,
        grid=(seq_len // block,),
        in_specs=[
            pl.BlockSpec((width, block), lambda i: (0, i)),
            pl.BlockSpec((block, width), lambda i: (i, 0)),
            pl.BlockSpec((block, 2 * width), lambda i: (i, 0)),
            pair,
            pl.BlockSpec((2, width), lambda i: (0, 0)),
            table,
            table,
        ],
        out_specs=[
            pl.BlockSpec((block, 2 * width), lambda i: (i, 0)),
            pair,
            pl.BlockSpec((2, width), lambda i: (0, 0)),
        ],
        out_shape=[
            jax.ShapeDtypeStruct((seq_len, 2 * width), f32),
            jax.ShapeDtypeStruct((seq_len, 2), f32),
            jax.ShapeDtypeStruct((2, width), f32),
        ],
        compiler_params=pltpu.CompilerParams(vmem_limit_bytes=48 << 20),
        cost_estimate=pl.CostEstimate(flops=20 * seq_len * width, bytes_accessed=24 * seq_len * width, transcendentals=0),
        name="unturn",
    )(dqt, dk, qkv, inv_scale, gains, cos_two, sin_two)


class Job:
    def __init__(self, gather, scatter, merge, weights, pieces, dim, spread, tile_ins, outs, slots, sums, body):
        self.gather, self.scatter, self.merge, self.spread = gather, scatter, merge, spread
        self.weights, self.pieces, self.dim = weights, pieces, dim
        self.tile_ins, self.outs = tile_ins, outs
        self.slots, self.sums, self.body = slots, sums, body


def tile_kernel(job, tp, chunks, *refs):
    refs = list(refs)

    def take(count):
        got = refs[:count]
        del refs[:count]
        return got

    (src_ref,) = take(1)
    w_hbm = [take(max(1, job.pieces)) for _ in range(job.weights)]
    ti_hbm = take(job.tile_ins)
    quarter_ref = take(1)[0] if job.spread else None
    full_ref = take(1)[0] if job.gather else src_ref
    out_hbm = take(job.outs)
    w_out = take(job.weights) if job.pieces else None
    spread_ref = take(1)[0] if job.spread else None
    total_ref = take(1)[0] if job.scatter else None
    w_ref = take(job.weights)
    (tile_ref,) = take(1)
    ti_ref = take(job.tile_ins)
    out_ref = take(job.outs)
    y_ref, rbuf, zbuf, tbuf = take(4) if job.scatter else (None,) * 4
    w_sem, tile_sem, ti_sem, out_sem, loc_sem = take(5)
    t_send, t_recv, r_send, r_recv = take(4)
    y_send, y_recv, z_send, z_recv = take(4)
    wl_sem, wr_send, wr_recv, q_send, q_recv = take(5)

    n_dp = lax.axis_size("dp")
    d, r, g, t = (lax.axis_index(name) for name in ("dp", "row", "zh", "zl"))
    rows = tile_ref.shape[1]
    if job.merge:
        mc = rows // (2 * chunks)
        order = [(s, 0) for s in range(tp)]
    else:
        mc = rows // 2
        order = [(s, c) for c in range(chunks) for s in range(tp)]
    if not job.gather:
        order = [(s, c) for s in list(range(1, tp)) + [0] for c in range(chunks)]
    row_dev = (d, 1 - r, g, t)

    def peer(step):
        return (d, r, g, lax.rem(t + step + tp, tp))

    def remote(src, dst, send, recv, dev):
        return pltpu.make_async_remote_copy(
            src_ref=src, dst_ref=dst, send_sem=send, recv_sem=recv, device_id=dev,
            device_id_type=pl.DeviceIdType.MESH,
        )

    def piece(s, c, rho):
        return full_ref.at[pl.ds(((s * chunks + c) * 2 + rho) * mc, mc)]

    barrier = pltpu.get_barrier_semaphore()
    pl.semaphore_signal(barrier, inc=1, device_id=row_dev, device_id_type=pl.DeviceIdType.MESH)
    for s in range(1, tp):
        pl.semaphore_signal(barrier, inc=1, device_id=peer(s), device_id_type=pl.DeviceIdType.MESH)

    count = tp
    if job.spread:
        for k in range(1, n_dp):
            dev = (lax.rem(d + k, n_dp), r, g, t)
            pl.semaphore_signal(barrier, inc=1, device_id=dev, device_id_type=pl.DeviceIdType.MESH)
            count += 1
    same = r == g
    other_core = jnp.logical_not(same)

    def half_view(i, half, row_at, row_count, col_at, col_count):
        ref = w_ref[i]
        if job.dim == 0:
            size = ref.shape[0] // 2
            start = pl.multiple_of(half * size + row_at, row_count)
            return ref.at[pl.ds(start, row_count), pl.ds(col_at, col_count)]
        size = ref.shape[1] // 2
        return ref.at[pl.ds(row_at, row_count), pl.ds(pl.multiple_of(half * size + col_at, col_count), col_count)]

    def piece_list(i):
        if len(w_hbm[i]) == 2:
            other = w_hbm[i][1]
            return [(other, 0, other.shape[0], 0, other.shape[1])]
        one, two, one_x, one_y, two_y, two_x = w_hbm[i][1:]
        rows_q, cut = one.shape
        low_bit, high_bit = lax.rem(d, 2), d // 2
        places = [
            ((high_bit * (1 - 2 * (k // 2)) + k // 2) * 2 + low_bit * (1 - 2 * (k % 2)) + k % 2) * rows_q
            for k in range(4)
        ]
        upper, lower = pl.ds(0, rows_q), pl.ds(rows_q, rows_q)
        return [
            (one, places[0], rows_q, 0, cut),
            (one_x, places[1], rows_q, 0, cut),
            (one_y.at[upper], places[2], rows_q, 0, cut),
            (one_y.at[lower], places[3], rows_q, 0, cut),
            (two, places[0], rows_q, cut, cut),
            (two_x.at[upper], places[1], rows_q, cut, cut),
            (two_y, places[2], rows_q, cut, cut),
            (two_x.at[lower], places[3], rows_q, cut, cut),
        ]

    def piece_recv_places(i):
        return [half_view(i, 1 - r, *spot[1:]) for spot in piece_list(i)]

    def low_copies(i):
        low = w_hbm[i][0]
        there = half_view(i, r, 0, low.shape[0], 0, low.shape[1])
        here = half_view(i, 1 - r, 0, low.shape[0], 0, low.shape[1])
        keep = pltpu.make_async_copy(low, there, wl_sem.at[i, 0])
        give = pltpu.make_async_remote_copy(
            src_ref=low, dst_ref=there, send_sem=wr_send.at[i, 0], recv_sem=wr_recv.at[i, 0],
            device_id=row_dev, device_id_type=pl.DeviceIdType.MESH,
        )
        got = pltpu.make_async_remote_copy(
            src_ref=low, dst_ref=here, send_sem=wr_send.at[i, 0], recv_sem=wr_recv.at[i, 0],
            device_id=row_dev, device_id_type=pl.DeviceIdType.MESH,
        )
        return keep, give, got

    def part_copies(i):
        keeps, gives, gots = [], [], []
        for p, spot in enumerate(piece_list(i)):
            there = half_view(i, r, *spot[1:])
            here = piece_recv_places(i)[p]
            keeps.append(pltpu.make_async_copy(spot[0], there, wl_sem.at[i, p]))
            for dst, into in ((there, gives), (here, gots)):
                into.append(
                    pltpu.make_async_remote_copy(
                        src_ref=spot[0], dst_ref=dst, send_sem=wr_send.at[i, p], recv_sem=wr_recv.at[i, p],
                        device_id=row_dev, device_id_type=pl.DeviceIdType.MESH,
                    )
                )
        return keeps, gives, gots

    def w_start(i):
        if not job.pieces:
            pltpu.make_async_copy(w_hbm[i][0], w_ref[i], w_sem.at[i]).start()
            return

        @pl.when(same)
        def _():
            low_copies(i)[0].start()
            for cp in part_copies(i)[1]:
                cp.start()

        @pl.when(other_core)
        def _():
            low_copies(i)[1].start()
            for cp in part_copies(i)[0]:
                cp.start()

    def w_wait(i):
        if not job.pieces:
            pltpu.make_async_copy(w_hbm[i][0], w_ref[i], w_sem.at[i]).wait()
            return

        @pl.when(same)
        def _():
            low_copies(i)[0].wait()
            low_copies(i)[2].wait_recv()

        @pl.when(other_core)
        def _():
            for cp in part_copies(i)[0]:
                cp.wait()
            for cp in part_copies(i)[2]:
                cp.wait_recv()

        pltpu.make_async_copy(w_ref[i], w_out[i], w_sem.at[i]).start()

    def w_end(i):

        @pl.when(same)
        def _():
            for cp in part_copies(i)[1]:
                cp.wait_send()

        @pl.when(other_core)
        def _():
            low_copies(i)[1].wait_send()

        pltpu.make_async_copy(w_ref[i], w_out[i], w_sem.at[i]).wait()

    if not job.pieces:
        for i in range(job.weights):
            w_start(i)
    pl.semaphore_wait(barrier, count)
    seen = set()

    def need(i):
        if i not in seen:
            seen.add(i)
            w_wait(i)

    sends = []

    def go(cp):
        cp.start()
        sends.append(cp)

    local = {}
    if job.gather:
        for c in range(chunks):
            own = src_ref.at[pl.ds(c * mc, mc)]
            for s in range(1, tp):
                go(remote(own, piece(s, c, 0), t_send.at[s, c], t_recv.at[s, c], peer(-s)))
            local[c] = pltpu.make_async_copy(own, piece(0, c, 0), loc_sem.at[c])
            local[c].start()
            go(remote(own, piece(0, c, 1), r_send.at[0, c], r_recv.at[0, c], row_dev))

    if job.pieces:
        for i in range(job.weights):
            w_start(i)
    if job.spread:
        rows_q = quarter_ref.shape[0]
        mine = spread_ref.at[pl.ds(pl.multiple_of(d * rows_q, rows_q), rows_q)]
        q_local = pltpu.make_async_copy(quarter_ref, mine, q_send.at[0])
        q_local.start()
        for k in range(1, n_dp):
            go(remote(quarter_ref, mine, q_send.at[k], q_recv.at[k], (lax.rem(d + k, n_dp), r, g, t)))

    relayed = set()

    def relay(s, c):
        if job.gather and s > 0 and (s, c) not in relayed:
            relayed.add((s, c))
            remote(piece(s, c, 0), piece(s, c, 0), t_send.at[s, c], t_recv.at[s, c], peer(-s)).wait_recv()
            go(remote(piece(s, c, 0), piece(s, c, 1), r_send.at[s, c], r_recv.at[s, c], row_dev))

    def tile_load(i):
        s, c = order[i]
        at = pl.ds((s if job.merge else s * chunks + c) * rows, rows)
        return pltpu.make_async_copy(full_ref.at[at], tile_ref.at[i % 2], tile_sem.at[i % 2])

    def ti_loads(i):
        s, c = order[i]
        at = pl.ds((s if job.merge else s * chunks + c) * rows, rows)
        return [pltpu.make_async_copy(ti_hbm[j].at[at], ti_ref[j], ti_sem.at[j]) for j in range(job.tile_ins)]

    def out_copies(i):
        s, c = order[i]
        at = pl.ds((s if job.merge else s * chunks + c) * rows, rows)
        slot = i % job.slots
        return [
            pltpu.make_async_copy(out_ref[j].at[slot], out_hbm[j].at[at], out_sem.at[j, slot])
            for j in range(job.outs)
        ]

    def combine(i):
        s, c = order[i]
        k = s * chunks + c
        cp = remote(
            y_ref.at[i % job.sums, pl.ds(mc, mc)], rbuf.at[k], y_send.at[s, c], y_recv.at[s, c], row_dev
        )
        cp.wait()
        step = min(64, mc)

        def add(b, carry):
            at = pl.ds(pl.multiple_of(b * step, step), step)
            summed = y_ref[i % job.sums, at, :].astype(f32) + rbuf[k, at, :].astype(f32)
            if s == 0:
                total_ref[pl.ds(pl.multiple_of(c * mc + b * step, step), step), :] = summed
            else:
                zbuf[k - chunks, at, :] = summed.astype(bf16)
            return carry

        lax.fori_loop(0, mc // step, add, 0)
        if s > 0:
            go(remote(zbuf.at[k - chunks], tbuf.at[k - chunks], z_send.at[s, c], z_recv.at[s, c], peer(s)))

    for cp in ti_loads(0):
        cp.start()
    if not job.gather:
        tile_load(0).start()
    for i, (s, c) in enumerate(order):
        if job.gather:
            held = range(chunks) if job.merge else [c]
            for cc in held:
                relay(s, cc)
                if s == 0:
                    local[cc].wait()
            for cc in held:
                remote(piece(s, cc, 1), piece(s, cc, 1), r_send.at[s, cc], r_recv.at[s, cc], row_dev).wait_recv()
            tile_load(i).start()
        tile_load(i).wait()
        if not job.gather and i + 1 < len(order):
            tile_load(i + 1).start()
        for cp in ti_loads(i):
            cp.wait()
        if i >= job.slots:
            for cp in out_copies(i - job.slots):
                cp.wait()

        def mid(i=i):
            if i + 1 < len(order):
                relay(*order[i + 1])
                for cp in ti_loads(i + 1):
                    cp.start()
            if job.scatter:
                for cp in out_copies(i):
                    cp.start()
                if i >= 1:
                    combine(i - 1)

        outs = [ref.at[i % job.slots] for ref in out_ref]
        y = y_ref.at[i % job.sums] if job.scatter else None
        job.body(tile_ref.at[i % 2], w_ref, need, ti_ref, outs, y, mid)
        if job.scatter:
            k = s * chunks + c
            remote(y.at[pl.ds(mc, mc)], rbuf.at[k], y_send.at[s, c], y_recv.at[s, c], row_dev).start()
        else:
            for cp in out_copies(i):
                cp.start()
    last = len(order)
    for i in range(max(0, last - job.slots), last):
        for cp in out_copies(i):
            cp.wait()
    if job.scatter:
        combine(last - 1)
        for c in range(chunks):
            for s in range(1, tp):
                k = (s - 1) * chunks + c
                remote(zbuf.at[k], tbuf.at[k], z_send.at[s, c], z_recv.at[s, c], peer(s)).wait_recv()
                step = min(64, mc)

                def add(b, carry, k=k, c=c):
                    at = pl.ds(pl.multiple_of(b * step, step), step)
                    to = pl.ds(pl.multiple_of(c * mc + b * step, step), step)
                    total_ref[to, :] = total_ref[to, :] + tbuf[k, at, :].astype(f32)
                    return carry

                lax.fori_loop(0, mc // step, add, 0)
    if job.pieces:
        for i in range(job.weights):
            w_end(i)
    if job.spread:
        q_local.wait()
        for k in range(1, n_dp):
            came = lax.rem(d + n_dp - k, n_dp)
            remote(
                quarter_ref, spread_ref.at[pl.ds(pl.multiple_of(came * rows_q, rows_q), rows_q)],
                q_send.at[k], q_recv.at[k], row_dev,
            ).wait_recv()
    for cp in sends:
        cp.wait_send()


def tile_call(job, ident, name, src, weights, shapes, tile_ins, out_widths, sum_width, flops, quarter=None):
    tp = lax.axis_size("zl")
    n_dp = lax.axis_size("dp")
    flat_weights = [v for group in weights for v in group]
    width = src.shape[1]
    m = src.shape[0] if job.gather else src.shape[0] // (2 * tp)
    chunks = 2 if tp == 2 else 1
    mc = m // chunks
    rows = 2 * (m if job.merge else mc)
    total_rows = 2 * tp * m
    anywhere = pl.BlockSpec(memory_space=pl.ANY)
    dma = pltpu.SemaphoreType.DMA
    out_specs, out_shape = [], []
    if job.gather:
        out_specs.append(anywhere)
        out_shape.append(jax.ShapeDtypeStruct((total_rows, width), bf16))
    for w in out_widths:
        out_specs.append(anywhere)
        out_shape.append(jax.ShapeDtypeStruct((total_rows, w), bf16))
    if job.pieces:
        out_specs.extend([anywhere] * len(shapes))
        out_shape.extend(jax.ShapeDtypeStruct(shape, bf16) for shape in shapes)
    if job.spread:
        out_specs.append(anywhere)
        out_shape.append(jax.ShapeDtypeStruct((n_dp * quarter.shape[0], quarter.shape[1]), bf16))
    if job.scatter:
        out_specs.append(pl.BlockSpec(memory_space=pltpu.VMEM))
        out_shape.append(jax.ShapeDtypeStruct((m, sum_width), f32))
    scratch = [pltpu.VMEM(shape, bf16) for shape in shapes]
    scratch.append(pltpu.VMEM((2, rows, width), bf16))
    scratch.extend(pltpu.VMEM((rows, v.shape[1]), bf16) for v in tile_ins)
    scratch.extend(pltpu.VMEM((job.slots, rows, w), bf16) for w in out_widths)
    if job.scatter:
        scratch.append(pltpu.VMEM((job.sums, rows, sum_width), bf16))
        scratch.append(pltpu.VMEM((tp * chunks, mc, sum_width), bf16))
        scratch.append(pltpu.VMEM(((tp - 1) * chunks, mc, sum_width), bf16))
        scratch.append(pltpu.VMEM(((tp - 1) * chunks, mc, sum_width), bf16))
    scratch.extend(
        [dma((len(weights),)), dma((2,)), dma((max(1, len(tile_ins)),)), dma((max(1, job.outs), job.slots)), dma((chunks,))]
    )
    scratch.extend(dma((tp, chunks)) for _ in range(8))
    scratch.extend(dma((len(weights), 8)) for _ in range(3))
    scratch.extend(dma((n_dp,)) for _ in range(2))
    extra = [quarter] if job.spread else []
    return pl.pallas_call(
        functools.partial(tile_kernel, job, tp, chunks),
        in_specs=[anywhere] * (1 + len(flat_weights) + len(tile_ins) + len(extra)),
        out_specs=out_specs,
        out_shape=out_shape,
        scratch_shapes=scratch,
        compiler_params=pltpu.CompilerParams(
            collective_id=ident, has_side_effects=True, vmem_limit_bytes=60 << 20
        ),
        cost_estimate=pl.CostEstimate(flops=flops, bytes_accessed=8 * total_rows * width, transcendentals=0),
        name=name,
    )(src, *flat_weights, *tile_ins, *extra)


def columns(n, size):
    return pl.ds(pl.multiple_of(n * size, size), size)


def loop(first, last, step):
    def body(n, carry):
        step(n)
        return carry

    lax.fori_loop(first, last, body, 0)


def gate_up_body(tile, w, need, ti, outs, y, mid):
    hidden_width = w[0].shape[1]
    nb = min(512, hidden_width)
    count = hidden_width // nb
    need(0)
    need(1)

    def step(n):
        cols = columns(n, nb)
        rows = tile[...]
        gate = jnp.dot(rows, w[0][:, cols], preferred_element_type=f32)
        up = jnp.dot(rows, w[1][:, cols], preferred_element_type=f32)
        outs[0][:, cols] = gate.astype(bf16)
        outs[1][:, cols] = up.astype(bf16)
        outs[2][:, cols] = (gate * jax.nn.sigmoid(gate) * up).astype(bf16)

    loop(0, count // 2, step)
    mid()
    loop(count // 2, count, step)


def down_body(tile, w, need, ti, outs, y, mid):
    nb = min(1024, w[0].shape[1])
    count = w[0].shape[1] // nb
    need(0)

    def step(n):
        cols = columns(n, nb)
        y[:, cols] = jnp.dot(tile[...], w[0][:, cols], preferred_element_type=f32).astype(bf16)

    loop(0, count // 2, step)
    mid()
    loop(count // 2, count, step)


def back_body(tile, w, need, ti, outs, y, mid):
    hidden_width = w[0].shape[0]
    nb = min(512, hidden_width)
    need(0)

    def first(n):
        cols = columns(n, nb)
        grad = lax.dot_general(tile[...], w[0][cols, :], NT, preferred_element_type=f32)
        grad = grad.astype(bf16).astype(f32)
        gate = ti[0][:, cols].astype(f32)
        up = ti[1][:, cols].astype(f32)
        sig = jax.nn.sigmoid(gate)
        passed = grad * sig
        outs[0][:, cols] = (passed * up * (1.0 + gate * (1.0 - sig))).astype(bf16)
        outs[1][:, cols] = (passed * gate).astype(bf16)

    loop(0, hidden_width // nb, first)
    mid()
    need(1)
    need(2)
    nd = 512

    def second(n):
        cols = columns(n, nd)
        grad = lax.dot_general(outs[0][...], w[1][cols, :], NT, preferred_element_type=f32)
        grad = grad + lax.dot_general(outs[1][...], w[2][cols, :], NT, preferred_element_type=f32)
        y[:, cols] = grad.astype(bf16)

    loop(0, w[1].shape[0] // nd, second)


gate_up_job = Job(True, False, False, 2, 7, 0, True, 0, 3, 2, 0, gate_up_body)
down_job = Job(False, True, False, 1, 2, 1, False, 0, 0, 1, 2, down_body)
back_job = Job(True, True, False, 3, 0, 0, False, 2, 2, 1, 1, back_body)


def last_kernel(
    chunks, dx_ref, down_ref, qkv_ref, up_ref, out_ref, down_out, qkv_out, up_out,
    own, from_row, near, from_t, give, from_zh,
    down_own, down_in, down_sum, down_late, qkv_own, qkv_in, qkv_sum, qkv_late, up_stay, up_late,
    own_sem, row_send, row_recv, t_send, t_recv, zh_send, zh_recv,
    g_sem, d_send, d_recv, f_local, f_send, f_recv,
):
    n_dp = lax.axis_size("dp")
    tp = lax.axis_size("zl")
    d, r, g, t = (lax.axis_index(name) for name in ("dp", "row", "zh", "zl"))
    same = r == g
    other_core = jnp.logical_not(same)
    seq_len, width = dx_ref.shape
    half = width // 2
    feat = half // (2 * tp)
    step = seq_len // chunks

    def remote(src, dst, send, recv, dev):
        return pltpu.make_async_remote_copy(
            src_ref=src, dst_ref=dst, send_sem=send, recv_sem=recv, device_id=dev,
            device_id_type=pl.DeviceIdType.MESH,
        )

    row_dev = (d, 1 - r, g, t)
    zh_dev = (d, r, 1 - g, t)
    cross_dev = (d, 1 - r, 1 - g, t)

    def dp_dev(k):
        return (lax.rem(d + k, n_dp), r, g, t)

    def t_dev(s):
        return (d, r, g, lax.rem(t + s, tp))

    partners = [row_dev, zh_dev, cross_dev]
    partners += [dp_dev(k) for k in range(1, n_dp)] + [t_dev(s) for s in range(1, tp)]
    barrier = pltpu.get_barrier_semaphore()
    for dev in partners:
        pl.semaphore_signal(barrier, inc=1, device_id=dev, device_id_type=pl.DeviceIdType.MESH)
    pl.semaphore_wait(barrier, len(partners))

    def owner_copies(i, pieces, late):
        return (
            remote(pieces.at[1 - r], late.at[0], f_send.at[i, 0], f_recv.at[i, 0], row_dev),
            remote(pieces.at[r], late.at[0], f_send.at[i, 1], f_recv.at[i, 1], zh_dev),
            remote(pieces.at[1 - r], late.at[1], f_send.at[i, 2], f_recv.at[i, 2], cross_dev),
        )

    def owner_start(i, pieces, late):
        @pl.when(same)
        def _():
            owner_copies(i, pieces, late)[0].start()

        @pl.when(other_core)
        def _():
            owner_copies(i, pieces, late)[1].start()
            owner_copies(i, pieces, late)[2].start()

    def owner_end(i, pieces, late, kept, total):
        @pl.when(same)
        def _():
            owner_copies(i, pieces, late)[1].wait_recv()
            total[...] = kept[...].astype(f32) + late[0].astype(f32)
            owner_copies(i, pieces, late)[0].wait_send()

        @pl.when(other_core)
        def _():
            owner_copies(i, pieces, late)[0].wait_recv()
            owner_copies(i, pieces, late)[2].wait_recv()
            total[...] = late[0].astype(f32) + late[1].astype(f32)
            owner_copies(i, pieces, late)[1].wait_send()
            owner_copies(i, pieces, late)[2].wait_send()

    up_local = pltpu.make_async_copy(up_ref.at[r], up_stay, f_local)
    up_local.start()
    owner_start(2, up_ref, up_late)

    def down_piece(which, group):
        rows, cols = down_own.shape[1:]
        return down_ref.at[
            pl.ds(pl.multiple_of(group * rows, rows), rows), pl.ds(pl.multiple_of(which * cols, cols), cols)
        ]

    def qkv_piece(which, group):
        rows = qkv_own.shape[1]
        return qkv_ref.at[pl.ds(pl.multiple_of((which * n_dp + group) * rows, rows), rows)]

    def group_copies(i, piece, mine, inbox):
        loads = [pltpu.make_async_copy(piece(which, d), mine.at[which], g_sem.at[i, which]) for which in range(2)]
        sends = [
            remote(
                piece(which, lax.rem(d + k, n_dp)), inbox.at[k - 1, which],
                d_send.at[i, k, which], d_recv.at[i, k, which], dp_dev(k),
            )
            for which in range(2)
            for k in range(1, n_dp)
        ]
        return loads, sends

    down_copies = group_copies(0, down_piece, down_own, down_in)
    qkv_copies = group_copies(1, qkv_piece, qkv_own, qkv_in)

    def cols_at(which):
        return pl.ds(pl.multiple_of(which * half, half), half)

    rows_copies, own_copies = [], []
    for c in range(chunks):
        rows = pl.ds(c * step, step)
        cp = remote(dx_ref.at[rows, cols_at(1 - r)], from_row.at[c], row_send.at[c], row_recv.at[c], row_dev)
        cp.start()
        rows_copies.append(cp)
        cp = pltpu.make_async_copy(dx_ref.at[rows, cols_at(r)], own.at[c], own_sem.at[c])
        cp.start()
        own_copies.append(cp)
    for loads, sends in (down_copies, qkv_copies):
        for cp in loads + sends:
            cp.start()

    t_copies = {}

    def row_stage(c):
        own_copies[c].wait()
        rows_copies[c].wait_recv()
        total = own[c].astype(f32) + from_row[c].astype(f32)
        for b in range(2 * tp):
            near[c, b] = total[:, b * feat : (b + 1) * feat].astype(bf16)
        for zh in range(2):
            for s in range(1, tp):
                cp = remote(
                    near.at[c, zh * tp + lax.rem(t + s, tp)], from_t.at[c, zh, s - 1],
                    t_send.at[c, zh, s], t_recv.at[c, zh, s], t_dev(s),
                )
                cp.start()
                t_copies[(c, zh, s)] = cp

    zh_copies = []

    def t_stage(c):
        for zh in range(2):
            for s in range(1, tp):
                t_copies[(c, zh, s)].wait_recv()

        def total_of(zh):
            total = near[c, zh * tp + t].astype(f32)
            for s in range(1, tp):
                total = total + from_t[c, zh, s - 1].astype(f32)
            return total

        give[c] = total_of(1 - g).astype(bf16)
        cp = remote(give.at[c], from_zh.at[c], zh_send.at[c], zh_recv.at[c], zh_dev)
        cp.start()
        zh_copies.append(cp)
        out_ref[pl.ds(pl.multiple_of(g * seq_len + c * step, step), step), :] = total_of(g)

    def group_stage(copies, mine, inbox, total_ref):
        for cp in copies[0]:
            cp.wait()
        for cp in copies[1]:
            cp.wait_recv()
        part = mine.shape[1]
        block = min(64, part)
        for which in range(2):

            def add(i, carry, which=which):
                at = pl.ds(pl.multiple_of(i * block, block), block)
                total = mine[which, at, :].astype(f32)
                for k in range(n_dp - 1):
                    total = total + inbox[k, which, at, :].astype(f32)
                total_ref[which, at, :] = total.astype(bf16)
                return carry

            lax.fori_loop(0, part // block, add, 0)

    for c in range(chunks):
        row_stage(c)
        if c >= 1:
            t_stage(c - 1)
    t_stage(chunks - 1)
    group_stage(down_copies, down_own, down_in, down_sum)
    owner_start(0, down_sum, down_late)
    group_stage(qkv_copies, qkv_own, qkv_in, qkv_sum)
    owner_start(1, qkv_sum, qkv_late)
    for c in range(chunks):
        zh_copies[c].wait_recv()
        out_ref[pl.ds(pl.multiple_of((1 - g) * seq_len + c * step, step), step), :] = from_zh[c].astype(f32)
    up_local.wait()
    owner_end(2, up_ref, up_late, up_stay, up_out)
    owner_end(0, down_sum, down_late, down_sum.at[r], down_out)
    owner_end(1, qkv_sum, qkv_late, qkv_sum.at[r], qkv_out)
    for cp in rows_copies + down_copies[1] + qkv_copies[1] + list(t_copies.values()) + zh_copies:
        cp.wait_send()


def last_sums(dx, down, qkv, up):
    n_dp = lax.axis_size("dp")
    tp = lax.axis_size("zl")
    seq_len, width = dx.shape
    chunks = 4
    half = width // 2
    feat = half // (2 * tp)
    step = seq_len // chunks
    anywhere = pl.BlockSpec(memory_space=pl.ANY)
    vmem = pl.BlockSpec(memory_space=pltpu.VMEM)
    dma = pltpu.SemaphoreType.DMA
    down_shape = (down.shape[0] // n_dp, down.shape[1] // 2)
    qkv_shape = (qkv.shape[0] // (2 * n_dp), qkv.shape[1])
    sums = []
    for shape in (down_shape, qkv_shape):
        sums += [
            pltpu.VMEM((2, *shape), bf16),
            pltpu.VMEM((n_dp - 1, 2, *shape), bf16),
            pltpu.VMEM((2, *shape), bf16),
            pltpu.VMEM((2, *shape), bf16),
        ]
    return pl.pallas_call(
        functools.partial(last_kernel, chunks),
        in_specs=[anywhere] * 4,
        out_specs=[vmem] * 4,
        out_shape=[
            jax.ShapeDtypeStruct((2 * seq_len, feat), f32),
            jax.ShapeDtypeStruct(down_shape, f32),
            jax.ShapeDtypeStruct(qkv_shape, f32),
            jax.ShapeDtypeStruct(up.shape[1:], f32),
        ],
        scratch_shapes=[
            pltpu.VMEM((chunks, step, half), bf16),
            pltpu.VMEM((chunks, step, half), bf16),
            pltpu.VMEM((chunks, 2 * tp, step, feat), bf16),
            pltpu.VMEM((chunks, 2, tp - 1, step, feat), bf16),
            pltpu.VMEM((chunks, step, feat), bf16),
            pltpu.VMEM((chunks, step, feat), bf16),
            *sums,
            pltpu.VMEM(up.shape[1:], bf16),
            pltpu.VMEM(up.shape, bf16),
            dma((chunks,)),
            dma((chunks,)),
            dma((chunks,)),
            dma((chunks, 2, tp)),
            dma((chunks, 2, tp)),
            dma((chunks,)),
            dma((chunks,)),
            dma((2, 2)),
            dma((2, n_dp, 2)),
            dma((2, n_dp, 2)),
            dma(()),
            dma((3, 3)),
            dma((3, 3)),
        ],
        compiler_params=pltpu.CompilerParams(collective_id=4, has_side_effects=True, vmem_limit_bytes=60 << 20),
        cost_estimate=pl.CostEstimate(flops=0, bytes_accessed=8 * seq_len * width, transcendentals=0),
        name="last_sums",
    )(dx, down, qkv, up)


def rotary(seq_len):
    half_width = HD // 2
    freqs = rope_base ** (-(jnp.arange(half_width, dtype=f32) * 2.0) / HD)
    angles = jnp.arange(seq_len, dtype=f32)[:, None] * freqs[None, :]
    cos_table, sin_table = jnp.cos(angles), jnp.sin(angles)
    return (
        jnp.concatenate([cos_table, cos_table], axis=1),
        jnp.concatenate([-sin_table, sin_table], axis=1),
    )


def norm_scale(vals):
    return lax.rsqrt(jnp.mean(vals * vals, axis=1, keepdims=True) + norm_eps)


def norm_back(pre_vals, scale, gains, gradient):
    weighted = gradient * gains
    inner = jnp.mean(weighted * pre_vals, axis=1, keepdims=True)
    grad_pre = scale * weighted - pre_vals * (scale * scale * scale * inner)
    grad_gain = jnp.sum(gradient * pre_vals * scale, axis=0)
    return grad_pre, grad_gain


def adamw_step(weight, gradient, first_mom, second_mom, step_rate, decay_rate):
    first_new = beta_one * first_mom + (1.0 - beta_one) * gradient
    second_new = beta_two * second_mom + (1.0 - beta_two) * gradient * gradient
    fix_one = 1.0 - beta_one**STEP
    fix_two = 1.0 - beta_two**STEP
    direction = first_new / fix_one / (jnp.sqrt(second_new / fix_two) + adam_eps)
    return (first_new, second_new, weight - step_rate * (direction + decay_rate * weight))


def matmul(left, right, dims=NN):
    return lax.dot_general(left, right, dims, preferred_element_type=f32)


def shards(
    tokens, cotangent, doc_lengths, qkv_weight, out_weight, gate_weight, up_weight, down_weight,
    head_gains, post_gains, qkv_first, qkv_second, out_first, out_second, gate_first, gate_second,
    up_first, up_second, down_first, down_second, head_first, head_second, post_first, post_second,
):
    n_dp = lax.axis_size("dp")
    tp = lax.axis_size("zl")
    group = 2 * tp
    n_col = 2 * tp
    d, r, g, t = (lax.axis_index(name) for name in ("dp", "row", "zh", "zl"))
    same = r == g
    block_at = r * tp + t
    rows_dev, feat = tokens.shape
    width = feat * 2 * n_col
    seq_len = rows_dev // 2
    mine = seq_len // group
    col_width = qkv_weight.shape[2]

    qkv_low = jnp.concatenate([qkv_weight[:, i, :].astype(bf16) for i in range(3)], axis=1)
    docs = doc_lengths.shape[1]
    small = [post_gains.T.reshape(-1), head_gains.reshape(-1), doc_lengths[0].astype(f32)]
    small = jnp.concatenate(small)
    pad = -small.shape[0] % 1024
    small = jnp.concatenate([small, jnp.zeros((pad,), f32)]).reshape(-1, 128)

    def quarter_of(weight):
        rows = weight.shape[0] // n_dp
        return lax.dynamic_slice_in_dim(weight, d * rows, rows, 0).astype(bf16)

    x_full, qkv_full, small_all, gate_quarter = first_gather(tokens, qkv_low, small, quarter_of(gate_weight))
    small_all = small_all.reshape(2 * n_col, -1)
    cut_one, cut_two = 2 * feat, 2 * feat + 2 * col_width
    post_all = small_all[:, :cut_one].reshape(2 * n_col, 2, feat).transpose(1, 0, 2).reshape(2, width)
    gains = lax.dynamic_slice_in_dim(small_all, block_at, 1, 0)[0, cut_one:cut_two].reshape(2, col_width)
    lengths = lax.dynamic_slice_in_dim(small_all, g * n_col, 1, 0)[0, cut_two : cut_two + docs]
    ends = jnp.cumsum(lengths.astype(jnp.int32))
    x_tok = lax.dynamic_slice_in_dim(x_full, block_at * mine, mine, 0)

    def halves(quarter):
        cut = quarter.shape[1] // 2
        return quarter[:, :cut], quarter[:, cut:]

    def gathered(one, two, one_x, two_y):
        one_y = swap_bit(jnp.concatenate([one, one_x]), "dp", 2)
        two_x = swap_bit(jnp.concatenate([two, two_y]), "dp", 1)
        return [one, two, one_x, one_y, two_y, two_x]

    gate_one, gate_two = halves(gate_quarter)
    up_one, up_two = halves(quarter_of(up_weight))
    up_one, up_two, post_all = tie(up_one, up_two, post_all)
    up_one, up_two = swap(up_one, "zh"), swap(up_two, "zh")
    gate_one_x, gate_two_y = swap_bit(gate_one, "dp", 1), swap_bit(gate_two, "dp", 2)

    out_rows = out_weight.shape[0] // n_dp
    out_part = lax.dynamic_slice_in_dim(out_weight, d * out_rows, out_rows, 0).astype(bf16)
    out_part, post_all = tie(lax.all_gather(out_part, ("zh", "zl"), axis=0), post_all)
    out_part = lax.all_gather(out_part, "dp", axis=1)

    cos_two, sin_two = rotary(seq_len)
    qkv = matmul(x_full, qkv_full)
    squares = jnp.stack(
        [
            jnp.sum(jnp.square(qkv[:, :col_width]), axis=1),
            jnp.sum(jnp.square(qkv[:, col_width : 2 * col_width]), axis=1),
        ],
        axis=0,
    )
    inv_scale = lax.rsqrt(small_sum(squares, ("row", "zl")) / width + norm_eps).T
    down_quarter = swap(quarter_of(down_weight), "zh")
    inv_scale, gate_one_x, gate_two_y = tie(inv_scale, gate_one_x, gate_two_y)
    query, key, key_t, value, value_t = prepare(qkv, inv_scale, gains, cos_two, sin_two)
    ends, up_one = tie(ends, up_one)
    out_part, key_t = tie(out_part, key_t)
    out_full = lax.all_gather(out_part.reshape(width, width // 2), "row", axis=1, tiled=True)
    att, log_total = attend(query, key, value_t, ends)
    gate_pieces = gathered(gate_one, gate_two, gate_one_x, gate_two_y)
    att, up_two, gate_pieces[3], gate_pieces[5] = tie(att, up_two, gate_pieces[3], gate_pieces[5])
    up_one_x, up_two_y = swap_bit(up_one, "dp", 1), swap_bit(up_two, "dp", 2)

    def to_tokens(vals):
        got = lax.all_to_all(vals.reshape(group, mine, col_width), ("row", "zl"), 0, 0)
        return got.transpose(1, 0, 2).reshape(mine, width)

    def to_heads(vals):
        sent = vals.reshape(mine, group, col_width).transpose(1, 0, 2)
        return lax.all_to_all(sent, ("row", "zl"), 0, 0).reshape(seq_len, col_width)

    att_tok = to_tokens(att)

    gain_attn, gain_mlp = post_all[0:1], post_all[1:2]
    att_tok, up_one_x, up_two_y = tie(att_tok, up_one_x, up_two_y)
    a_pre = matmul(att_tok, out_full)
    a_scale = norm_scale(a_pre)
    h_tok = x_tok.astype(f32) + a_pre * a_scale * gain_attn

    cot = cotangent.reshape(2, 2, tp, mine, feat).transpose(1, 0, 2, 3, 4).reshape(2 * n_col, mine, feat)
    cot, a_scale = tie(cot, a_scale)
    cot = lax.all_to_all(cot, ("row", "zh", "zl"), 0, 0)
    cot_tok = cot.transpose(1, 0, 2).reshape(mine, width).astype(f32)

    up_pieces = gathered(up_one, up_two, up_one_x, up_two_y)
    gate_low, up_low, down_low = (
        v.astype(bf16) for v in (gate_weight, up_weight, down_weight)
    )
    hidden_width = gate_low.shape[1]
    work = 2 * seq_len * width * hidden_width
    wide, tall = (width, hidden_width), (hidden_width, width)
    h_full, gate_all, up_all, hidden, gate_full, up_full, down_other = tile_call(
        gate_up_job, 1, "gate_up", h_tok.astype(bf16), [[gate_low, *gate_pieces], [up_low, *up_pieces]],
        [wide, wide], [], [hidden_width] * 3, 0, 2 * work, down_quarter,
    )
    down_full, m_pre = tile_call(
        down_job, 2, "down", hidden, [[down_low, down_other]], [tall], [], [], width, work
    )
    m_scale = norm_scale(m_pre)
    mixed_tok = (h_tok + m_pre * m_scale * gain_mlp).astype(bf16)

    def to_features(vals):
        out = lax.all_to_all(
            vals.reshape(mine, 2 * n_col, feat).transpose(1, 0, 2), ("row", "zh", "zl"), 0, 0
        )
        return out.reshape(2, 2, tp, mine, feat).transpose(1, 0, 2, 3, 4).reshape(rows_dev, feat)

    mixed = to_features(mixed_tok)

    grad_m, grad_gain_mlp = norm_back(m_pre, m_scale, gain_mlp, cot_tok)
    dm_full, grad_gate, grad_up, dh_sum = tile_call(
        back_job, 3, "feed_back", grad_m.astype(bf16), [[down_full], [gate_full], [up_full]], [tall, wide, wide],
        [gate_all, up_all], [hidden_width] * 2, width, 3 * work,
    )
    dh_tok = cot_tok + dh_sum

    grad_a, grad_gain_attn = norm_back(a_pre, a_scale, gain_attn, dh_tok)
    grad_a = grad_a.astype(bf16)
    datt = matmul(grad_a, out_full, NT).astype(bf16)
    datt, hidden, h_full = tie(datt, hidden, h_full)
    grad_att = to_heads(datt)
    grad_gate_w = matmul(h_full, grad_gate, TN).astype(bf16)
    grad_up_w = matmul(h_full, grad_up, TN).astype(bf16)
    grad_att, grad_gate_w, grad_up_w = tie(grad_att, grad_gate_w, grad_up_w)
    grad_down_w = matmul(hidden, dm_full, TN).astype(bf16)
    grad_out = matmul(att_tok, grad_a, TN).astype(bf16)

    dqt, dk, dv = attend_back(query, key, key_t, value, grad_att, att, log_total, ends)
    weighted, inner, grad_head = unturn(dqt, dk, qkv, inv_scale, gains, cos_two, sin_two)
    def data_sums(grad):
        half = grad.shape[0] // 2
        return [
            lax.psum_scatter(grad[i * half : (i + 1) * half], "dp", scatter_dimension=0, tiled=True)
            for i in range(2)
        ]

    def owner_parts(pieces):
        keep = jnp.where(r == 0, pieces[0], pieces[1])
        give = jnp.where(r == 0, pieces[1], pieces[0])
        axes = ("row", "zh")
        return [
            keep,
            lax.ppermute(keep, axes, [(1, 0), (2, 3)]),
            lax.ppermute(give, axes, [(1, 2), (2, 1)]),
            lax.ppermute(give, axes, [(0, 2), (3, 1)]),
        ]

    gate_parts = owner_parts(data_sums(grad_gate_w))
    up_sums = data_sums(grad_up_w)
    inner = (small_sum(inner.T, ("row", "zl")) / width).T
    cube = inv_scale * inv_scale * inv_scale * inner
    dqkv = jnp.concatenate(
        [
            (inv_scale[:, 0:1] * weighted[:, :col_width] - qkv[:, :col_width] * cube[:, 0:1]).astype(bf16),
            (inv_scale[:, 1:2] * weighted[:, col_width:] - qkv[:, col_width : 2 * col_width] * cube[:, 1:2]).astype(bf16),
            dv,
        ],
        axis=1,
    )
    grad_qkv = matmul(x_full, dqkv, TN).astype(bf16)

    qkv_full, *gate_parts = tie(qkv_full, *gate_parts)
    sum_gate = jnp.where(same, gate_parts[0].astype(f32), 0.0)
    for part in gate_parts[1:]:
        sum_gate = sum_gate + part.astype(f32)
    dx = matmul(dqkv, qkv_full, NT).astype(bf16)
    here = lax.dynamic_slice_in_dim(dx, block_at * mine, mine, 0).astype(f32) + dh_tok
    dx = lax.dynamic_update_slice_in_dim(dx, here.astype(bf16), block_at * mine, 0)
    dtokens, sum_down, sum_qkv, sum_up = last_sums(dx, grad_down_w, grad_qkv, jnp.stack(up_sums))
    sum_qkv = sum_qkv.reshape(qkv_first.shape)

    half_w = width // 2
    half = lax.dynamic_slice_in_dim(grad_out, r * half_w, half_w, 1).astype(f32) + swap(
        lax.dynamic_slice_in_dim(grad_out, (1 - r) * half_w, half_w, 1), "row"
    ).astype(f32)
    half = half.astype(bf16).reshape(n_col, n_dp, out_rows, width // 2)
    half = lax.psum_scatter(half, "dp", scatter_dimension=1, tiled=False)
    sum_out = lax.psum_scatter(half, ("zh", "zl"), scatter_dimension=0, tiled=False).astype(f32)

    head_place = lax.dynamic_update_slice_in_dim(
        jnp.zeros((2, width), f32), grad_head, block_at * col_width, 1
    )
    small = jnp.concatenate([head_place, grad_gain_attn[None], grad_gain_mlp[None]], axis=0)
    small, sum_down = tie(small, sum_down)
    small = small_sum(small, ("dp", "row", "zh", "zl"))
    col_at = g * tp + t
    sum_head = lax.dynamic_slice_in_dim(small[:2], col_at * col_width, col_width, 1)
    post_rows = post_first.shape[0]
    sum_post = lax.dynamic_slice_in_dim(
        small[2:], ((r * n_col + col_at) * n_dp + d) * post_rows, post_rows, 1
    ).T

    def owned_rows(weight, part_rows):
        return lax.dynamic_slice_in_dim(weight, d * part_rows, part_rows, 0)

    results = []
    for weight, total, first, second in (
        (qkv_weight, sum_qkv, qkv_first, qkv_second),
        (out_weight, sum_out, out_first, out_second),
        (gate_weight, sum_gate, gate_first, gate_second),
        (up_weight, sum_up, up_first, up_second),
        (down_weight, sum_down, down_first, down_second),
    ):
        results.extend(
            adamw_step(owned_rows(weight, total.shape[0]), total, first, second, rate_matrix, weight_decay)
        )
    results.extend(adamw_step(head_gains, sum_head, head_first, head_second, rate_gain, 0.0))
    results.extend(
        adamw_step(owned_rows(post_gains, post_rows), sum_post, post_first, post_second, rate_gain, 0.0)
    )
    return (mixed, dtokens, *results)


def solution(mesh):
    n_dp, n_row, n_col = (mesh.shape[name] for name in ("dp", "row", "col"))
    grid = Mesh(mesh.devices.reshape(n_dp, n_row, 2, n_col // 2), ("dp", "row", "zh", "zl"))
    col = ("zh", "zl")
    moved = P("dp", ("row", *col))
    qkv_part = P(("row", "dp"), None, col)
    flat_part = P((*col, "dp"), "row")
    wide_part = P(("row", "dp"), col)
    head_part = P(None, col)
    post_part = P(("row", *col, "dp"), None)
    in_specs = (
        moved,
        moved,
        P(("dp", "row"), None),
        P("row", None, col),
        P(col, "row"),
        P("row", col),
        P("row", col),
        P(col, "row"),
        head_part,
        P(("row", *col), None),
        *[spec for spec in (qkv_part, flat_part, wide_part, wide_part, flat_part, head_part, post_part) for _ in range(2)],
    )
    out_specs = (
        moved,
        moved,
        *[spec for spec in (qkv_part, flat_part, wide_part, wide_part, flat_part, head_part, post_part) for _ in range(3)],
    )
    return jax.shard_map(shards, mesh=grid, in_specs=in_specs, out_specs=out_specs, check_vma=False)
```

```python
import functools

import jax
import jax.numpy as jnp
from jax import lax
from jax.experimental import pallas as pl
from jax.experimental.pallas import tpu as pltpu
from jax.sharding import Mesh
from jax.sharding import PartitionSpec as P

HD = 128
STEP = 10

norm_eps = 1e-06
rope_base = 500000.0
beta_one = 0.9
beta_two = 0.95
adam_eps = 1e-08
weight_decay = 0.1
rate_matrix = 0.02
rate_gain = 0.6
big_negative = -1e30
log2_e = 1.4426950408889634

f32 = jnp.float32
bf16 = jnp.bfloat16
NN = (((1,), (0,)), ((), ()))
NT = (((1,), (1,)), ((), ()))
TN = (((0,), (0,)), ((), ()))


def swap(piece, axis):
    return lax.ppermute(piece, axis, [(0, 1), (1, 0)])


def shift(piece, axis, step):
    size = lax.axis_size(axis)
    return lax.ppermute(piece, axis, [(i, (i + step) % size) for i in range(size)])


def swap_bit(piece, axis, bit):
    return lax.ppermute(piece, axis, [(i, i ^ bit) for i in range(lax.axis_size(axis))])


def small_sum(vals, axes):
    for axis in axes:
        bit = 1
        while bit < lax.axis_size(axis):
            vals = vals + swap_bit(vals, axis, bit)
            bit *= 2
    return vals


def tie(*vals):
    return lax.optimization_barrier(vals)


def small_sum(vals, axes):
    for axis in axes:
        bit = 1
        while bit < lax.axis_size(axis):
            vals = vals + swap_bit(vals, axis, bit)
            bit *= 2
    return vals


def gather_kernel(
    chunks, tok_ref, low_ref, post_ref, next_ref, x_ref, w_ref, all_ref, ex_ref, got_ref,
    own_sem, zh_send, zh_recv, t_send, t_recv, r_send, r_recv,
    wz_send, wz_recv, wd_send, wd_recv, wr_send, wr_recv, wl_sem, p_send, p_recv, n_send, n_recv,
):
    n_dp = lax.axis_size("dp")
    tp = lax.axis_size("zl")
    d, r, g, t = (lax.axis_index(name) for name in ("dp", "row", "zh", "zl"))
    same = r == g
    feat = tok_ref.shape[1]
    seq_len = tok_ref.shape[0] // 2
    step = seq_len // chunks
    half = low_ref.shape[0]
    rows = half // n_dp

    def place(row, zh, zl):
        return (row * 2 + zh) * tp + zl

    def land(block, c):
        return x_ref.at[block, pl.ds(c * step, step)]

    def remote(src, dst, send, recv, dev):
        return pltpu.make_async_remote_copy(
            src_ref=src, dst_ref=dst, send_sem=send, recv_sem=recv, device_id=dev,
            device_id_type=pl.DeviceIdType.MESH,
        )

    barrier = pltpu.get_barrier_semaphore()
    count = 0
    for dd in range(n_dp):
        for rr in range(2):
            if dd or rr:
                dev = (lax.rem(d + dd, n_dp), lax.rem(r + rr, 2), g, t)
                pl.semaphore_signal(barrier, inc=1, device_id=dev, device_id_type=pl.DeviceIdType.MESH)
                count += 1
    for rr in range(2):
        for gg in range(2):
            for tt in range(tp):
                if gg or tt:
                    dev = (d, lax.rem(r + rr, 2), lax.rem(g + gg, 2), lax.rem(t + tt, tp))
                    pl.semaphore_signal(barrier, inc=1, device_id=dev, device_id_type=pl.DeviceIdType.MESH)
                    count += 1
    pl.semaphore_wait(barrier, count)

    row_dev = (d, 1 - r, g, t)
    zh_dev = (d, r, 1 - g, t)
    mine = place(r, g, t)
    pending = []

    wz = remote(low_ref.at[pl.ds(pl.multiple_of(d * rows, rows), rows)], ex_ref, wz_send, wz_recv, zh_dev)
    wz.start()

    def own_src(c):
        return tok_ref.at[pl.ds(pl.multiple_of(g * seq_len + c * step, step), step)]

    zh_copies = []
    for c in range(chunks):
        src = tok_ref.at[pl.ds(pl.multiple_of((1 - g) * seq_len + c * step, step), step)]
        zh_copies.append(remote(src, land(mine, c), zh_send.at[c], zh_recv.at[c], zh_dev))
        for s in range(1, tp):
            cp = remote(
                own_src(c), land(mine, c), t_send.at[s, 0, c], t_recv.at[s, 0, c], (d, r, g, lax.rem(t + s, tp))
            )
            cp.start()
            pending.append(cp)
    local = []
    for c in range(chunks):
        cp = pltpu.make_async_copy(own_src(c), land(mine, c), own_sem.at[c])
        cp.start()
        local.append(cp)
        cp = remote(own_src(c), land(mine, c), r_send.at[0, 0, c], r_recv.at[0, 0, c], row_dev)
        cp.start()
        pending.append(cp)

    wz.wait_send()
    lead = max(1, chunks // 4)
    for cp in zh_copies[:lead]:
        cp.start()

    half_at = pl.ds(pl.multiple_of(r * half, half), half)
    w_row = remote(low_ref, w_ref.at[half_at], wr_send, wr_recv, row_dev)
    w_loc = pltpu.make_async_copy(low_ref, w_ref.at[half_at], wl_sem.at[0])

    @pl.when(same)
    def _():
        w_loc.start()

    @pl.when(jnp.logical_not(same))
    def _():
        w_row.start()

    posts = []
    n_all = 4 * tp
    p_loc = pltpu.make_async_copy(post_ref, all_ref.at[mine], wl_sem.at[1])
    p_loc.start()
    index = 0
    for rr in range(2):
        for gg in range(2):
            for tt in range(tp):
                if rr or gg or tt:
                    dev = (d, lax.rem(r + rr, 2), lax.rem(g + gg, 2), lax.rem(t + tt, tp))
                    cp = remote(post_ref, all_ref.at[mine], p_send.at[index], p_recv.at[index], dev)
                    cp.start()
                    posts.append(cp)
                    index += 1

    def drain_zh(c):
        zh_copies[c].wait_recv()
        theirs = place(r, 1 - g, t)
        for s in range(1, tp):
            cp = remote(
                land(theirs, c), land(theirs, c), t_send.at[s, 1, c], t_recv.at[s, 1, c],
                (d, r, g, lax.rem(t + s, tp)),
            )
            cp.start()
            pending.append(cp)
        cp = remote(land(theirs, c), land(theirs, c), r_send.at[0, 1, c], r_recv.at[0, 1, c], row_dev)
        cp.start()
        pending.append(cp)

    def drain_t(z, c):
        for s in range(1, tp):
            came = place(r, g if z == 0 else 1 - g, lax.rem(t + tp - s, tp))
            remote(
                land(came, c), land(came, c), t_send.at[s, z, c], t_recv.at[s, z, c],
                (d, r, g, lax.rem(t + s, tp)),
            ).wait_recv()
            cp = remote(land(came, c), land(came, c), r_send.at[s, z, c], r_recv.at[s, z, c], row_dev)
            cp.start()
            pending.append(cp)

    wz.wait_recv()
    spot = pl.ds(pl.multiple_of(r * half + d * rows, rows), rows)
    far = []
    for dd in range(1, n_dp):
        cp = remote(
            ex_ref, w_ref.at[spot], wd_send.at[dd], wd_recv.at[dd, r], (lax.rem(d + dd, n_dp), 1 - g, g, t)
        )
        cp.start()
        far.append(cp)
        for late in zh_copies[lead:][dd - 1 : dd]:
            late.start()
    for late in zh_copies[lead:][n_dp - 1 :]:
        late.start()
    following = remote(next_ref, got_ref, n_send, n_recv, zh_dev)
    following.start()
    near_remote = remote(ex_ref, w_ref.at[spot], wd_send.at[0], wd_recv.at[0, r], row_dev)
    near_local = pltpu.make_async_copy(ex_ref, w_ref.at[spot], wl_sem.at[2])

    @pl.when(same)
    def _():
        near_remote.start()

    @pl.when(jnp.logical_not(same))
    def _():
        near_local.start()

    for c in range(chunks):
        drain_t(0, c)
        drain_zh(c)
        if c >= 1:
            drain_t(1, c - 1)
    drain_t(1, chunks - 1)

    for c in range(chunks):
        for z in range(2):
            for s in range(tp):
                came = place(1 - r, g if z == 0 else 1 - g, lax.rem(t + tp - s, tp))
                remote(
                    land(came, c), land(came, c), r_send.at[s, z, c], r_recv.at[s, z, c], row_dev
                ).wait_recv()
    for cp in local:
        cp.wait()
    for cp in pending:
        cp.wait_send()
    for cp in zh_copies:
        cp.wait_send()
    following.wait()
    p_loc.wait()
    for cp in posts:
        cp.wait_send()
    index = 0
    for rr in range(2):
        for gg in range(2):
            for tt in range(tp):
                if rr or gg or tt:
                    came = place(
                        lax.rem(r + 2 - rr, 2), lax.rem(g + 2 - gg, 2), lax.rem(t + tp - tt, tp)
                    )
                    remote(
                        post_ref, all_ref.at[came], p_send.at[index], p_recv.at[index], row_dev
                    ).wait_recv()
                    index += 1
    for cp in far:
        cp.wait_send()

    @pl.when(same)
    def _():
        w_loc.wait()
        near_remote.wait_send()
        remote(
            low_ref, w_ref.at[pl.ds(pl.multiple_of((1 - r) * half, half), half)], wr_send, wr_recv, row_dev
        ).wait_recv()

    @pl.when(jnp.logical_not(same))
    def _():
        w_row.wait_send()
        near_local.wait()
        for dd in range(n_dp):
            for rr in range(2):
                src_d = lax.rem(d + n_dp - dd, n_dp)
                src_r = r if rr == 0 else 1 - r
                if dd == 0 and rr == 0:
                    continue
                at = pl.ds(pl.multiple_of(src_r * half + src_d * rows, rows), rows)
                remote(ex_ref, w_ref.at[at], wd_send.at[dd], wd_recv.at[dd, src_r], row_dev).wait_recv()


def first_gather(tokens, low, post, following):
    n_dp = lax.axis_size("dp")
    tp = lax.axis_size("zl")
    rows_dev, feat = tokens.shape
    seq_len = rows_dev // 2
    width = feat * 4 * tp
    chunks = 4 if tp == 2 else 1
    anywhere = pl.BlockSpec(memory_space=pl.ANY)
    dma = pltpu.SemaphoreType.DMA
    x_shape = (4 * tp, seq_len, feat)
    x_full, w_full, post_all, _, got = pl.pallas_call(
        functools.partial(gather_kernel, chunks),
        in_specs=[anywhere] * 4,
        out_specs=[anywhere] * 5,
        out_shape=[
            jax.ShapeDtypeStruct(x_shape, bf16),
            jax.ShapeDtypeStruct((2 * low.shape[0], low.shape[1]), bf16),
            jax.ShapeDtypeStruct((4 * tp, *post.shape), f32),
            jax.ShapeDtypeStruct((low.shape[0] // n_dp, low.shape[1]), bf16),
            jax.ShapeDtypeStruct(following.shape, bf16),
        ],
        scratch_shapes=[
            dma((chunks,)),
            dma((chunks,)),
            dma((chunks,)),
            dma((tp, 2, chunks)),
            dma((tp, 2, chunks)),
            dma((tp, 2, chunks)),
            dma((tp, 2, chunks)),
            dma(()),
            dma(()),
            dma((n_dp,)),
            dma((n_dp, 2)),
            dma(()),
            dma(()),
            dma((3,)),
            dma((4 * tp,)),
            dma((4 * tp,)),
            dma(()),
            dma(()),
        ],
        compiler_params=pltpu.CompilerParams(collective_id=0, has_side_effects=True),
        cost_estimate=pl.CostEstimate(flops=0, bytes_accessed=6 * seq_len * width, transcendentals=0),
        name="first_gather",
    )(tokens, low, post, following)
    x_full = x_full.transpose(1, 0, 2).reshape(seq_len, width)
    return x_full, w_full, post_all, got


def doc_start(ends_ref, docs, places):
    start = jnp.zeros_like(places)
    for i in range(docs):
        end = ends_ref[i]
        start = jnp.where(places >= end, end, start)
    return start


def attend_kernel(docs, bk, ends_ref, q_ref, k_ref, vt_ref, o_ref, lse_ref):
    bq = q_ref.shape[0]
    q0 = pl.program_id(1) * bq
    places = q0 + lax.broadcasted_iota(jnp.int32, (1, bq), 1)
    start = doc_start(ends_ref, docs, places)
    lowest = jnp.int32(0)
    for i in range(docs):
        lowest = jnp.where(ends_ref[i] <= q0, ends_ref[i], lowest)
    query = q_ref[...]
    scale = log2_e * HD ** (-0.5)

    def step(j, carry):
        top, total, acc = carry
        k0 = pl.multiple_of(j * bk, bk)
        key = k_ref[pl.ds(k0, bk), :]
        scores = lax.dot_general(key, query, NT, preferred_element_type=f32) * scale
        rows = k0 + lax.broadcasted_iota(jnp.int32, (bk, 1), 0)
        scores = jnp.where((rows <= places) & (rows >= start), scores, big_negative)
        top_new = jnp.maximum(top, jnp.max(scores, axis=0, keepdims=True))
        prob = jnp.exp2(scores - top_new)
        fade = jnp.exp2(top - top_new)
        total = total * fade + jnp.sum(prob, axis=0, keepdims=True)
        acc = acc * fade + lax.dot_general(
            vt_ref[:, pl.ds(k0, bk)], prob.astype(bf16), NN, preferred_element_type=f32
        )
        return top_new, total, acc

    first = (
        jnp.full((1, bq), big_negative, f32),
        jnp.zeros((1, bq), f32),
        jnp.zeros((HD, bq), f32),
    )
    top, total, acc = lax.fori_loop(lowest // bk, (q0 + bq - 1) // bk + 1, step, first)
    o_ref[...] = (acc * (1.0 / total)).T.astype(bf16)
    lse_ref[0] = top + jnp.log2(total)


def attend(query, key, value_t, ends):
    seq_len, width = query.shape
    heads = width // HD
    block = min(512, seq_len)
    docs = ends.shape[0]
    return pl.pallas_call(
        functools.partial(attend_kernel, docs, block),
        grid_spec=pltpu.PrefetchScalarGridSpec(
            num_scalar_prefetch=1,
            grid=(heads, seq_len // block),
            in_specs=[
                pl.BlockSpec((block, HD), lambda h, i, e: (i, h)),
                pl.BlockSpec((seq_len, HD), lambda h, i, e: (0, h)),
                pl.BlockSpec((HD, seq_len), lambda h, i, e: (h, 0)),
            ],
            out_specs=[
                pl.BlockSpec((block, HD), lambda h, i, e: (i, h)),
                pl.BlockSpec((1, 1, block), lambda h, i, e: (h, 0, i)),
            ],
        ),
        out_shape=[
            jax.ShapeDtypeStruct((seq_len, width), bf16),
            jax.ShapeDtypeStruct((heads, 1, seq_len), f32),
        ],
        compiler_params=pltpu.CompilerParams(vmem_limit_bytes=48 << 20),
        cost_estimate=pl.CostEstimate(
            flops=2 * heads * seq_len * seq_len * HD,
            bytes_accessed=8 * seq_len * width,
            transcendentals=heads * seq_len * seq_len // 2,
        ),
        name="attend",
    )(ends, query, key, value_t)


def attend_back_kernel(
    docs, bq, ends_ref, q_ref, k_ref, kt_ref, v_ref, do_ref, o_ref, lse_ref,
    dqt_ref, dk_ref, dv_ref, dk_acc, dv_acc, delta_acc
):
    bk = k_ref.shape[0]
    seq_len = q_ref.shape[0]
    j = pl.program_id(1)
    k0 = j * bk
    scale = HD ** (-0.5)
    last = jnp.int32(seq_len)
    for i in reversed(range(docs)):
        last = jnp.where(ends_ref[i] > k0 + bk - 1, ends_ref[i], last)
    rows = k0 + lax.broadcasted_iota(jnp.int32, (bk, 1), 0)

    @pl.when(j == 0)
    def _():
        dqt_ref[...] = jnp.zeros_like(dqt_ref)
        ones = jnp.ones((8, HD), bf16)
        for i in range(seq_len // bq):
            part = slice(i * bq, (i + 1) * bq)
            prod = do_ref[part, :].astype(f32) * o_ref[part, :].astype(f32)
            high = prod.astype(bf16)
            low = (prod - high.astype(f32)).astype(bf16)
            delta_acc[:, part] = lax.dot_general(
                ones, high, NT, preferred_element_type=f32
            ) + lax.dot_general(ones, low, NT, preferred_element_type=f32)

    dk_acc[...] = jnp.zeros_like(dk_acc)
    dv_acc[...] = jnp.zeros_like(dv_acc)
    key = k_ref[...]
    value = v_ref[...]
    key_t = kt_ref[...]

    def step(i, carry):
        q0 = pl.multiple_of(i * bq, bq)
        cols = pl.ds(q0, bq)
        query = q_ref[cols, :]
        grad = do_ref[cols, :]
        places = q0 + lax.broadcasted_iota(jnp.int32, (1, bq), 1)
        start = doc_start(ends_ref, docs, places)
        scores = lax.dot_general(key, query, NT, preferred_element_type=f32) * (scale * log2_e)
        allowed = (rows <= places) & (rows >= start)
        prob = jnp.where(allowed, jnp.exp2(scores - lse_ref[0, :, cols]), 0.0)
        dv_acc[...] += lax.dot_general(prob.astype(bf16), grad, NN, preferred_element_type=f32)
        grad_prob = lax.dot_general(value, grad, NT, preferred_element_type=f32)
        grad_score = (prob * (grad_prob - delta_acc[0:1, cols])).astype(bf16)
        dk_acc[...] += lax.dot_general(grad_score, query, NN, preferred_element_type=f32)
        dqt_ref[:, cols] += lax.dot_general(key_t, grad_score, NN, preferred_element_type=f32) * scale
        return carry

    lax.fori_loop(k0 // bq, (last + bq - 1) // bq, step, 0)
    dk_ref[...] = dk_acc[...] * scale
    dv_ref[...] = dv_acc[...].astype(bf16)


def attend_back(query, key, key_t, value, grad, att, log_total, ends):
    seq_len, width = query.shape
    heads = width // HD
    block = min(512, seq_len)
    docs = ends.shape[0]
    whole = pl.BlockSpec((seq_len, HD), lambda h, j, e: (0, h))
    part = pl.BlockSpec((block, HD), lambda h, j, e: (j, h))
    line = pl.BlockSpec((1, 1, seq_len), lambda h, j, e: (h, 0, 0))
    return pl.pallas_call(
        functools.partial(attend_back_kernel, docs, block),
        grid_spec=pltpu.PrefetchScalarGridSpec(
            num_scalar_prefetch=1,
            grid=(heads, seq_len // block),
            in_specs=[
                whole,
                part,
                pl.BlockSpec((HD, block), lambda h, j, e: (h, j)),
                part,
                whole,
                whole,
                line,
            ],
            out_specs=[
                pl.BlockSpec((HD, seq_len), lambda h, j, e: (h, 0)),
                part,
                part,
            ],
            scratch_shapes=[
                pltpu.VMEM((block, HD), f32),
                pltpu.VMEM((block, HD), f32),
                pltpu.VMEM((8, seq_len), f32),
            ],
        ),
        out_shape=[
            jax.ShapeDtypeStruct((width, seq_len), f32),
            jax.ShapeDtypeStruct((seq_len, width), f32),
            jax.ShapeDtypeStruct((seq_len, width), bf16),
        ],
        compiler_params=pltpu.CompilerParams(vmem_limit_bytes=48 << 20),
        cost_estimate=pl.CostEstimate(
            flops=5 * heads * seq_len * seq_len * HD,
            bytes_accessed=20 * seq_len * width,
            transcendentals=heads * seq_len * seq_len // 2,
        ),
        name="attend_back",
    )(ends, query, key, key_t, value, grad, att, log_total)


def turn(values, cos_two, sin_two):
    return values * cos_two + pltpu.roll(values, HD // 2, 1) * sin_two


def prepare_kernel(qkv_ref, scale_ref, gains_ref, cos_ref, sin_ref, q_ref, k_ref, kt_ref, v_ref, vt_ref):
    width = q_ref.shape[1]
    cos_two = cos_ref[...]
    sin_two = sin_ref[...]
    for which, out_ref in ((0, q_ref), (1, k_ref)):
        scale = scale_ref[:, which : which + 1]
        for head in range(width // HD):
            cols = slice(head * HD, (head + 1) * HD)
            vals = qkv_ref[:, which * width + head * HD : which * width + (head + 1) * HD]
            out = turn(vals * scale * gains_ref[which : which + 1, cols], cos_two, sin_two)
            out_ref[:, cols] = out.astype(bf16)
            if which == 1:
                kt_ref[cols, :] = out.T.astype(bf16)
    value = qkv_ref[:, 2 * width :]
    v_ref[...] = value.astype(bf16)
    vt_ref[...] = value.T.astype(bf16)


def prepare(qkv, inv_scale, gains, cos_two, sin_two):
    seq_len, triple = qkv.shape
    width = triple // 3
    block = min(256, seq_len)
    flat = pl.BlockSpec((block, width), lambda i: (i, 0))
    tall = pl.BlockSpec((width, block), lambda i: (0, i))
    table = pl.BlockSpec((block, HD), lambda i: (i, 0))
    return pl.pallas_call(
        prepare_kernel,
        grid=(seq_len // block,),
        in_specs=[
            pl.BlockSpec((block, triple), lambda i: (i, 0)),
            pl.BlockSpec((block, 2), lambda i: (i, 0)),
            pl.BlockSpec((2, width), lambda i: (0, 0)),
            table,
            table,
        ],
        out_specs=[flat, flat, tall, flat, tall],
        out_shape=[
            jax.ShapeDtypeStruct((seq_len, width), bf16),
            jax.ShapeDtypeStruct((seq_len, width), bf16),
            jax.ShapeDtypeStruct((width, seq_len), bf16),
            jax.ShapeDtypeStruct((seq_len, width), bf16),
            jax.ShapeDtypeStruct((width, seq_len), bf16),
        ],
        compiler_params=pltpu.CompilerParams(vmem_limit_bytes=48 << 20),
        cost_estimate=pl.CostEstimate(flops=10 * seq_len * triple, bytes_accessed=8 * seq_len * triple, transcendentals=0),
        name="prepare",
    )(qkv, inv_scale, gains, cos_two, sin_two)


def unturn_kernel(dqt_ref, dk_ref, qkv_ref, scale_ref, gains_ref, cos_ref, sin_ref, hat_ref, inner_ref, gain_ref):
    width = dk_ref.shape[1]
    cos_two = cos_ref[...]
    sin_two = sin_ref[...]

    @pl.when(pl.program_id(0) == 0)
    def _():
        gain_ref[...] = jnp.zeros_like(gain_ref)

    for which in range(2):
        scale = scale_ref[:, which : which + 1]
        inner = jnp.zeros((dk_ref.shape[0], HD), f32)
        for head in range(width // HD):
            cols = slice(head * HD, (head + 1) * HD)
            off = which * width + head * HD
            grad = dqt_ref[cols, :].T if which == 0 else dk_ref[:, cols]
            hat = turn(grad, cos_two, -sin_two)
            pre = qkv_ref[:, off : off + HD]
            prod = hat * pre
            gain_ref[which : which + 1, cols] += jnp.sum(prod * scale, axis=0, keepdims=True)
            inner = inner + prod * gains_ref[which : which + 1, cols]
            hat_ref[:, off : off + HD] = hat * gains_ref[which : which + 1, cols]
        inner_ref[:, which : which + 1] = jnp.sum(inner, axis=1, keepdims=True)


def unturn(dqt, dk, qkv, inv_scale, gains, cos_two, sin_two):
    seq_len, width = dk.shape
    block = min(256, seq_len)
    table = pl.BlockSpec((block, HD), lambda i: (i, 0))
    pair = pl.BlockSpec((block, 2), lambda i: (i, 0))
    return pl.pallas_call(
        unturn_kernel,
        grid=(seq_len // block,),
        in_specs=[
            pl.BlockSpec((width, block), lambda i: (0, i)),
            pl.BlockSpec((block, width), lambda i: (i, 0)),
            pl.BlockSpec((block, 2 * width), lambda i: (i, 0)),
            pair,
            pl.BlockSpec((2, width), lambda i: (0, 0)),
            table,
            table,
        ],
        out_specs=[
            pl.BlockSpec((block, 2 * width), lambda i: (i, 0)),
            pair,
            pl.BlockSpec((2, width), lambda i: (0, 0)),
        ],
        out_shape=[
            jax.ShapeDtypeStruct((seq_len, 2 * width), f32),
            jax.ShapeDtypeStruct((seq_len, 2), f32),
            jax.ShapeDtypeStruct((2, width), f32),
        ],
        compiler_params=pltpu.CompilerParams(vmem_limit_bytes=48 << 20),
        cost_estimate=pl.CostEstimate(flops=20 * seq_len * width, bytes_accessed=24 * seq_len * width, transcendentals=0),
        name="unturn",
    )(dqt, dk, qkv, inv_scale, gains, cos_two, sin_two)


class Job:
    def __init__(self, gather, scatter, merge, weights, pieces, dim, spread, tile_ins, outs, slots, sums, body):
        self.gather, self.scatter, self.merge, self.spread = gather, scatter, merge, spread
        self.weights, self.pieces, self.dim = weights, pieces, dim
        self.tile_ins, self.outs = tile_ins, outs
        self.slots, self.sums, self.body = slots, sums, body


def tile_kernel(job, tp, chunks, *refs):
    refs = list(refs)

    def take(count):
        got = refs[:count]
        del refs[:count]
        return got

    (src_ref,) = take(1)
    w_hbm = [take(max(1, job.pieces)) for _ in range(job.weights)]
    ti_hbm = take(job.tile_ins)
    quarter_ref = take(1)[0] if job.spread else None
    full_ref = take(1)[0] if job.gather else src_ref
    out_hbm = take(job.outs)
    w_out = take(job.weights) if job.pieces else None
    spread_ref = take(1)[0] if job.spread else None
    total_ref = take(1)[0] if job.scatter else None
    w_ref = take(job.weights)
    (tile_ref,) = take(1)
    ti_ref = take(job.tile_ins)
    out_ref = take(job.outs)
    y_ref, rbuf, zbuf, tbuf = take(4) if job.scatter else (None,) * 4
    w_sem, tile_sem, ti_sem, out_sem, loc_sem = take(5)
    t_send, t_recv, r_send, r_recv = take(4)
    y_send, y_recv, z_send, z_recv = take(4)
    wl_sem, wr_send, wr_recv, q_send, q_recv = take(5)

    n_dp = lax.axis_size("dp")
    d, r, g, t = (lax.axis_index(name) for name in ("dp", "row", "zh", "zl"))
    rows = tile_ref.shape[1]
    if job.merge:
        mc = rows // (2 * chunks)
        order = [(s, 0) for s in range(tp)]
    else:
        mc = rows // 2
        order = [(s, c) for c in range(chunks) for s in range(tp)]
    if not job.gather:
        order = [(s, c) for s in list(range(1, tp)) + [0] for c in range(chunks)]
    row_dev = (d, 1 - r, g, t)

    def peer(step):
        return (d, r, g, lax.rem(t + step + tp, tp))

    def remote(src, dst, send, recv, dev):
        return pltpu.make_async_remote_copy(
            src_ref=src, dst_ref=dst, send_sem=send, recv_sem=recv, device_id=dev,
            device_id_type=pl.DeviceIdType.MESH,
        )

    def piece(s, c, rho):
        return full_ref.at[pl.ds(((s * chunks + c) * 2 + rho) * mc, mc)]

    barrier = pltpu.get_barrier_semaphore()
    pl.semaphore_signal(barrier, inc=1, device_id=row_dev, device_id_type=pl.DeviceIdType.MESH)
    for s in range(1, tp):
        pl.semaphore_signal(barrier, inc=1, device_id=peer(s), device_id_type=pl.DeviceIdType.MESH)

    count = tp
    if job.spread:
        for k in range(1, n_dp):
            dev = (lax.rem(d + k, n_dp), r, g, t)
            pl.semaphore_signal(barrier, inc=1, device_id=dev, device_id_type=pl.DeviceIdType.MESH)
            count += 1
    same = r == g
    other_core = jnp.logical_not(same)

    def half_view(i, half, row_at, row_count, col_at, col_count):
        ref = w_ref[i]
        if job.dim == 0:
            size = ref.shape[0] // 2
            start = pl.multiple_of(half * size + row_at, row_count)
            return ref.at[pl.ds(start, row_count), pl.ds(col_at, col_count)]
        size = ref.shape[1] // 2
        return ref.at[pl.ds(row_at, row_count), pl.ds(pl.multiple_of(half * size + col_at, col_count), col_count)]

    def piece_list(i):
        if len(w_hbm[i]) == 2:
            other = w_hbm[i][1]
            return [(other, 0, other.shape[0], 0, other.shape[1])]
        one, two, one_x, one_y, two_y, two_x = w_hbm[i][1:]
        rows_q, cut = one.shape
        low_bit, high_bit = lax.rem(d, 2), d // 2
        places = [
            ((high_bit * (1 - 2 * (k // 2)) + k // 2) * 2 + low_bit * (1 - 2 * (k % 2)) + k % 2) * rows_q
            for k in range(4)
        ]
        upper, lower = pl.ds(0, rows_q), pl.ds(rows_q, rows_q)
        return [
            (one, places[0], rows_q, 0, cut),
            (one_x, places[1], rows_q, 0, cut),
            (one_y.at[upper], places[2], rows_q, 0, cut),
            (one_y.at[lower], places[3], rows_q, 0, cut),
            (two, places[0], rows_q, cut, cut),
            (two_x.at[upper], places[1], rows_q, cut, cut),
            (two_y, places[2], rows_q, cut, cut),
            (two_x.at[lower], places[3], rows_q, cut, cut),
        ]

    def piece_recv_places(i):
        return [half_view(i, 1 - r, *spot[1:]) for spot in piece_list(i)]

    def low_copies(i):
        low = w_hbm[i][0]
        there = half_view(i, r, 0, low.shape[0], 0, low.shape[1])
        here = half_view(i, 1 - r, 0, low.shape[0], 0, low.shape[1])
        keep = pltpu.make_async_copy(low, there, wl_sem.at[i, 0])
        give = pltpu.make_async_remote_copy(
            src_ref=low, dst_ref=there, send_sem=wr_send.at[i, 0], recv_sem=wr_recv.at[i, 0],
            device_id=row_dev, device_id_type=pl.DeviceIdType.MESH,
        )
        got = pltpu.make_async_remote_copy(
            src_ref=low, dst_ref=here, send_sem=wr_send.at[i, 0], recv_sem=wr_recv.at[i, 0],
            device_id=row_dev, device_id_type=pl.DeviceIdType.MESH,
        )
        return keep, give, got

    def part_copies(i):
        keeps, gives, gots = [], [], []
        for p, spot in enumerate(piece_list(i)):
            there = half_view(i, r, *spot[1:])
            here = piece_recv_places(i)[p]
            keeps.append(pltpu.make_async_copy(spot[0], there, wl_sem.at[i, p]))
            for dst, into in ((there, gives), (here, gots)):
                into.append(
                    pltpu.make_async_remote_copy(
                        src_ref=spot[0], dst_ref=dst, send_sem=wr_send.at[i, p], recv_sem=wr_recv.at[i, p],
                        device_id=row_dev, device_id_type=pl.DeviceIdType.MESH,
                    )
                )
        return keeps, gives, gots

    def w_start(i):
        if not job.pieces:
            pltpu.make_async_copy(w_hbm[i][0], w_ref[i], w_sem.at[i]).start()
            return

        @pl.when(same)
        def _():
            low_copies(i)[0].start()
            for cp in part_copies(i)[1]:
                cp.start()

        @pl.when(other_core)
        def _():
            low_copies(i)[1].start()
            for cp in part_copies(i)[0]:
                cp.start()

    def w_wait(i):
        if not job.pieces:
            pltpu.make_async_copy(w_hbm[i][0], w_ref[i], w_sem.at[i]).wait()
            return

        @pl.when(same)
        def _():
            low_copies(i)[0].wait()
            low_copies(i)[2].wait_recv()

        @pl.when(other_core)
        def _():
            for cp in part_copies(i)[0]:
                cp.wait()
            for cp in part_copies(i)[2]:
                cp.wait_recv()

        pltpu.make_async_copy(w_ref[i], w_out[i], w_sem.at[i]).start()

    def w_end(i):

        @pl.when(same)
        def _():
            for cp in part_copies(i)[1]:
                cp.wait_send()

        @pl.when(other_core)
        def _():
            low_copies(i)[1].wait_send()

        pltpu.make_async_copy(w_ref[i], w_out[i], w_sem.at[i]).wait()

    if not job.pieces:
        for i in range(job.weights):
            w_start(i)
    pl.semaphore_wait(barrier, count)
    seen = set()

    def need(i):
        if i not in seen:
            seen.add(i)
            w_wait(i)

    sends = []

    def go(cp):
        cp.start()
        sends.append(cp)

    local = {}
    if job.gather:
        for c in range(chunks):
            own = src_ref.at[pl.ds(c * mc, mc)]
            for s in range(1, tp):
                go(remote(own, piece(s, c, 0), t_send.at[s, c], t_recv.at[s, c], peer(-s)))
            local[c] = pltpu.make_async_copy(own, piece(0, c, 0), loc_sem.at[c])
            local[c].start()
            go(remote(own, piece(0, c, 1), r_send.at[0, c], r_recv.at[0, c], row_dev))

    if job.pieces:
        for i in range(job.weights):
            w_start(i)
    if job.spread:
        rows_q = quarter_ref.shape[0]
        mine = spread_ref.at[pl.ds(pl.multiple_of(d * rows_q, rows_q), rows_q)]
        q_local = pltpu.make_async_copy(quarter_ref, mine, q_send.at[0])
        q_local.start()
        for k in range(1, n_dp):
            go(remote(quarter_ref, mine, q_send.at[k], q_recv.at[k], (lax.rem(d + k, n_dp), r, g, t)))

    relayed = set()

    def relay(s, c):
        if job.gather and s > 0 and (s, c) not in relayed:
            relayed.add((s, c))
            remote(piece(s, c, 0), piece(s, c, 0), t_send.at[s, c], t_recv.at[s, c], peer(-s)).wait_recv()
            go(remote(piece(s, c, 0), piece(s, c, 1), r_send.at[s, c], r_recv.at[s, c], row_dev))

    def tile_load(i):
        s, c = order[i]
        at = pl.ds((s if job.merge else s * chunks + c) * rows, rows)
        return pltpu.make_async_copy(full_ref.at[at], tile_ref.at[i % 2], tile_sem.at[i % 2])

    def ti_loads(i):
        s, c = order[i]
        at = pl.ds((s if job.merge else s * chunks + c) * rows, rows)
        return [pltpu.make_async_copy(ti_hbm[j].at[at], ti_ref[j], ti_sem.at[j]) for j in range(job.tile_ins)]

    def out_copies(i):
        s, c = order[i]
        at = pl.ds((s if job.merge else s * chunks + c) * rows, rows)
        slot = i % job.slots
        return [
            pltpu.make_async_copy(out_ref[j].at[slot], out_hbm[j].at[at], out_sem.at[j, slot])
            for j in range(job.outs)
        ]

    def combine(i):
        s, c = order[i]
        k = s * chunks + c
        cp = remote(
            y_ref.at[i % job.sums, pl.ds(mc, mc)], rbuf.at[k], y_send.at[s, c], y_recv.at[s, c], row_dev
        )
        cp.wait()
        step = min(64, mc)

        def add(b, carry):
            at = pl.ds(pl.multiple_of(b * step, step), step)
            summed = y_ref[i % job.sums, at, :].astype(f32) + rbuf[k, at, :].astype(f32)
            if s == 0:
                total_ref[pl.ds(pl.multiple_of(c * mc + b * step, step), step), :] = summed
            else:
                zbuf[k - chunks, at, :] = summed.astype(bf16)
            return carry

        lax.fori_loop(0, mc // step, add, 0)
        if s > 0:
            go(remote(zbuf.at[k - chunks], tbuf.at[k - chunks], z_send.at[s, c], z_recv.at[s, c], peer(s)))

    for cp in ti_loads(0):
        cp.start()
    if not job.gather:
        tile_load(0).start()
    for i, (s, c) in enumerate(order):
        if job.gather:
            held = range(chunks) if job.merge else [c]
            for cc in held:
                relay(s, cc)
                if s == 0:
                    local[cc].wait()
            for cc in held:
                remote(piece(s, cc, 1), piece(s, cc, 1), r_send.at[s, cc], r_recv.at[s, cc], row_dev).wait_recv()
            tile_load(i).start()
        tile_load(i).wait()
        if not job.gather and i + 1 < len(order):
            tile_load(i + 1).start()
        for cp in ti_loads(i):
            cp.wait()
        if i >= job.slots:
            for cp in out_copies(i - job.slots):
                cp.wait()

        def mid(i=i):
            if i + 1 < len(order):
                relay(*order[i + 1])
                for cp in ti_loads(i + 1):
                    cp.start()
            if job.scatter:
                for cp in out_copies(i):
                    cp.start()
                if i >= 1:
                    combine(i - 1)

        outs = [ref.at[i % job.slots] for ref in out_ref]
        y = y_ref.at[i % job.sums] if job.scatter else None
        job.body(tile_ref.at[i % 2], w_ref, need, ti_ref, outs, y, mid)
        if job.scatter:
            k = s * chunks + c
            remote(y.at[pl.ds(mc, mc)], rbuf.at[k], y_send.at[s, c], y_recv.at[s, c], row_dev).start()
        else:
            for cp in out_copies(i):
                cp.start()
    last = len(order)
    for i in range(max(0, last - job.slots), last):
        for cp in out_copies(i):
            cp.wait()
    if job.scatter:
        combine(last - 1)
        for c in range(chunks):
            for s in range(1, tp):
                k = (s - 1) * chunks + c
                remote(zbuf.at[k], tbuf.at[k], z_send.at[s, c], z_recv.at[s, c], peer(s)).wait_recv()
                step = min(64, mc)

                def add(b, carry, k=k, c=c):
                    at = pl.ds(pl.multiple_of(b * step, step), step)
                    to = pl.ds(pl.multiple_of(c * mc + b * step, step), step)
                    total_ref[to, :] = total_ref[to, :] + tbuf[k, at, :].astype(f32)
                    return carry

                lax.fori_loop(0, mc // step, add, 0)
    if job.pieces:
        for i in range(job.weights):
            w_end(i)
    if job.spread:
        q_local.wait()
        for k in range(1, n_dp):
            came = lax.rem(d + n_dp - k, n_dp)
            remote(
                quarter_ref, spread_ref.at[pl.ds(pl.multiple_of(came * rows_q, rows_q), rows_q)],
                q_send.at[k], q_recv.at[k], row_dev,
            ).wait_recv()
    for cp in sends:
        cp.wait_send()


def tile_call(job, ident, name, src, weights, shapes, tile_ins, out_widths, sum_width, flops, quarter=None):
    tp = lax.axis_size("zl")
    n_dp = lax.axis_size("dp")
    flat_weights = [v for group in weights for v in group]
    width = src.shape[1]
    m = src.shape[0] if job.gather else src.shape[0] // (2 * tp)
    chunks = 2 if tp == 2 else 1
    mc = m // chunks
    rows = 2 * (m if job.merge else mc)
    total_rows = 2 * tp * m
    anywhere = pl.BlockSpec(memory_space=pl.ANY)
    dma = pltpu.SemaphoreType.DMA
    out_specs, out_shape = [], []
    if job.gather:
        out_specs.append(anywhere)
        out_shape.append(jax.ShapeDtypeStruct((total_rows, width), bf16))
    for w in out_widths:
        out_specs.append(anywhere)
        out_shape.append(jax.ShapeDtypeStruct((total_rows, w), bf16))
    if job.pieces:
        out_specs.extend([anywhere] * len(shapes))
        out_shape.extend(jax.ShapeDtypeStruct(shape, bf16) for shape in shapes)
    if job.spread:
        out_specs.append(anywhere)
        out_shape.append(jax.ShapeDtypeStruct((n_dp * quarter.shape[0], quarter.shape[1]), bf16))
    if job.scatter:
        out_specs.append(pl.BlockSpec(memory_space=pltpu.VMEM))
        out_shape.append(jax.ShapeDtypeStruct((m, sum_width), f32))
    scratch = [pltpu.VMEM(shape, bf16) for shape in shapes]
    scratch.append(pltpu.VMEM((2, rows, width), bf16))
    scratch.extend(pltpu.VMEM((rows, v.shape[1]), bf16) for v in tile_ins)
    scratch.extend(pltpu.VMEM((job.slots, rows, w), bf16) for w in out_widths)
    if job.scatter:
        scratch.append(pltpu.VMEM((job.sums, rows, sum_width), bf16))
        scratch.append(pltpu.VMEM((tp * chunks, mc, sum_width), bf16))
        scratch.append(pltpu.VMEM(((tp - 1) * chunks, mc, sum_width), bf16))
        scratch.append(pltpu.VMEM(((tp - 1) * chunks, mc, sum_width), bf16))
    scratch.extend(
        [dma((len(weights),)), dma((2,)), dma((max(1, len(tile_ins)),)), dma((max(1, job.outs), job.slots)), dma((chunks,))]
    )
    scratch.extend(dma((tp, chunks)) for _ in range(8))
    scratch.extend(dma((len(weights), 8)) for _ in range(3))
    scratch.extend(dma((n_dp,)) for _ in range(2))
    extra = [quarter] if job.spread else []
    return pl.pallas_call(
        functools.partial(tile_kernel, job, tp, chunks),
        in_specs=[anywhere] * (1 + len(flat_weights) + len(tile_ins) + len(extra)),
        out_specs=out_specs,
        out_shape=out_shape,
        scratch_shapes=scratch,
        compiler_params=pltpu.CompilerParams(
            collective_id=ident, has_side_effects=True, vmem_limit_bytes=60 << 20
        ),
        cost_estimate=pl.CostEstimate(flops=flops, bytes_accessed=8 * total_rows * width, transcendentals=0),
        name=name,
    )(src, *flat_weights, *tile_ins, *extra)


def columns(n, size):
    return pl.ds(pl.multiple_of(n * size, size), size)


def loop(first, last, step):
    def body(n, carry):
        step(n)
        return carry

    lax.fori_loop(first, last, body, 0)


def gate_up_body(tile, w, need, ti, outs, y, mid):
    hidden_width = w[0].shape[1]
    nb = min(512, hidden_width)
    count = hidden_width // nb
    need(0)
    need(1)

    def step(n):
        cols = columns(n, nb)
        rows = tile[...]
        gate = jnp.dot(rows, w[0][:, cols], preferred_element_type=f32)
        up = jnp.dot(rows, w[1][:, cols], preferred_element_type=f32)
        outs[0][:, cols] = gate.astype(bf16)
        outs[1][:, cols] = up.astype(bf16)
        outs[2][:, cols] = (gate * jax.nn.sigmoid(gate) * up).astype(bf16)

    loop(0, count // 2, step)
    mid()
    loop(count // 2, count, step)


def down_body(tile, w, need, ti, outs, y, mid):
    nb = min(1024, w[0].shape[1])
    count = w[0].shape[1] // nb
    need(0)

    def step(n):
        cols = columns(n, nb)
        y[:, cols] = jnp.dot(tile[...], w[0][:, cols], preferred_element_type=f32).astype(bf16)

    loop(0, count // 2, step)
    mid()
    loop(count // 2, count, step)


def back_body(tile, w, need, ti, outs, y, mid):
    hidden_width = w[0].shape[0]
    nb = min(512, hidden_width)
    need(0)

    def first(n):
        cols = columns(n, nb)
        grad = lax.dot_general(tile[...], w[0][cols, :], NT, preferred_element_type=f32)
        grad = grad.astype(bf16).astype(f32)
        gate = ti[0][:, cols].astype(f32)
        up = ti[1][:, cols].astype(f32)
        sig = jax.nn.sigmoid(gate)
        passed = grad * sig
        outs[0][:, cols] = (passed * up * (1.0 + gate * (1.0 - sig))).astype(bf16)
        outs[1][:, cols] = (passed * gate).astype(bf16)

    loop(0, hidden_width // nb, first)
    mid()
    need(1)
    need(2)
    nd = 512

    def second(n):
        cols = columns(n, nd)
        grad = lax.dot_general(outs[0][...], w[1][cols, :], NT, preferred_element_type=f32)
        grad = grad + lax.dot_general(outs[1][...], w[2][cols, :], NT, preferred_element_type=f32)
        y[:, cols] = grad.astype(bf16)

    loop(0, w[1].shape[0] // nd, second)


gate_up_job = Job(True, False, False, 2, 7, 0, True, 0, 3, 2, 0, gate_up_body)
down_job = Job(False, True, False, 1, 2, 1, False, 0, 0, 1, 2, down_body)
back_job = Job(True, True, False, 3, 0, 0, False, 2, 2, 1, 1, back_body)


def last_kernel(
    chunks, dx_ref, down_ref, qkv_ref, up_ref, out_ref, down_out, qkv_out, up_out,
    own, from_row, near, from_t, give, from_zh,
    down_own, down_in, down_next, down_sum, down_late, qkv_own, qkv_in, qkv_next, qkv_sum, qkv_late,
    up_stay, up_late,
    own_sem, row_send, row_recv, t_send, t_recv, zh_send, zh_recv,
    g_sem, d_send, d_recv, f_local, f_send, f_recv,
):
    n_dp = lax.axis_size("dp")
    tp = lax.axis_size("zl")
    d, r, g, t = (lax.axis_index(name) for name in ("dp", "row", "zh", "zl"))
    same = r == g
    other_core = jnp.logical_not(same)
    seq_len, width = dx_ref.shape
    half = width // 2
    feat = half // (2 * tp)
    step = seq_len // chunks

    def remote(src, dst, send, recv, dev):
        return pltpu.make_async_remote_copy(
            src_ref=src, dst_ref=dst, send_sem=send, recv_sem=recv, device_id=dev,
            device_id_type=pl.DeviceIdType.MESH,
        )

    row_dev = (d, 1 - r, g, t)
    zh_dev = (d, r, 1 - g, t)
    cross_dev = (d, 1 - r, 1 - g, t)

    bits = (lax.rem(d, 2), d // 2)
    near_devs = ((bits[1] * 2 + 1 - bits[0], r, g, t), ((1 - bits[1]) * 2 + bits[0], r, g, t))

    def t_dev(s):
        return (d, r, g, lax.rem(t + s, tp))

    partners = [row_dev, zh_dev, cross_dev, *near_devs] + [t_dev(s) for s in range(1, tp)]
    barrier = pltpu.get_barrier_semaphore()
    for dev in partners:
        pl.semaphore_signal(barrier, inc=1, device_id=dev, device_id_type=pl.DeviceIdType.MESH)
    pl.semaphore_wait(barrier, len(partners))

    def owner_copies(i, pieces, late):
        return (
            remote(pieces.at[1 - r], late.at[0], f_send.at[i, 0], f_recv.at[i, 0], row_dev),
            remote(pieces.at[r], late.at[0], f_send.at[i, 1], f_recv.at[i, 1], zh_dev),
            remote(pieces.at[1 - r], late.at[1], f_send.at[i, 2], f_recv.at[i, 2], cross_dev),
        )

    def owner_start(i, pieces, late):
        @pl.when(same)
        def _():
            owner_copies(i, pieces, late)[0].start()

        @pl.when(other_core)
        def _():
            owner_copies(i, pieces, late)[1].start()
            owner_copies(i, pieces, late)[2].start()

    def owner_end(i, pieces, late, kept, total):
        @pl.when(same)
        def _():
            owner_copies(i, pieces, late)[1].wait_recv()
            total[...] = kept[...].astype(f32) + late[0].astype(f32)
            owner_copies(i, pieces, late)[0].wait_send()

        @pl.when(other_core)
        def _():
            owner_copies(i, pieces, late)[0].wait_recv()
            owner_copies(i, pieces, late)[2].wait_recv()
            total[...] = late[0].astype(f32) + late[1].astype(f32)
            owner_copies(i, pieces, late)[1].wait_send()
            owner_copies(i, pieces, late)[2].wait_send()

    up_local = pltpu.make_async_copy(up_ref.at[r], up_stay, f_local)
    up_local.start()
    owner_start(2, up_ref, up_late)

    def down_piece(which, group):
        rows, cols = down_sum.shape[1:]
        return down_ref.at[
            pl.ds(pl.multiple_of(group * rows, rows), rows), pl.ds(pl.multiple_of(which * cols, cols), cols)
        ]

    def qkv_piece(which, group):
        rows = qkv_sum.shape[1]
        return qkv_ref.at[pl.ds(pl.multiple_of((which * n_dp + group) * rows, rows), rows)]

    def group_at(which, first, second):
        return second * 2 + first if which == 0 else first * 2 + second

    def group_copies(i, piece, mine, inbox, following):
        loads, sends, nexts = [], [], []
        for which in range(2):
            for other in range(2):
                at = which * 2 + other
                loads.append(
                    pltpu.make_async_copy(
                        piece(which, group_at(which, bits[which], other)), mine.at[at], g_sem.at[i, at]
                    )
                )
                sends.append(
                    remote(
                        piece(which, group_at(which, 1 - bits[which], other)), inbox.at[at],
                        d_send.at[i, at], d_recv.at[i, at], near_devs[which],
                    )
                )
            nexts.append(
                remote(
                    mine.at[which * 2 + 1 - bits[1 - which]], following.at[which],
                    d_send.at[i, 4 + which], d_recv.at[i, 4 + which], near_devs[1 - which],
                )
            )
        return loads, sends, nexts

    down_copies = group_copies(0, down_piece, down_own, down_in, down_next)
    qkv_copies = group_copies(1, qkv_piece, qkv_own, qkv_in, qkv_next)

    def cols_at(which):
        return pl.ds(pl.multiple_of(which * half, half), half)

    rows_copies, own_copies = [], []
    for c in range(chunks):
        rows = pl.ds(c * step, step)
        cp = remote(dx_ref.at[rows, cols_at(1 - r)], from_row.at[c], row_send.at[c], row_recv.at[c], row_dev)
        cp.start()
        rows_copies.append(cp)
        cp = pltpu.make_async_copy(dx_ref.at[rows, cols_at(r)], own.at[c], own_sem.at[c])
        cp.start()
        own_copies.append(cp)
    for loads, sends, _ in (down_copies, qkv_copies):
        for cp in loads + sends:
            cp.start()

    t_copies = {}

    def row_stage(c):
        own_copies[c].wait()
        rows_copies[c].wait_recv()
        total = own[c].astype(f32) + from_row[c].astype(f32)
        for b in range(2 * tp):
            near[c, b] = total[:, b * feat : (b + 1) * feat].astype(bf16)
        for zh in range(2):
            for s in range(1, tp):
                cp = remote(
                    near.at[c, zh * tp + lax.rem(t + s, tp)], from_t.at[c, zh, s - 1],
                    t_send.at[c, zh, s], t_recv.at[c, zh, s], t_dev(s),
                )
                cp.start()
                t_copies[(c, zh, s)] = cp

    zh_copies = []

    def t_stage(c):
        for zh in range(2):
            for s in range(1, tp):
                t_copies[(c, zh, s)].wait_recv()

        def total_of(zh):
            total = near[c, zh * tp + t].astype(f32)
            for s in range(1, tp):
                total = total + from_t[c, zh, s - 1].astype(f32)
            return total

        give[c] = total_of(1 - g).astype(bf16)
        cp = remote(give.at[c], from_zh.at[c], zh_send.at[c], zh_recv.at[c], zh_dev)
        cp.start()
        zh_copies.append(cp)
        out_ref[pl.ds(pl.multiple_of(g * seq_len + c * step, step), step), :] = total_of(g)

    def group_first(copies, mine, inbox):
        block = min(64, mine.shape[1])
        for at in range(4):
            copies[0][at].wait()
            copies[1][at].wait_recv()

            def add(i, carry, at=at):
                span = pl.ds(pl.multiple_of(i * block, block), block)
                mine[at, span, :] = (mine[at, span, :].astype(f32) + inbox[at, span, :].astype(f32)).astype(bf16)
                return carry

            lax.fori_loop(0, mine.shape[1] // block, add, 0)
        for cp in copies[2]:
            cp.start()

    def group_second(copies, mine, following, total_ref):
        block = min(64, mine.shape[1])
        for which in range(2):
            copies[2][which].wait_recv()

            def add(i, carry, which=which):
                span = pl.ds(pl.multiple_of(i * block, block), block)
                kept = mine[which * 2 + bits[1 - which], span, :].astype(f32)
                total_ref[which, span, :] = (kept + following[which, span, :].astype(f32)).astype(bf16)
                return carry

            lax.fori_loop(0, mine.shape[1] // block, add, 0)

    for c in range(chunks):
        row_stage(c)
        if c >= 1:
            t_stage(c - 1)
    t_stage(chunks - 1)
    group_first(down_copies, down_own, down_in)
    group_first(qkv_copies, qkv_own, qkv_in)
    group_second(down_copies, down_own, down_next, down_sum)
    owner_start(0, down_sum, down_late)
    group_second(qkv_copies, qkv_own, qkv_next, qkv_sum)
    owner_start(1, qkv_sum, qkv_late)
    for c in range(chunks):
        zh_copies[c].wait_recv()
        out_ref[pl.ds(pl.multiple_of((1 - g) * seq_len + c * step, step), step), :] = from_zh[c].astype(f32)
    up_local.wait()
    owner_end(2, up_ref, up_late, up_stay, up_out)
    owner_end(0, down_sum, down_late, down_sum.at[r], down_out)
    owner_end(1, qkv_sum, qkv_late, qkv_sum.at[r], qkv_out)
    for cp in down_copies[1] + qkv_copies[1] + down_copies[2] + qkv_copies[2]:
        cp.wait_send()
    for cp in rows_copies + list(t_copies.values()) + zh_copies:
        cp.wait_send()


def last_sums(dx, down, qkv, up):
    n_dp = lax.axis_size("dp")
    tp = lax.axis_size("zl")
    seq_len, width = dx.shape
    chunks = 4
    half = width // 2
    feat = half // (2 * tp)
    step = seq_len // chunks
    anywhere = pl.BlockSpec(memory_space=pl.ANY)
    vmem = pl.BlockSpec(memory_space=pltpu.VMEM)
    dma = pltpu.SemaphoreType.DMA
    down_shape = (down.shape[0] // n_dp, down.shape[1] // 2)
    qkv_shape = (qkv.shape[0] // (2 * n_dp), qkv.shape[1])
    sums = []
    for shape in (down_shape, qkv_shape):
        sums += [
            pltpu.VMEM((4, *shape), bf16),
            pltpu.VMEM((4, *shape), bf16),
            pltpu.VMEM((2, *shape), bf16),
            pltpu.VMEM((2, *shape), bf16),
            pltpu.VMEM((2, *shape), bf16),
        ]
    return pl.pallas_call(
        functools.partial(last_kernel, chunks),
        in_specs=[anywhere] * 4,
        out_specs=[vmem] * 4,
        out_shape=[
            jax.ShapeDtypeStruct((2 * seq_len, feat), f32),
            jax.ShapeDtypeStruct(down_shape, f32),
            jax.ShapeDtypeStruct(qkv_shape, f32),
            jax.ShapeDtypeStruct(up.shape[1:], f32),
        ],
        scratch_shapes=[
            pltpu.VMEM((chunks, step, half), bf16),
            pltpu.VMEM((chunks, step, half), bf16),
            pltpu.VMEM((chunks, 2 * tp, step, feat), bf16),
            pltpu.VMEM((chunks, 2, tp - 1, step, feat), bf16),
            pltpu.VMEM((chunks, step, feat), bf16),
            pltpu.VMEM((chunks, step, feat), bf16),
            *sums,
            pltpu.VMEM(up.shape[1:], bf16),
            pltpu.VMEM(up.shape, bf16),
            dma((chunks,)),
            dma((chunks,)),
            dma((chunks,)),
            dma((chunks, 2, tp)),
            dma((chunks, 2, tp)),
            dma((chunks,)),
            dma((chunks,)),
            dma((2, 4)),
            dma((2, 6)),
            dma((2, 6)),
            dma(()),
            dma((3, 3)),
            dma((3, 3)),
        ],
        compiler_params=pltpu.CompilerParams(collective_id=4, has_side_effects=True, vmem_limit_bytes=60 << 20),
        cost_estimate=pl.CostEstimate(flops=0, bytes_accessed=8 * seq_len * width, transcendentals=0),
        name="last_sums",
    )(dx, down, qkv, up)


def rotary(seq_len):
    half_width = HD // 2
    freqs = rope_base ** (-(jnp.arange(half_width, dtype=f32) * 2.0) / HD)
    angles = jnp.arange(seq_len, dtype=f32)[:, None] * freqs[None, :]
    cos_table, sin_table = jnp.cos(angles), jnp.sin(angles)
    return (
        jnp.concatenate([cos_table, cos_table], axis=1),
        jnp.concatenate([-sin_table, sin_table], axis=1),
    )


def norm_scale(vals):
    return lax.rsqrt(jnp.mean(vals * vals, axis=1, keepdims=True) + norm_eps)


def norm_back(pre_vals, scale, gains, gradient):
    weighted = gradient * gains
    inner = jnp.mean(weighted * pre_vals, axis=1, keepdims=True)
    grad_pre = scale * weighted - pre_vals * (scale * scale * scale * inner)
    grad_gain = jnp.sum(gradient * pre_vals * scale, axis=0)
    return grad_pre, grad_gain


def adamw_step(weight, gradient, first_mom, second_mom, step_rate, decay_rate):
    first_new = beta_one * first_mom + (1.0 - beta_one) * gradient
    second_new = beta_two * second_mom + (1.0 - beta_two) * gradient * gradient
    fix_one = 1.0 - beta_one**STEP
    fix_two = 1.0 - beta_two**STEP
    direction = first_new / fix_one / (jnp.sqrt(second_new / fix_two) + adam_eps)
    return (first_new, second_new, weight - step_rate * (direction + decay_rate * weight))


def matmul(left, right, dims=NN):
    return lax.dot_general(left, right, dims, preferred_element_type=f32)


def shards(
    tokens, cotangent, doc_lengths, qkv_weight, out_weight, gate_weight, up_weight, down_weight,
    head_gains, post_gains, qkv_first, qkv_second, out_first, out_second, gate_first, gate_second,
    up_first, up_second, down_first, down_second, head_first, head_second, post_first, post_second,
):
    n_dp = lax.axis_size("dp")
    tp = lax.axis_size("zl")
    group = 2 * tp
    n_col = 2 * tp
    d, r, g, t = (lax.axis_index(name) for name in ("dp", "row", "zh", "zl"))
    same = r == g
    block_at = r * tp + t
    rows_dev, feat = tokens.shape
    width = feat * 2 * n_col
    seq_len = rows_dev // 2
    mine = seq_len // group
    col_width = qkv_weight.shape[2]

    qkv_low = jnp.concatenate([qkv_weight[:, i, :].astype(bf16) for i in range(3)], axis=1)
    docs = doc_lengths.shape[1]
    small = [post_gains.T.reshape(-1), head_gains.reshape(-1), doc_lengths[0].astype(f32)]
    small = jnp.concatenate(small)
    pad = -small.shape[0] % 1024
    small = jnp.concatenate([small, jnp.zeros((pad,), f32)]).reshape(-1, 128)

    def quarter_of(weight):
        rows = weight.shape[0] // n_dp
        return lax.dynamic_slice_in_dim(weight, d * rows, rows, 0).astype(bf16)

    x_full, qkv_full, small_all, gate_quarter = first_gather(tokens, qkv_low, small, quarter_of(gate_weight))
    small_all = small_all.reshape(2 * n_col, -1)
    cut_one, cut_two = 2 * feat, 2 * feat + 2 * col_width
    post_all = small_all[:, :cut_one].reshape(2 * n_col, 2, feat).transpose(1, 0, 2).reshape(2, width)
    gains = lax.dynamic_slice_in_dim(small_all, block_at, 1, 0)[0, cut_one:cut_two].reshape(2, col_width)
    lengths = lax.dynamic_slice_in_dim(small_all, g * n_col, 1, 0)[0, cut_two : cut_two + docs]
    ends = jnp.cumsum(lengths.astype(jnp.int32))
    x_tok = lax.dynamic_slice_in_dim(x_full, block_at * mine, mine, 0)

    def halves(quarter):
        cut = quarter.shape[1] // 2
        return quarter[:, :cut], quarter[:, cut:]

    def gathered(one, two, one_x, two_y):
        one_y = swap_bit(jnp.concatenate([one, one_x]), "dp", 2)
        two_x = swap_bit(jnp.concatenate([two, two_y]), "dp", 1)
        return [one, two, one_x, one_y, two_y, two_x]

    gate_one, gate_two = halves(gate_quarter)
    up_one, up_two = halves(quarter_of(up_weight))
    up_one, up_two, post_all = tie(up_one, up_two, post_all)
    up_one, up_two = swap(up_one, "zh"), swap(up_two, "zh")
    gate_one_x, gate_two_y = swap_bit(gate_one, "dp", 1), swap_bit(gate_two, "dp", 2)

    out_rows = out_weight.shape[0] // n_dp
    out_part = lax.dynamic_slice_in_dim(out_weight, d * out_rows, out_rows, 0).astype(bf16)
    out_part, post_all = tie(lax.all_gather(out_part, ("zh", "zl"), axis=0), post_all)
    out_part = lax.all_gather(out_part, "dp", axis=1)

    cos_two, sin_two = rotary(seq_len)
    qkv = matmul(x_full, qkv_full)
    squares = jnp.stack(
        [
            jnp.sum(jnp.square(qkv[:, :col_width]), axis=1),
            jnp.sum(jnp.square(qkv[:, col_width : 2 * col_width]), axis=1),
        ],
        axis=0,
    )
    inv_scale = lax.rsqrt(small_sum(squares, ("row", "zl")) / width + norm_eps).T
    down_quarter = swap(quarter_of(down_weight), "zh")
    inv_scale, gate_one_x, gate_two_y = tie(inv_scale, gate_one_x, gate_two_y)
    query, key, key_t, value, value_t = prepare(qkv, inv_scale, gains, cos_two, sin_two)
    ends, up_one = tie(ends, up_one)
    out_part, key_t = tie(out_part, key_t)
    out_full = lax.all_gather(out_part.reshape(width, width // 2), "row", axis=1, tiled=True)
    att, log_total = attend(query, key, value_t, ends)
    gate_pieces = gathered(gate_one, gate_two, gate_one_x, gate_two_y)
    att, up_two, gate_pieces[3], gate_pieces[5] = tie(att, up_two, gate_pieces[3], gate_pieces[5])
    up_one_x, up_two_y = swap_bit(up_one, "dp", 1), swap_bit(up_two, "dp", 2)

    def data_sums(grad):
        half = grad.shape[0] // 2
        return [
            lax.psum_scatter(grad[i * half : (i + 1) * half], "dp", scatter_dimension=0, tiled=True)
            for i in range(2)
        ]

    def to_tokens(vals):
        got = lax.all_to_all(vals.reshape(group, mine, col_width), ("row", "zl"), 0, 0)
        return got.transpose(1, 0, 2).reshape(mine, width)

    def to_heads(vals):
        sent = vals.reshape(mine, group, col_width).transpose(1, 0, 2)
        return lax.all_to_all(sent, ("row", "zl"), 0, 0).reshape(seq_len, col_width)

    att_tok = to_tokens(att)

    gain_attn, gain_mlp = post_all[0:1], post_all[1:2]
    att_tok, up_one_x, up_two_y = tie(att_tok, up_one_x, up_two_y)
    a_pre = matmul(att_tok, out_full)
    a_scale = norm_scale(a_pre)
    h_tok = x_tok.astype(f32) + a_pre * a_scale * gain_attn

    cot = cotangent.reshape(2, 2, tp, mine, feat).transpose(1, 0, 2, 3, 4).reshape(2 * n_col, mine, feat)
    cot, a_scale = tie(cot, a_scale)
    cot = lax.all_to_all(cot, ("row", "zh", "zl"), 0, 0)
    cot_tok = cot.transpose(1, 0, 2).reshape(mine, width).astype(f32)

    up_pieces = gathered(up_one, up_two, up_one_x, up_two_y)
    gate_low, up_low, down_low = (
        v.astype(bf16) for v in (gate_weight, up_weight, down_weight)
    )
    hidden_width = gate_low.shape[1]
    work = 2 * seq_len * width * hidden_width
    wide, tall = (width, hidden_width), (hidden_width, width)
    h_full, gate_all, up_all, hidden, gate_full, up_full, down_other = tile_call(
        gate_up_job, 1, "gate_up", h_tok.astype(bf16), [[gate_low, *gate_pieces], [up_low, *up_pieces]],
        [wide, wide], [], [hidden_width] * 3, 0, 2 * work, down_quarter,
    )
    down_full, m_pre = tile_call(
        down_job, 2, "down", hidden, [[down_low, down_other]], [tall], [], [], width, work
    )
    m_scale = norm_scale(m_pre)
    mixed_tok = (h_tok + m_pre * m_scale * gain_mlp).astype(bf16)

    def to_features(vals):
        out = lax.all_to_all(
            vals.reshape(mine, 2 * n_col, feat).transpose(1, 0, 2), ("row", "zh", "zl"), 0, 0
        )
        return out.reshape(2, 2, tp, mine, feat).transpose(1, 0, 2, 3, 4).reshape(rows_dev, feat)

    mixed = to_features(mixed_tok)

    grad_m, grad_gain_mlp = norm_back(m_pre, m_scale, gain_mlp, cot_tok)
    dm_full, grad_gate, grad_up, dh_sum = tile_call(
        back_job, 3, "feed_back", grad_m.astype(bf16), [[down_full], [gate_full], [up_full]], [tall, wide, wide],
        [gate_all, up_all], [hidden_width] * 2, width, 3 * work,
    )
    dh_tok = cot_tok + dh_sum

    grad_a, grad_gain_attn = norm_back(a_pre, a_scale, gain_attn, dh_tok)
    grad_a = grad_a.astype(bf16)
    datt = matmul(grad_a, out_full, NT).astype(bf16)
    datt, hidden, h_full = tie(datt, hidden, h_full)
    grad_att = to_heads(datt)
    grad_gate_w = matmul(h_full, grad_gate, TN).astype(bf16)
    grad_up_w = matmul(h_full, grad_up, TN).astype(bf16)
    gate_sums = data_sums(grad_gate_w)
    grad_att, grad_up_w = tie(grad_att, grad_up_w)
    up_sums = data_sums(grad_up_w)
    grad_down_w = matmul(hidden, dm_full, TN).astype(bf16)
    grad_out = matmul(att_tok, grad_a, TN).astype(bf16)

    dqt, dk, dv = attend_back(query, key, key_t, value, grad_att, att, log_total, ends)
    weighted, inner, grad_head = unturn(dqt, dk, qkv, inv_scale, gains, cos_two, sin_two)
    def owner_parts(pieces):
        keep = jnp.where(r == 0, pieces[0], pieces[1])
        give = jnp.where(r == 0, pieces[1], pieces[0])
        axes = ("row", "zh")
        return [
            keep,
            lax.ppermute(keep, axes, [(1, 0), (2, 3)]),
            lax.ppermute(give, axes, [(1, 2), (2, 1)]),
            lax.ppermute(give, axes, [(0, 2), (3, 1)]),
        ]

    gate_parts = owner_parts(gate_sums)
    inner = (small_sum(inner.T, ("row", "zl")) / width).T
    cube = inv_scale * inv_scale * inv_scale * inner
    dqkv = jnp.concatenate(
        [
            (inv_scale[:, 0:1] * weighted[:, :col_width] - qkv[:, :col_width] * cube[:, 0:1]).astype(bf16),
            (inv_scale[:, 1:2] * weighted[:, col_width:] - qkv[:, col_width : 2 * col_width] * cube[:, 1:2]).astype(bf16),
            dv,
        ],
        axis=1,
    )
    grad_qkv = matmul(x_full, dqkv, TN).astype(bf16)

    qkv_full, *gate_parts = tie(qkv_full, *gate_parts)
    sum_gate = jnp.where(same, gate_parts[0].astype(f32), 0.0)
    for part in gate_parts[1:]:
        sum_gate = sum_gate + part.astype(f32)
    dx = matmul(dqkv, qkv_full, NT).astype(bf16)
    here = lax.dynamic_slice_in_dim(dx, block_at * mine, mine, 0).astype(f32) + dh_tok
    dx = lax.dynamic_update_slice_in_dim(dx, here.astype(bf16), block_at * mine, 0)
    dtokens, sum_down, sum_qkv, sum_up = last_sums(dx, grad_down_w, grad_qkv, jnp.stack(up_sums))
    sum_qkv = sum_qkv.reshape(qkv_first.shape)

    half_w = width // 2
    half = lax.dynamic_slice_in_dim(grad_out, r * half_w, half_w, 1).astype(f32) + swap(
        lax.dynamic_slice_in_dim(grad_out, (1 - r) * half_w, half_w, 1), "row"
    ).astype(f32)
    half = half.astype(bf16).reshape(n_col, n_dp, out_rows, width // 2)
    half = lax.psum_scatter(half, "dp", scatter_dimension=1, tiled=False)
    sum_out = lax.psum_scatter(half, ("zh", "zl"), scatter_dimension=0, tiled=False).astype(f32)

    head_place = lax.dynamic_update_slice_in_dim(
        jnp.zeros((2, width), f32), grad_head, block_at * col_width, 1
    )
    small = jnp.concatenate([head_place, grad_gain_attn[None], grad_gain_mlp[None]], axis=0)
    small, sum_down = tie(small, sum_down)
    small = small_sum(small, ("dp", "row", "zh", "zl"))
    col_at = g * tp + t
    sum_head = lax.dynamic_slice_in_dim(small[:2], col_at * col_width, col_width, 1)
    post_rows = post_first.shape[0]
    sum_post = lax.dynamic_slice_in_dim(
        small[2:], ((r * n_col + col_at) * n_dp + d) * post_rows, post_rows, 1
    ).T

    def owned_rows(weight, part_rows):
        return lax.dynamic_slice_in_dim(weight, d * part_rows, part_rows, 0)

    results = []
    for weight, total, first, second in (
        (qkv_weight, sum_qkv, qkv_first, qkv_second),
        (out_weight, sum_out, out_first, out_second),
        (gate_weight, sum_gate, gate_first, gate_second),
        (up_weight, sum_up, up_first, up_second),
        (down_weight, sum_down, down_first, down_second),
    ):
        results.extend(
            adamw_step(owned_rows(weight, total.shape[0]), total, first, second, rate_matrix, weight_decay)
        )
    results.extend(adamw_step(head_gains, sum_head, head_first, head_second, rate_gain, 0.0))
    results.extend(
        adamw_step(owned_rows(post_gains, post_rows), sum_post, post_first, post_second, rate_gain, 0.0)
    )
    return (mixed, dtokens, *results)


def solution(mesh):
    n_dp, n_row, n_col = (mesh.shape[name] for name in ("dp", "row", "col"))
    grid = Mesh(mesh.devices.reshape(n_dp, n_row, 2, n_col // 2), ("dp", "row", "zh", "zl"))
    col = ("zh", "zl")
    moved = P("dp", ("row", *col))
    qkv_part = P(("row", "dp"), None, col)
    flat_part = P((*col, "dp"), "row")
    wide_part = P(("row", "dp"), col)
    head_part = P(None, col)
    post_part = P(("row", *col, "dp"), None)
    in_specs = (
        moved,
        moved,
        P(("dp", "row"), None),
        P("row", None, col),
        P(col, "row"),
        P("row", col),
        P("row", col),
        P(col, "row"),
        head_part,
        P(("row", *col), None),
        *[spec for spec in (qkv_part, flat_part, wide_part, wide_part, flat_part, head_part, post_part) for _ in range(2)],
    )
    out_specs = (
        moved,
        moved,
        *[spec for spec in (qkv_part, flat_part, wide_part, wide_part, flat_part, head_part, post_part) for _ in range(3)],
    )
    return jax.shard_map(shards, mesh=grid, in_specs=in_specs, out_specs=out_specs, check_vma=False)
```
